32 devices in a mesh: depth: 4 (over x, core), lat: 8 (over z, y).
Axes of the slice: x: 2, y: 2, z: 4, core: 2. Of those that a mesh axis runs over, the one named last changes fastest.
Arguments:
- source_field: float32 [2, 4, 256, 1024], P(None, None, 'lat'), may hold values from -9 to 9, as said below
- receiver_field: float32 [2, 4, 256, 1024], P(None, None, 'lat'), may hold values from -9 to 9, as said below
- zone_index: int32 [16, 256, 1024], P('depth', 'lat'), may hold values from 0 to 2
- blend_weight: int32 [16, 256, 1024], P('depth', 'lat'), may hold values from 0 to 16
- ref_velocity: float32 [4], replicated, may hold values from 1500 to 4500
- frequencies: int32 [4], replicated, may hold values from 5 to 40
Outputs:
- migrated_image: float32 [16, 256, 1024], P('depth', 'lat')
The draws below stay inside these ranges and needn't reach their ends.
Inputs may be any that keep to these rules, and one draw needn't show every extreme that they name: `source_field`: surface wavefields of order one. `receiver_field`: recorded wavefields of order one.
All inputs are finite; a program needn't handle non-finite values.
Results may differ from the reference program's by a relative error of at most 0.0003.
Values sent between devices are 32-bit elements; how exact they have to be, the bound alone decides.
No kernel may reach another device: no remote copies, remote signals or barrier semaphores. Data moves between devices by JAX's collectives and lax.ppermute only.
A program may use at most 64 MiB of HBM per device.

```python
import math
import jax
import jax.numpy as jnp
from jax import lax

NY = 1024
NFREQ = 4
NREF = 4
HALF = 7
BLEND = 16
NX = 256
NZ = 16


def plane_waves(key):
    keys = jax.random.split(key, 5)
    wave_count = 8
    spread = 0.6
    amplitude = jax.random.uniform(keys[0], (NFREQ, wave_count), jnp.float32, -spread, spread)
    along_x = jax.random.uniform(keys[1], (NFREQ, wave_count), jnp.float32, -0.25, 0.25)
    along_y = jax.random.uniform(keys[2], (NFREQ, wave_count), jnp.float32, -0.25, 0.25)
    offset_phase = jax.random.uniform(keys[3], (NFREQ, wave_count), jnp.float32, 0.0, 2.0 * math.pi)
    coord_x = jnp.arange(NX, dtype=jnp.float32)[:, None]
    coord_y = jnp.arange(NY, dtype=jnp.float32)[None, :]
    field_re = jnp.zeros((NFREQ, NX, NY), jnp.float32)
    field_im = jnp.zeros((NFREQ, NX, NY), jnp.float32)
    for number in range(wave_count):
        argument = along_x[:, number, None, None] * coord_x[None] + along_y[:, number, None, None] * coord_y[None] + offset_phase[:, number, None, None]
        field_re = field_re + amplitude[:, number, None, None] * jnp.cos(argument)
        field_im = field_im + amplitude[:, number, None, None] * jnp.sin(argument)
    noise = 0.4 * jax.random.truncated_normal(keys[4], -3.0, 3.0, (2, NFREQ, NX, NY), jnp.float32)
    return jnp.stack([field_re, field_im]) + noise


def draw_source_field(key, part):
    return plane_waves(jax.random.fold_in(key, 11)).astype(jnp.float32)


def draw_receiver_field(key, part):
    return plane_waves(jax.random.fold_in(key, 23)).astype(jnp.float32)


def set_ends(values, own_key, smallest, high):
    place = [jax.random.randint(jax.random.fold_in(own_key, axis), (), 0, length) for axis, length in enumerate(values.shape)]
    main_axis = values.shape.index(max(values.shape))
    next_to = place[:main_axis] + [(place[main_axis] + 1) % values.shape[main_axis]] + place[main_axis + 1:]
    return values.at[tuple(place)].set(smallest).at[tuple(next_to)].set(high)


def setup_inputs(seed: int = 0) -> dict:
    key_of = jax.random.split(jax.random.key(seed), 7)
    return {
        "source_field": draw_source_field(jax.random.fold_in(key_of[6], 71), 0),
        "receiver_field": draw_receiver_field(jax.random.fold_in(key_of[6], 71), 0),
        "zone_index": set_ends(jax.random.randint(key_of[2], (NZ, NX, NY), 0, NREF - 1), jax.random.fold_in(key_of[2], 1), 0, (NREF - 1) - 1).astype(jnp.int32),
        "blend_weight": set_ends(jax.random.randint(key_of[3], (NZ, NX, NY), 0, BLEND + 1), jax.random.fold_in(key_of[3], 1), 0, BLEND).astype(jnp.int32),
        "ref_velocity": jnp.clip(jax.random.uniform(key_of[4], (NREF,), jnp.float32, 1500.0, 4500.0), 1500.0, 4500.0),
        "frequencies": set_ends(jax.random.randint(key_of[5], (NFREQ,), 5, 41), jax.random.fold_in(key_of[5], 1), 5, 40).astype(jnp.int32),
    }


cell_width = 5.0
depth_step = 10.0
taper_width = 16.0

def kernels(frequencies, ref_velocity):
    offsets = jnp.arange(-HALF, HALF + 1, dtype=jnp.int32).astype(jnp.float32)
    wavenumber = 2.0 * math.pi * frequencies.astype(jnp.float32)[:, None] / ref_velocity[None, :]
    curvature = wavenumber * (cell_width * cell_width / (2.0 * depth_step))
    phase_turn = wavenumber * depth_step
    chirp_angle = curvature[:, :, None] * (offsets * offsets)[None, None, :]
    envelope = jnp.exp(-offsets * offsets / taper_width)
    raw_re = envelope * jnp.cos(chirp_angle)
    raw_im = envelope * jnp.sin(chirp_angle)
    magnitude = jnp.sqrt(lax.optimization_barrier(jnp.sum(raw_re, axis=-1)) ** 2 + lax.optimization_barrier(jnp.sum(raw_im, axis=-1)) ** 2)[:, :, None]
    return (raw_re / magnitude, raw_im / magnitude, jnp.cos(phase_turn), jnp.sin(phase_turn))

def convolve_rows(real, imag, tap_re, tap_im):
    length = real.shape[0] - 2 * HALF
    out_re = jnp.zeros((tap_re.shape[0], length, real.shape[1]), jnp.float32)
    out_im = jnp.zeros((tap_re.shape[0], length, real.shape[1]), jnp.float32)
    for offset in range(2 * HALF + 1):
        part_re = real[offset:offset + length][None]
        part_im = imag[offset:offset + length][None]
        coef_re = tap_re[:, offset][:, None, None]
        coef_im = tap_im[:, offset][:, None, None]
        out_re = out_re + coef_re * part_re - coef_im * part_im
        out_im = out_im + coef_re * part_im + coef_im * part_re
    return (out_re, out_im)

def convolve_cols(real, imag, tap_re, tap_im):
    length = real.shape[2] - 2 * HALF
    out_re = jnp.zeros(real.shape[:2] + (length,), jnp.float32)
    out_im = jnp.zeros(real.shape[:2] + (length,), jnp.float32)
    for offset in range(2 * HALF + 1):
        part_re = real[:, :, offset:offset + length]
        part_im = imag[:, :, offset:offset + length]
        coef_re = tap_re[:, offset][:, None, None]
        coef_im = tap_im[:, offset][:, None, None]
        out_re = out_re + coef_re * part_re - coef_im * part_im
        out_im = out_im + coef_re * part_im + coef_im * part_re
    return (out_re, out_im)

def advance(pad_re, pad_im, tap_re, tap_im, turn_cos, turn_sin, zone_level, weight_level):
    rows_re, rows_im = convolve_rows(pad_re, pad_im, tap_re, tap_im)
    widths = ((0, 0), (0, 0), (HALF, HALF))
    both_re, both_im = convolve_cols(jnp.pad(rows_re, widths), jnp.pad(rows_im, widths), tap_re, tap_im)
    phased_re = both_re * turn_cos[:, None, None] - both_im * turn_sin[:, None, None]
    phased_im = both_re * turn_sin[:, None, None] + both_im * turn_cos[:, None, None]
    reference_ids = jnp.arange(tap_re.shape[0], dtype=jnp.int32)[:, None, None]
    weights = jnp.where(reference_ids == zone_level[None], 1.0 - weight_level[None], 0.0)
    weights = weights + jnp.where(reference_ids == zone_level[None] + 1, weight_level[None], 0.0)
    return (lax.optimization_barrier(jnp.sum(weights * phased_re, axis=0)), lax.optimization_barrier(jnp.sum(weights * phased_im, axis=0)))

def reference(source_field, receiver_field, zone_index, blend_weight, ref_velocity, frequencies):
    tap_re, tap_im, turn_cos, turn_sin = kernels(frequencies, ref_velocity)
    weight_levels = blend_weight.astype(jnp.float32) / BLEND
    widths = ((HALF, HALF), (0, 0))

    def each_frequency(migrated, which):

        def each_level(fields, depth_level):
            source_re, source_im, receiver_re, receiver_im = fields
            zone_level = zone_index[depth_level]
            weight_level = weight_levels[depth_level]
            source_re, source_im = advance(jnp.pad(source_re, widths), jnp.pad(source_im, widths), tap_re[which], tap_im[which], turn_cos[which], turn_sin[which], zone_level, weight_level)
            receiver_re, receiver_im = advance(jnp.pad(receiver_re, widths), jnp.pad(receiver_im, widths), tap_re[which], -tap_im[which], turn_cos[which], -turn_sin[which], zone_level, weight_level)
            return ((source_re, source_im, receiver_re, receiver_im), source_re * receiver_re + source_im * receiver_im)
        start = (source_field[0, which], source_field[1, which], receiver_field[0, which], receiver_field[1, which])
        _, pieces = lax.scan(each_level, start, jnp.arange(NZ, dtype=jnp.int32))
        return (migrated + pieces, None)
    migrated, _ = lax.scan(each_frequency, jnp.zeros((NZ, NX, NY), jnp.float32), jnp.arange(NFREQ, dtype=jnp.int32))
    return migrated / NFREQ
```

```python
import functools
import math

import jax
import jax.numpy as jnp
from jax import lax
from jax.experimental import pallas as pl
from jax.experimental.pallas import tpu as pltpu
from jax.sharding import PartitionSpec as P

HALF = 7
BLEND = 16
TAPS = 2 * HALF + 1
SPAN = 2 * HALF
LANES = 128
WIN = LANES - SPAN
BLK = 16
AXES = ("depth", "lat")
OFF = 8

cell_width = 5.0
depth_step = 10.0
taper_width = 16.0

f32 = jnp.float32
bf16 = jnp.bfloat16


def cdiv(a, b):
    return -(-a // b)


def kernels(frequencies, ref_velocity):
    offsets = jnp.arange(-HALF, HALF + 1, dtype=jnp.int32).astype(jnp.float32)
    wavenumber = 2.0 * math.pi * frequencies.astype(jnp.float32)[:, None] / ref_velocity[None, :]
    curvature = wavenumber * (cell_width * cell_width / (2.0 * depth_step))
    phase_turn = wavenumber * depth_step
    chirp_angle = curvature[:, :, None] * (offsets * offsets)[None, None, :]
    envelope = jnp.exp(-offsets * offsets / taper_width)
    raw_re = envelope * jnp.cos(chirp_angle)
    raw_im = envelope * jnp.sin(chirp_angle)
    magnitude = jnp.sqrt(jnp.sum(raw_re, axis=-1) ** 2 + jnp.sum(raw_im, axis=-1) ** 2)[:, :, None]
    return (raw_re / magnitude, raw_im / magnitude, jnp.cos(phase_turn), jnp.sin(phase_turn))


def halves(x):
    high = lax.reduce_precision(x, 8, 7)
    return high.astype(bf16), (x - high).astype(bf16)


def operators(tap_re, tap_im, turn_cos, turn_sin):
    def band(taps, index, valid):
        out = jnp.zeros(taps.shape[:-1] + index.shape, f32)
        for m in range(TAPS):
            out = out + jnp.where((index == m) & valid, taps[..., m][..., None, None], 0.0)
        return out

    count, refs = tap_re.shape[:2]
    index = jnp.arange(2 * BLK)[None, :] - jnp.arange(BLK)[:, None]
    re, im = band(tap_re, index, True), band(tap_im, index, True)
    rows = jnp.stack([jnp.concatenate([re, -im], -1), jnp.concatenate([im, re], -1)], 2)
    high, low = halves(rows.reshape(count, refs * 2 * BLK, 4 * BLK))
    by_rows = jnp.concatenate([high, high, low], -1)
    ph_re = tap_re * turn_cos[..., None] - tap_im * turn_sin[..., None]
    ph_im = tap_re * turn_sin[..., None] + tap_im * turn_cos[..., None]
    column = jnp.arange(LANES)[None, :]
    index = jnp.arange(LANES)[:, None] - column
    re, im = band(ph_re, index, column < WIN), band(ph_im, index, column < WIN)
    cols = jnp.concatenate(
        [jnp.concatenate([re, im], -1), jnp.concatenate([-im, re], -1)], -2
    )
    high, low = halves(cols)
    by_cols = jnp.concatenate([high, high, low], -2)
    return by_rows, by_cols


def split(v):
    high = v.astype(bf16)
    return high, (v - high.astype(f32)).astype(bf16)


def window(x, start, b):
    low = start + WIN * b
    high = min(low + LANES, x.shape[1])
    part = x[:, low:high]
    if high - low < LANES:
        part = jnp.concatenate(
            [part, jnp.zeros((x.shape[0], LANES - (high - low)), x.dtype)], axis=1
        )
    return part


def dense(get, start, count):
    pieces = []
    n = start
    while n < start + count:
        b = n // WIN
        end = min(WIN * (b + 1), start + count)
        pieces.append(get(b)[:, n - WIN * b : end - WIN * b])
        n = end
    return jnp.concatenate(pieces, axis=1)


def stage_kernel(
    levels, rows, cols, windows, blocks, refs,
    tile_ref, t_ref, a_ref, c_ref, out_ref, img_ref, cur_ref, y_ref, tw_ref, im_ref,
):
    height = tile_ref.shape[1]
    held = cur_ref.shape[2]
    each = 2 * windows
    lanes = windows * LANES
    for l in range(levels):
        h = height - SPAN * (l + 1)
        x = t_ref[l, HALF * l : HALF * l + h, :]
        for b in range(windows):
            tw_ref[l, 0:h, b * LANES : (b + 1) * LANES] = window(x, HALF * l, b)
        tw_ref[l, h:held, :] = jnp.full((held - h, lanes), -8.0, f32)
    for f in range(2):
        for p in range(2):
            x = tile_ref[2 * f + p]
            for b in range(windows):
                high, low = split(window(x, 0, b))
                at = (f * windows + b) * LANES
                cur_ref[p, 0, 0:height, at : at + LANES] = high
                cur_ref[p, 1, 0:height, at : at + LANES] = low
    if held > height:
        cur_ref[:, :, height:held, :] = jnp.zeros((2, 2, held - height, 2 * lanes), bf16)
    lane = lax.broadcasted_iota(jnp.int32, (BLK, LANES), 1)

    def chunk(l, i, carry):
        base = pl.multiple_of(i * (BLK * blocks), BLK * blocks)
        for k in range(blocks):
            r = pl.ds(pl.multiple_of(base + BLK * k, BLK), 2 * BLK)
            rhi, rlo = cur_ref[0, 0, r, :], cur_ref[0, 1, r, :]
            ihi, ilo = cur_ref[1, 0, r, :], cur_ref[1, 1, r, :]
            rhs = jnp.concatenate([rhi, ihi, rlo, ilo, rhi, ihi], axis=0)
            g = jnp.dot(a_ref[...], rhs, preferred_element_type=f32)
            high, low = split(g)
            for j in range(refs):
                for p in range(2):
                    s = (2 * j + p) * BLK
                    for q in range(each):
                        rr = (k * each + q) * BLK
                        at = q * LANES
                        y_ref[j, rr : rr + BLK, p * LANES : (p + 1) * LANES] = high[
                            s : s + BLK, at : at + LANES
                        ]
                        y_ref[j, rr : rr + BLK, (2 + p) * LANES : (3 + p) * LANES] = low[
                            s : s + BLK, at : at + LANES
                        ]
        t = tw_ref[l, pl.ds(base, BLK * blocks), :]
        acc = None
        for j in range(refs):
            y = y_ref[j]
            full = jnp.dot(
                jnp.concatenate([y, y[:, : 2 * LANES]], axis=1),
                c_ref[j],
                preferred_element_type=f32,
            )
            w = jnp.maximum(1.0 - jnp.abs(t - float(j)), 0.0)
            new = []
            for k in range(blocks):
                for f in range(2):
                    for b in range(windows):
                        rr = (k * each + f * windows + b) * BLK
                        wk = w[BLK * k : BLK * (k + 1), b * LANES : (b + 1) * LANES]
                        new.append(
                            (wk * full[rr : rr + BLK, :LANES], wk * full[rr : rr + BLK, LANES:])
                        )
            if acc is None:
                acc = new
            else:
                acc = [(a0 + b0, a1 + b1) for (a0, a1), (b0, b1) in zip(acc, new)]
        for k in range(blocks):
            r = pl.ds(pl.multiple_of(base + BLK * k, BLK), BLK)
            for b in range(windows):
                s = acc[k * each + b]
                q = acc[k * each + windows + b]
                im_ref[l, r, b * LANES : (b + 1) * LANES] = s[0] * q[0] - s[1] * q[1]
            for f in range(2):
                for b in range(windows):
                    at = (f * windows + b) * LANES
                    for p in range(2):
                        v = acc[k * each + f * windows + b][p]
                        if b + 1 < windows:
                            after = pltpu.roll(acc[k * each + f * windows + b + 1][p], WIN, 1)
                            v = jnp.where(lane < WIN, v, after)
                        high, low = split(v)
                        cur_ref[p, 0, r, at : at + LANES] = high
                        cur_ref[p, 1, r, at : at + LANES] = low
        return carry

    def level(l, carry):
        count = (height - SPAN * (l + 1) + BLK * blocks - 1) // (BLK * blocks)
        return lax.fori_loop(0, count, functools.partial(chunk, l), carry)

    lax.fori_loop(0, levels, level, 0)
    for f in range(2):
        for p in range(2):

            def get(b):
                at = (f * windows + b) * LANES
                return cur_ref[p, 0, 0:rows, at : at + LANES].astype(f32) + cur_ref[
                    p, 1, 0:rows, at : at + LANES
                ].astype(f32)

            out_ref[2 * f + p] = dense(get, 0, cols)
    for l in range(levels):
        o = HALF * (levels - 1 - l)
        img_ref[l] = dense(
            lambda b: im_ref[l, o : o + rows, b * LANES : (b + 1) * LANES], o, cols
        )


def stage(tile, t, by_rows, by_cols, rows, cols, blocks=4):
    levels = t.shape[0]
    height = tile.shape[1]
    refs = by_cols.shape[0]
    windows = cdiv(cols + SPAN * (levels - 1), WIN)
    step = BLK * blocks
    held = max(cdiv(height - SPAN, step) * step + BLK, cdiv(height, BLK) * BLK)
    body = functools.partial(stage_kernel, levels, rows, cols, windows, blocks, refs)
    area = levels * (height + rows) // 2 * windows * LANES
    return pl.pallas_call(
        body,
        out_shape=[
            jax.ShapeDtypeStruct((4, rows, cols), f32),
            jax.ShapeDtypeStruct((levels, rows, cols), f32),
        ],
        scratch_shapes=[
            pltpu.VMEM((2, 2, held, 2 * windows * LANES), bf16),
            pltpu.VMEM((refs, blocks * 2 * windows * BLK, 4 * LANES), bf16),
            pltpu.VMEM((levels, held, windows * LANES), f32),
            pltpu.VMEM((levels, held, windows * LANES), f32),
        ],
        compiler_params=pltpu.CompilerParams(vmem_limit_bytes=40 * 2**20),
        cost_estimate=pl.CostEstimate(
            flops=area * 2 * refs * 2 * 3 * 512, bytes_accessed=4 * tile.size, transcendentals=0
        ),
    )(tile, t, by_rows, by_cols)


def local(source_field, receiver_field, zone_index, blend_weight, ref_velocity, frequencies):
    depth, lat = lax.axis_size("depth"), lax.axis_size("lat")
    d, l = lax.axis_index("depth"), lax.axis_index("lat")
    hi, core = d // 2, d % 2
    pair, side = l // 2, l % 2
    if depth != 4 or lat % 2:
        raise ValueError("mesh")
    levels, strip, width = zone_index.shape
    freq_count = source_field.shape[1]
    per_core = freq_count // 2
    rows, cols = 2 * strip, width // 4
    halo = HALF * levels
    edge = halo - HALF

    def permutation(move):
        out = []
        for i in range(depth * lat):
            dd, ll = divmod(i, lat)
            target = move(dd // 2, dd % 2, ll // 2, ll % 2)
            if target is None:
                continue
            h2, c2, p2, s2 = target
            if 0 <= p2 < lat // 2:
                out.append((i, (h2 * 2 + c2) * lat + p2 * 2 + s2))
        return out

    across_hi = permutation(lambda h, c, p, s: (1 - h, c, p, s))
    across_side = permutation(lambda h, c, p, s: (h, c, p, 1 - s))
    across_both = permutation(lambda h, c, p, s: (1 - h, c, p, 1 - s))
    across_core = permutation(lambda h, c, p, s: (h, 1 - c, p, s))
    pairs_even = permutation(lambda h, c, p, s: (h, c, p + 1 - 2 * (p % 2), s))
    pairs_odd = permutation(lambda h, c, p, s: (h, c, p - 1 + 2 * (p % 2), s))
    middle = permutation(lambda h, c, p, s: (1 - h, c, p, s) if s == 1 else None)

    def move(x, pairs):
        return lax.ppermute(x, AXES, pairs)

    def place(h, s):
        return 2 * h + jnp.where(h == 0, s, 1 - s)

    block = place(hi, side)

    def exchange_rows(x, count, axis):
        size = x.shape[axis]
        top = lax.slice_in_dim(x, 0, count, axis=axis)
        bottom = lax.slice_in_dim(x, size - count, size, axis=axis)
        even = pair % 2 == 0
        got_a = move(jnp.where(even, bottom, top), pairs_even)
        got_b = move(jnp.where(even, top, bottom), pairs_odd)
        return jnp.where(even, got_b, got_a), jnp.where(even, got_a, got_b)

    def exchange_cols(x, count):
        even = block % 2 == 0
        left, right = x[..., :count], x[..., -count:]
        got_a = move(jnp.where(even, right, left), across_side)
        got_b = move(jnp.where(even, left, right), middle)
        return jnp.where(even, got_b, got_a), jnp.where(even, got_a, got_b)

    def columns(x, which, size):
        return lax.dynamic_slice_in_dim(x, which * cols, size, x.ndim - 1)

    def by_side(mine, other, axis):
        return jnp.concatenate(
            [jnp.where(side == 0, mine, other), jnp.where(side == 0, other, mine)], axis=axis
        )

    tables = jnp.stack([zone_index + OFF, blend_weight])
    tables = jnp.pad(tables, ((0, 0),) * 3 + ((edge, edge),))
    size = cols + 2 * edge
    mine = columns(tables, block, size)
    got_hi = move(columns(tables, place(1 - hi, side), size), across_hi)
    got_side = move(columns(tables, place(hi, 1 - side), size), across_side)
    got_both = move(columns(tables, place(1 - hi, 1 - side), size), across_both)
    stage_t = [None] * 4
    for s in range(2):
        whole = by_side(
            jnp.where(hi == s, mine, got_hi), jnp.where(hi == s, got_side, got_both), 2
        )
        above, below = exchange_rows(whole, edge, 2)
        whole = jnp.concatenate([above, whole, below], axis=2)
        other = move(whole, across_core)
        for k in range(2):
            pick = jnp.where(core == k, whole, other)
            stage_t[2 * s + k] = (pick[0] - OFF).astype(f32) + pick[1].astype(f32) / BLEND

    surface = jnp.stack(
        [source_field[0], source_field[1], receiver_field[0], -receiver_field[1]], axis=1
    )
    surface = lax.dynamic_slice_in_dim(surface, core * per_core, per_core, 0)
    surface = jnp.pad(surface, ((0, 0),) * 3 + ((halo, halo),))
    size = cols + 2 * halo
    tiles = []
    for q in range(per_core):
        mine = columns(surface[q], block, size)
        other = move(columns(surface[q], place(hi, 1 - side), size), across_side)
        tile = by_side(mine, other, 1)
        above, below = exchange_rows(tile, halo, 1)
        tiles.append(jnp.concatenate([above, tile, below], axis=1))

    tap_re, tap_im, turn_cos, turn_sin = kernels(frequencies, ref_velocity)
    by_rows, by_cols = operators(tap_re, tap_im, turn_cos, turn_sin)
    by_rows = lax.dynamic_slice_in_dim(by_rows, core * per_core, per_core, 0)
    by_cols = lax.dynamic_slice_in_dim(by_cols, core * per_core, per_core, 0)

    images = []
    for s in range(4):
        image = None
        for q in range(per_core):
            field, part = stage(tiles[q], stage_t[s], by_rows[q], by_cols[q], rows, cols)
            image = part if image is None else image + part
            if s < 3:
                above, below = exchange_rows(field, halo, 1)
                field = jnp.concatenate([above, field, below], axis=1)
                left, right = exchange_cols(field, halo)
                tiles[q] = jnp.concatenate([left, field, right], axis=2)
        images.append(image)

    sums = []
    for s in range(2):
        mine = jnp.where(core == 0, images[2 * s], images[2 * s + 1])
        other = jnp.where(core == 0, images[2 * s + 1], images[2 * s])
        sums.append(mine + move(other, across_core))
    here = jnp.where(hi == 0, sums[0], sums[1])
    there = jnp.where(hi == 0, sums[1], sums[0])

    def strip_of(x, s):
        return lax.dynamic_slice_in_dim(x, s * strip, strip, 1)

    mine = strip_of(here, side)
    got_hi = move(strip_of(there, side), across_hi)
    got_side = move(strip_of(here, 1 - side), across_side)
    got_both = move(strip_of(there, 1 - side), across_both)
    pieces = []
    for k in range(4):
        piece = jnp.where(
            block == k,
            mine,
            jnp.where(
                place(1 - hi, side) == k,
                got_hi,
                jnp.where(place(hi, 1 - side) == k, got_side, got_both),
            ),
        )
        pieces.append(piece)
    return jnp.concatenate(pieces, axis=2) * (1.0 / freq_count)


def solution(mesh):
    in_specs = (
        P(None, None, "lat", None),
        P(None, None, "lat", None),
        P("depth", "lat", None),
        P("depth", "lat", None),
        P(),
        P(),
    )
    out_specs = P("depth", "lat", None)
    return jax.shard_map(local, mesh=mesh, in_specs=in_specs, out_specs=out_specs, check_vma=False)
```

```python
import functools
import math

import jax
import jax.numpy as jnp
from jax import lax
from jax.experimental import pallas as pl
from jax.experimental.pallas import tpu as pltpu
from jax.sharding import PartitionSpec as P

HALF = 7
BLEND = 16
TAPS = 2 * HALF + 1
SPAN = 2 * HALF
LANES = 128
WIN = LANES - SPAN
BLK = 16
AXES = ("depth", "lat")
OFF = 8

cell_width = 5.0
depth_step = 10.0
taper_width = 16.0

f32 = jnp.float32
bf16 = jnp.bfloat16


def cdiv(a, b):
    return -(-a // b)


def kernels(frequencies, ref_velocity):
    offsets = jnp.arange(-HALF, HALF + 1, dtype=jnp.int32).astype(jnp.float32)
    wavenumber = 2.0 * math.pi * frequencies.astype(jnp.float32)[:, None] / ref_velocity[None, :]
    curvature = wavenumber * (cell_width * cell_width / (2.0 * depth_step))
    phase_turn = wavenumber * depth_step
    chirp_angle = curvature[:, :, None] * (offsets * offsets)[None, None, :]
    envelope = jnp.exp(-offsets * offsets / taper_width)
    raw_re = envelope * jnp.cos(chirp_angle)
    raw_im = envelope * jnp.sin(chirp_angle)
    magnitude = jnp.sqrt(jnp.sum(raw_re, axis=-1) ** 2 + jnp.sum(raw_im, axis=-1) ** 2)[:, :, None]
    return (raw_re / magnitude, raw_im / magnitude, jnp.cos(phase_turn), jnp.sin(phase_turn))


def halves(x):
    high = lax.reduce_precision(x, 8, 7)
    return high.astype(bf16), (x - high).astype(bf16)


def operators(tap_re, tap_im, turn_cos, turn_sin):
    def band(taps, index, valid):
        out = jnp.zeros(taps.shape[:-1] + index.shape, f32)
        for m in range(TAPS):
            out = out + jnp.where((index == m) & valid, taps[..., m][..., None, None], 0.0)
        return out

    count, refs = tap_re.shape[:2]
    index = jnp.arange(2 * BLK)[None, :] - jnp.arange(BLK)[:, None]
    re, im = band(tap_re, index, True), band(tap_im, index, True)
    rows = jnp.stack([jnp.concatenate([re, -im], -1), jnp.concatenate([im, re], -1)], 2)
    high, low = halves(rows.reshape(count, refs * 2 * BLK, 4 * BLK))
    by_rows = jnp.concatenate([high, high, low], -1)
    ph_re = tap_re * turn_cos[..., None] - tap_im * turn_sin[..., None]
    ph_im = tap_re * turn_sin[..., None] + tap_im * turn_cos[..., None]
    column = jnp.arange(LANES)[None, :]
    index = jnp.arange(LANES)[:, None] - column
    re, im = band(ph_re, index, column < WIN), band(ph_im, index, column < WIN)
    cols = jnp.concatenate(
        [jnp.concatenate([re, im], -1), jnp.concatenate([-im, re], -1)], -2
    )
    high, low = halves(cols)
    by_cols = jnp.concatenate([high, high, low], -2)
    return by_rows, by_cols


def split(v):
    high = v.astype(bf16)
    return high, (v - high.astype(f32)).astype(bf16)


def window(x, start, b):
    low = start + WIN * b
    high = min(low + LANES, x.shape[1])
    part = x[:, low:high]
    if high - low < LANES:
        part = jnp.concatenate(
            [part, jnp.zeros((x.shape[0], LANES - (high - low)), x.dtype)], axis=1
        )
    return part


def dense(get, start, count):
    pieces = []
    n = start
    while n < start + count:
        b = n // WIN
        end = min(WIN * (b + 1), start + count)
        pieces.append(get(b)[:, n - WIN * b : end - WIN * b])
        n = end
    return jnp.concatenate(pieces, axis=1)


CORE, HI, SIDE, EVEN_PAIR, FIRST_PAIR, LAST_PAIR, BLOCK, REL = range(8)


def pack_kernel(halo, edge, info, src, rcv, zone, blend, keep, give, mine, send):
    per_core = mine.shape[0]
    strip, width = zone.shape[1:]
    cols = width // 4
    half = zone.shape[0] // 2
    core = info[CORE]

    def sides(x, k, n):
        left = x[:, cols * k - n : cols * k] if k > 0 else jnp.zeros((strip, n), x.dtype)
        right = x[:, cols * (k + 1) : cols * (k + 1) + n] if k < 3 else jnp.zeros((strip, n), x.dtype)
        return left, right

    for k in range(4):
        slot = info[REL + k]
        for h in range(2):
            for v in range(half):
                z = zone[h * half + v] + OFF
                w = blend[h * half + v]
                zl, zr = sides(z, k, edge)
                wl, wr = sides(w, k, edge)
                rest = jnp.zeros((strip, LANES - 4 * edge), jnp.int32)
                lanes = jnp.concatenate([zl, zr, wl, wr, rest], axis=1)

                def put(ref):
                    ref[slot, v, :, 0:cols] = z[:, cols * k : cols * (k + 1)]
                    ref[slot, v, :, cols : 2 * cols] = w[:, cols * k : cols * (k + 1)]
                    ref[slot, v, :, 2 * cols : 2 * cols + LANES] = lanes

                pl.when(core == h)(functools.partial(put, keep))
                pl.when(core != h)(functools.partial(put, give))
        for place, ref in ((0, mine), (2, send)):

            @pl.when(slot == place)
            def _():
                for q in range(per_core):
                    at = core * per_core + q
                    lefts, rights = [], []
                    for p in range(4):
                        x = (src if p < 2 else rcv)[p % 2, at]
                        if p == 3:
                            x = -x
                        ref[q, :, p * cols : (p + 1) * cols] = x[:, cols * k : cols * (k + 1)]
                        left, right = sides(x, k, halo)
                        lefts.append(left)
                        rights.append(right)
                    rest = jnp.zeros((strip, LANES - 4 * halo), f32)
                    ref[q, :, 4 * cols : 4 * cols + LANES] = jnp.concatenate(lefts + [rest], axis=1)
                    ref[q, :, 4 * cols + LANES : 4 * cols + 2 * LANES] = jnp.concatenate(
                        rights + [rest], axis=1
                    )


def edges_out(info, ref, send_a, send_b, count):
    size = ref.shape[-2]
    lead = (slice(None),) * (len(ref.shape) - 2)

    def put(top_to, bottom_to):
        top_to[lead + (slice(0, count),)] = ref[lead + (slice(0, count),)]
        bottom_to[lead + (slice(0, count),)] = ref[lead + (slice(size - count, size),)]

    pl.when(info[EVEN_PAIR] == 1)(lambda: put(send_b, send_a))
    pl.when(info[EVEN_PAIR] == 0)(lambda: put(send_a, send_b))


def join_tables_kernel(edge, info, mine, got_hi, got_side, got_both, whole, send_a, send_b):
    strip = mine.shape[1]
    for s in range(2):
        near = jnp.where(info[HI] == s, mine[...], got_hi[...])
        far = jnp.where(info[HI] == s, got_side[...], got_both[...])
        first = info[SIDE] == 0
        whole[s, :, 0:strip, :] = jnp.where(first, near, far)
        whole[s, :, strip : 2 * strip, :] = jnp.where(first, far, near)
        edges_out(info, whole.at[s], send_a.at[s], send_b.at[s], edge)


def join_fields_kernel(halo, info, mine, got, whole, send_a, send_b):
    strip = mine.shape[0]
    first = info[SIDE] == 0
    whole[0:strip, :] = jnp.where(first, mine[...], got[...])
    whole[strip : 2 * strip, :] = jnp.where(first, got[...], mine[...])
    edges_out(info, whole, send_a, send_b, halo)


def columns_kernel(halo, info, mid, got_a, got_b, send_a, send_b):
    even = info[EVEN_PAIR] == 1
    cols = mid.shape[1] // 4
    lefts, rights = [], []
    for p in range(4):
        for start, out in ((p * cols, lefts), ((p + 1) * cols - LANES, rights)):
            lanes = slice(start, start + LANES)
            a, b, m = got_a[:, lanes], got_b[:, lanes], mid[:, lanes]
            top = jnp.where(info[FIRST_PAIR] == 1, 0.0, jnp.where(even, b, a))
            bottom = jnp.where(info[LAST_PAIR] == 1, 0.0, jnp.where(even, a, b))
            rows = jnp.concatenate([top, m, bottom], axis=0)
            out.append(rows[:, :halo] if out is lefts else rows[:, LANES - halo :])
    rest = jnp.zeros((lefts[0].shape[0], LANES - 4 * halo), f32)
    left = jnp.concatenate(lefts + [rest], axis=1)
    right = jnp.concatenate(rights + [rest], axis=1)
    inner = info[BLOCK] % 2 == 0
    send_a[...] = jnp.where(inner, right, left)
    send_b[...] = jnp.where(inner, left, right)


def tables_kernel(
    cols, edge, windows, info, whole_m, whole_o, a_m, a_o, b_m, b_o, out
):
    half = whole_m.shape[0]
    levels, held = out.shape[:2]
    even = info[EVEN_PAIR] == 1
    for v in range(levels):
        own = info[CORE] == v // half
        i = v % half
        a = jnp.where(own, a_m[i], a_o[i])[:edge]
        b = jnp.where(own, b_m[i], b_o[i])[:edge]
        w = jnp.where(own, whole_m[i], whole_o[i])
        top = jnp.where(info[FIRST_PAIR] == 1, 0, jnp.where(even, b, a))
        bottom = jnp.where(info[LAST_PAIR] == 1, 0, jnp.where(even, a, b))
        x = jnp.concatenate([top, w, bottom], axis=0)
        s = 2 * cols
        z = jnp.concatenate([x[:, s : s + edge], x[:, :cols], x[:, s + edge : s + 2 * edge]], 1)
        s += 2 * edge
        w = jnp.concatenate(
            [x[:, s : s + edge], x[:, cols : 2 * cols], x[:, s + edge : s + 2 * edge]], 1
        )
        t = (z - OFF).astype(f32) + w.astype(f32) * (1.0 / BLEND)
        h = x.shape[0] - SPAN * v
        t = t[HALF * v : HALF * v + h]
        for b in range(windows):
            out[v, 0:h, b * LANES : (b + 1) * LANES] = window(t, HALF * v, b)
        out[v, h:held, :] = jnp.full((held - h, windows * LANES), -8.0, f32)


def stage_kernel(
    levels, halo, windows, blocks, refs, first, last, carried, *args
):
    args = list(args)
    info = args.pop(0)
    mid, got_a, got_b = args[:3]
    del args[:3]
    if not first:
        got_y, got_m = args[:2]
        del args[:2]
    tw_ref, a_ref, c_ref = args[:3]
    del args[:3]
    if carried:
        before = args.pop(0)
    img_ref = args.pop(0)
    if not last:
        out_ref, send_a, send_b = args[:3]
        del args[:3]
    cur_ref, y_ref, im_ref = args
    rows = mid.shape[0]
    cols = img_ref.shape[2]
    height = rows + 2 * halo
    held = cur_ref.shape[2]
    each = 2 * windows
    lanes = windows * LANES

    even = info[EVEN_PAIR] == 1
    inner = info[BLOCK] % 2 == 0

    def rows_of(lane):
        a, b = got_a[:, lane], got_b[:, lane]
        top = jnp.where(info[FIRST_PAIR] == 1, 0.0, jnp.where(even, b, a))
        bottom = jnp.where(info[LAST_PAIR] == 1, 0.0, jnp.where(even, a, b))
        return jnp.concatenate([top, mid[:, lane], bottom], axis=0)

    if first:
        left = rows_of(slice(4 * cols, 4 * cols + LANES))
        right = rows_of(slice(4 * cols + LANES, 4 * cols + 2 * LANES))
    else:
        left = jnp.where(info[BLOCK] == 0, 0.0, jnp.where(inner, got_m[...], got_y[...]))
        right = jnp.where(info[BLOCK] == 3, 0.0, jnp.where(inner, got_y[...], got_m[...]))
    for f in range(2):
        for p in range(2):
            n = 2 * f + p
            x = jnp.concatenate(
                [
                    left[:, n * halo : (n + 1) * halo],
                    rows_of(slice(n * cols, (n + 1) * cols)),
                    right[:, n * halo : (n + 1) * halo],
                ],
                axis=1,
            )
            for b in range(windows):
                high, low = split(window(x, 0, b))
                at = (f * windows + b) * LANES
                cur_ref[p, 0, 0:height, at : at + LANES] = high
                cur_ref[p, 1, 0:height, at : at + LANES] = low
    if held > height:
        cur_ref[:, :, height:held, :] = jnp.zeros((2, 2, held - height, 2 * lanes), bf16)
    lane = lax.broadcasted_iota(jnp.int32, (BLK, LANES), 1)

    def chunk(l, i, carry):
        base = pl.multiple_of(i * (BLK * blocks), BLK * blocks)
        for k in range(blocks):
            r = pl.ds(pl.multiple_of(base + BLK * k, BLK), 2 * BLK)
            rhi, rlo = cur_ref[0, 0, r, :], cur_ref[0, 1, r, :]
            ihi, ilo = cur_ref[1, 0, r, :], cur_ref[1, 1, r, :]
            rhs = jnp.concatenate([rhi, ihi, rlo, ilo, rhi, ihi], axis=0)
            g = jnp.dot(a_ref[...], rhs, preferred_element_type=f32)
            high, low = split(g)
            for j in range(refs):
                for p in range(2):
                    s = (2 * j + p) * BLK
                    for q in range(each):
                        rr = (k * each + q) * BLK
                        at = q * LANES
                        y_ref[j, rr : rr + BLK, p * LANES : (p + 1) * LANES] = high[
                            s : s + BLK, at : at + LANES
                        ]
                        y_ref[j, rr : rr + BLK, (2 + p) * LANES : (3 + p) * LANES] = low[
                            s : s + BLK, at : at + LANES
                        ]
        t = tw_ref[l, pl.ds(base, BLK * blocks), :]
        acc = None
        for j in range(refs):
            y = y_ref[j]
            full = jnp.dot(
                jnp.concatenate([y, y[:, : 2 * LANES]], axis=1),
                c_ref[j],
                preferred_element_type=f32,
            )
            w = jnp.maximum(1.0 - jnp.abs(t - float(j)), 0.0)
            new = []
            for k in range(blocks):
                for f in range(2):
                    for b in range(windows):
                        rr = (k * each + f * windows + b) * BLK
                        wk = w[BLK * k : BLK * (k + 1), b * LANES : (b + 1) * LANES]
                        new.append(
                            (wk * full[rr : rr + BLK, :LANES], wk * full[rr : rr + BLK, LANES:])
                        )
            if acc is None:
                acc = new
            else:
                acc = [(a0 + b0, a1 + b1) for (a0, a1), (b0, b1) in zip(acc, new)]
        for k in range(blocks):
            r = pl.ds(pl.multiple_of(base + BLK * k, BLK), BLK)
            for b in range(windows):
                s = acc[k * each + b]
                q = acc[k * each + windows + b]
                im_ref[l, r, b * LANES : (b + 1) * LANES] = s[0] * q[0] - s[1] * q[1]
            for f in range(2):
                for b in range(windows):
                    at = (f * windows + b) * LANES
                    for p in range(2):
                        v = acc[k * each + f * windows + b][p]
                        if b + 1 < windows:
                            after = pltpu.roll(acc[k * each + f * windows + b + 1][p], WIN, 1)
                            v = jnp.where(lane < WIN, v, after)
                        high, low = split(v)
                        cur_ref[p, 0, r, at : at + LANES] = high
                        cur_ref[p, 1, r, at : at + LANES] = low
        return carry

    def level(l, carry):
        count = (height - SPAN * (l + 1) + BLK * blocks - 1) // (BLK * blocks)
        return lax.fori_loop(0, count, functools.partial(chunk, l), carry)

    lax.fori_loop(0, levels, level, 0)
    if not last:
        for f in range(2):
            for p in range(2):

                def get(b):
                    at = (f * windows + b) * LANES
                    return cur_ref[p, 0, 0:rows, at : at + LANES].astype(f32) + cur_ref[
                        p, 1, 0:rows, at : at + LANES
                    ].astype(f32)

                n = 2 * f + p
                out_ref[:, n * cols : (n + 1) * cols] = dense(get, 0, cols)
        edges_out(info, out_ref, send_a, send_b, halo)
    for l in range(levels):
        o = HALF * (levels - 1 - l)
        part = dense(
            lambda b: im_ref[l, o : o + rows, b * LANES : (b + 1) * LANES], o, cols
        )
        img_ref[l] = part + before[l] if carried else part


def call(body, out_shape, info, *args, **more):
    specs = [pl.BlockSpec(memory_space=pltpu.SMEM)] + [pl.BlockSpec(memory_space=pltpu.VMEM)] * len(args)
    return pl.pallas_call(
        body,
        in_specs=specs,
        out_specs=jax.tree.map(lambda _: pl.BlockSpec(memory_space=pltpu.VMEM), out_shape),
        out_shape=out_shape,
        compiler_params=pltpu.CompilerParams(vmem_limit_bytes=40 * 2**20),
        **more,
    )(info, *args)


def shape(*dims, dtype=f32):
    return jax.ShapeDtypeStruct(dims, dtype)


def local(source_field, receiver_field, zone_index, blend_weight, ref_velocity, frequencies):
    depth, lat = lax.axis_size("depth"), lax.axis_size("lat")
    d, l = lax.axis_index("depth"), lax.axis_index("lat")
    hi, core = d // 2, d % 2
    pair, side = l // 2, l % 2
    if depth != 4 or lat % 4:
        raise ValueError("mesh")
    levels, strip, width = zone_index.shape
    freq_count, refs = frequencies.shape[0], ref_velocity.shape[0]
    per_core = freq_count // 2
    rows, cols = 2 * strip, width // 4
    halo = HALF * levels
    edge = halo - HALF
    half = levels // 2
    windows = cdiv(cols + SPAN * (levels - 1), WIN)
    blocks = 4
    step = BLK * blocks
    held = cdiv(rows + 2 * halo - SPAN, step) * step + BLK

    def permutation(move):
        out = []
        for i in range(depth * lat):
            dd, ll = divmod(i, lat)
            h, c, p, s = dd // 2, dd % 2, ll // 2, ll % 2
            target = move(h, c, p, s)
            if target is None or not 0 <= target[2] < lat // 2:
                target = (h, 1 - c, p, s)
            h, c, p, s = target
            out.append((i, (h * 2 + c) * lat + p * 2 + s))
        return out

    across_hi = permutation(lambda h, c, p, s: (1 - h, c, p, s))
    across_side = permutation(lambda h, c, p, s: (h, c, p, 1 - s))
    across_both = permutation(lambda h, c, p, s: (1 - h, c, p, 1 - s))
    across_core = permutation(lambda h, c, p, s: (h, 1 - c, p, s))
    pairs_even = permutation(lambda h, c, p, s: (h, c, p + 1 - 2 * (p % 2), s))
    pairs_odd = permutation(lambda h, c, p, s: (h, c, p - 1 + 2 * (p % 2), s))
    middle = permutation(lambda h, c, p, s: (1 - h, c, p, s) if s == 1 else None)

    def move(x, pairs):
        return lax.ppermute(x, AXES, pairs)

    def place(h, s):
        return 2 * h + jnp.where(h == 0, s, 1 - s)

    block = place(hi, side)
    rel = []
    for k in range(4):
        kh = k // 2
        ks = k % 2 if kh == 0 else 1 - k % 2
        rel.append(jnp.where(hi == kh, 0, 1) + jnp.where(side == ks, 0, 2))
    info = jnp.stack(
        [
            core,
            hi,
            side,
            (pair % 2 == 0).astype(jnp.int32),
            (pair == 0).astype(jnp.int32),
            (pair == lat // 2 - 1).astype(jnp.int32),
            block,
        ]
        + rel
    ).astype(jnp.int32)

    lane_t = 2 * cols + LANES
    lane_f = 4 * cols + 2 * LANES
    packed = shape(4, half, strip, lane_t, dtype=jnp.int32)
    keep, give, mine, send = call(
        functools.partial(pack_kernel, halo, edge),
        [packed, packed] + [shape(per_core, strip, lane_f)] * 2,
        info,
        source_field,
        receiver_field,
        zone_index,
        blend_weight,
    )
    swapped = move(give, across_core)
    got = [move(send[q], across_side) for q in range(per_core)]

    def spread(k):
        own = jnp.where(core == k, keep, swapped)
        return (
            own[0],
            move(own[1], across_hi),
            move(own[2], across_side),
            move(own[3], across_both),
        )

    def join(parts):
        return call(
            functools.partial(join_tables_kernel, edge),
            [shape(2, half, rows, lane_t, dtype=jnp.int32)]
            + [shape(2, half, cdiv(edge, 8) * 8, lane_t, dtype=jnp.int32)] * 2,
            info,
            *parts,
        )

    def finish(whole, send_a, send_b):
        got_a, got_b = move(send_a, pairs_even), move(send_b, pairs_odd)
        return call(
            functools.partial(tables_kernel, cols, edge, windows),
            shape(levels, held, windows * LANES),
            info,
            whole,
            move(whole, across_core),
            got_a,
            move(got_a, across_core),
            got_b,
            move(got_b, across_core),
        )

    tables = [None] * 4
    joined = [join(spread(0)), None]
    tables[0] = finish(*[x[0] for x in joined[0]])

    state = []
    for q in range(per_core):
        whole, send_a, send_b = call(
            functools.partial(join_fields_kernel, halo),
            [shape(rows, lane_f), shape(halo, lane_f), shape(halo, lane_f)],
            info,
            mine[q],
            got[q],
        )
        state.append((whole, move(send_a, pairs_even), move(send_b, pairs_odd)))

    taps = kernels(frequencies, ref_velocity)
    taps = [lax.dynamic_slice_in_dim(x, core * per_core, per_core, 0) for x in taps]
    by_rows, by_cols = operators(*taps)

    area = levels * (rows + halo) * windows * LANES
    images = []
    for s in range(4):
        image = []
        for q in range(per_core):
            out_shape = [shape(levels, rows, cols)]
            if s < 3:
                out_shape += [shape(rows, 4 * cols)] + [shape(halo, 4 * cols)] * 2
            image, *fields = call(
                functools.partial(
                    stage_kernel, levels, halo, windows, blocks, refs, s == 0, s == 3, q > 0
                ),
                out_shape,
                info,
                *state[q],
                tables[s],
                by_rows[q],
                by_cols[q],
                *([image] if q else []),
                scratch_shapes=[
                    pltpu.VMEM((2, 2, held, 2 * windows * LANES), bf16),
                    pltpu.VMEM((refs, blocks * 2 * windows * BLK, 4 * LANES), bf16),
                    pltpu.VMEM((levels, held, windows * LANES), f32),
                ],
                cost_estimate=pl.CostEstimate(
                    flops=area * 2 * refs * 2 * 3 * 512, bytes_accessed=2**21, transcendentals=0
                ),
            )
            if s < 3:
                field, send_a, send_b = fields
                got_a, got_b = move(send_a, pairs_even), move(send_b, pairs_odd)
                side_a, side_b = call(
                    functools.partial(columns_kernel, halo),
                    [shape(rows + 2 * halo, LANES)] * 2,
                    info,
                    field,
                    got_a,
                    got_b,
                )
                state[q] = (
                    field, got_a, got_b, move(side_a, across_side), move(side_b, middle),
                )
            if s == 0 and q == 0:
                keep, swapped, _ = lax.optimization_barrier((keep, swapped, image))
                joined[1] = join(spread(1))
                tables[1] = finish(*[x[0] for x in joined[1]])
                tables[2] = finish(*[x[1] for x in joined[0]])
                tables[3] = finish(*[x[1] for x in joined[1]])
        images.append(image)

    sums = [x + move(x, across_core) for x in images]
    sets = [jnp.where(core == 0, sums[2 * s], sums[2 * s + 1]) for s in range(2)]
    here = jnp.where(hi == 0, sets[0], sets[1])
    there = jnp.where(hi == 0, sets[1], sets[0])

    def strip_of(x, s):
        return lax.dynamic_slice_in_dim(x, s * strip, strip, 1)

    mine = strip_of(here, side)
    got_hi = move(strip_of(there, side), across_hi)
    got_side = move(strip_of(here, 1 - side), across_side)
    got_both = move(strip_of(there, 1 - side), across_both)
    pieces = []
    for k in range(4):
        piece = jnp.where(
            block == k,
            mine,
            jnp.where(
                place(1 - hi, side) == k,
                got_hi,
                jnp.where(place(hi, 1 - side) == k, got_side, got_both),
            ),
        )
        pieces.append(piece)
    return jnp.concatenate(pieces, axis=2) * (1.0 / freq_count)


def solution(mesh):
    in_specs = (
        P(None, None, "lat", None),
        P(None, None, "lat", None),
        P("depth", "lat", None),
        P("depth", "lat", None),
        P(),
        P(),
    )
    out_specs = P("depth", "lat", None)
    return jax.shard_map(local, mesh=mesh, in_specs=in_specs, out_specs=out_specs, check_vma=False)
```

```python
import functools
import math

import jax
import jax.numpy as jnp
from jax import lax
from jax.experimental import pallas as pl
from jax.experimental.pallas import tpu as pltpu
from jax.sharding import PartitionSpec as P

HALF = 7
BLEND = 16
TAPS = 2 * HALF + 1
SPAN = 2 * HALF
LANES = 128
WIN = LANES - SPAN
BLK = 16
AXES = ("depth", "lat")
OFF = 8

cell_width = 5.0
depth_step = 10.0
taper_width = 16.0

f32 = jnp.float32
bf16 = jnp.bfloat16


def cdiv(a, b):
    return -(-a // b)


def kernels(frequencies, ref_velocity):
    offsets = jnp.arange(-HALF, HALF + 1, dtype=jnp.int32).astype(jnp.float32)
    wavenumber = 2.0 * math.pi * frequencies.astype(jnp.float32)[:, None] / ref_velocity[None, :]
    curvature = wavenumber * (cell_width * cell_width / (2.0 * depth_step))
    phase_turn = wavenumber * depth_step
    chirp_angle = curvature[:, :, None] * (offsets * offsets)[None, None, :]
    envelope = jnp.exp(-offsets * offsets / taper_width)
    raw_re = envelope * jnp.cos(chirp_angle)
    raw_im = envelope * jnp.sin(chirp_angle)
    magnitude = jnp.sqrt(jnp.sum(raw_re, axis=-1) ** 2 + jnp.sum(raw_im, axis=-1) ** 2)[:, :, None]
    return (raw_re / magnitude, raw_im / magnitude, jnp.cos(phase_turn), jnp.sin(phase_turn))


def halves(x):
    high = lax.reduce_precision(x, 8, 7)
    return high.astype(bf16), (x - high).astype(bf16)


def operators(tap_re, tap_im, turn_cos, turn_sin):
    def band(taps, index, valid):
        out = jnp.zeros(taps.shape[:-1] + index.shape, f32)
        for m in range(TAPS):
            out = out + jnp.where((index == m) & valid, taps[..., m][..., None, None], 0.0)
        return out

    count, refs = tap_re.shape[:2]
    index = jnp.arange(2 * BLK)[None, :] - jnp.arange(BLK)[:, None]
    re, im = band(tap_re, index, True), band(tap_im, index, True)
    rows = jnp.stack([jnp.concatenate([re, -im], -1), jnp.concatenate([im, re], -1)], 2)
    high, low = halves(rows.reshape(count, refs * 2 * BLK, 4 * BLK))
    by_rows = jnp.concatenate([high, high, low], -1)
    ph_re = tap_re * turn_cos[..., None] - tap_im * turn_sin[..., None]
    ph_im = tap_re * turn_sin[..., None] + tap_im * turn_cos[..., None]
    column = jnp.arange(LANES)[None, :]
    index = jnp.arange(LANES)[:, None] - column
    re, im = band(ph_re, index, column < WIN), band(ph_im, index, column < WIN)
    cols = jnp.concatenate(
        [jnp.concatenate([re, im], -1), jnp.concatenate([-im, re], -1)], -2
    )
    high, low = halves(cols)
    by_cols = jnp.concatenate([high, high, low], -2)
    return by_rows, by_cols


def split(v):
    high = v.astype(bf16)
    return high, (v - high.astype(f32)).astype(bf16)


def window(x, start, b):
    low = start + WIN * b
    high = min(low + LANES, x.shape[1])
    part = x[:, low:high]
    if high - low < LANES:
        part = jnp.concatenate(
            [part, jnp.zeros((x.shape[0], LANES - (high - low)), x.dtype)], axis=1
        )
    return part


def dense(get, start, count):
    pieces = []
    n = start
    while n < start + count:
        b = n // WIN
        end = min(WIN * (b + 1), start + count)
        pieces.append(get(b)[:, n - WIN * b : end - WIN * b])
        n = end
    return jnp.concatenate(pieces, axis=1)


CORE, HI, SIDE, EVEN_PAIR, FIRST_PAIR, LAST_PAIR, BLOCK, REL = range(8)


def pack_kernel(halo, edge, info, src, rcv, zone, blend, keep, give, mine, send):
    per_core = mine.shape[0]
    strip, width = zone.shape[1:]
    cols = width // 4
    half = zone.shape[0] // 2
    core = info[CORE]

    def sides(x, k, n):
        left = x[:, cols * k - n : cols * k] if k > 0 else jnp.zeros((strip, n), x.dtype)
        right = x[:, cols * (k + 1) : cols * (k + 1) + n] if k < 3 else jnp.zeros((strip, n), x.dtype)
        return left, right

    for k in range(4):
        slot = info[REL + k]
        for h in range(2):
            for v in range(half):
                z = zone[h * half + v] + OFF
                w = blend[h * half + v]
                zl, zr = sides(z, k, edge)
                wl, wr = sides(w, k, edge)
                rest = jnp.zeros((strip, LANES - 4 * edge), jnp.int32)
                lanes = jnp.concatenate([zl, zr, wl, wr, rest], axis=1)

                def put(ref):
                    ref[slot, v, :, 0:cols] = z[:, cols * k : cols * (k + 1)]
                    ref[slot, v, :, cols : 2 * cols] = w[:, cols * k : cols * (k + 1)]
                    ref[slot, v, :, 2 * cols : 2 * cols + LANES] = lanes

                pl.when(core == h)(functools.partial(put, keep))
                pl.when(core != h)(functools.partial(put, give))
        for place, ref in ((0, mine), (2, send)):

            @pl.when(slot == place)
            def _():
                for q in range(per_core):
                    at = core * per_core + q
                    lefts, rights = [], []
                    for p in range(4):
                        x = (src if p < 2 else rcv)[p % 2, at]
                        if p == 3:
                            x = -x
                        ref[q, :, p * cols : (p + 1) * cols] = x[:, cols * k : cols * (k + 1)]
                        left, right = sides(x, k, halo)
                        lefts.append(left)
                        rights.append(right)
                    rest = jnp.zeros((strip, LANES - 4 * halo), f32)
                    ref[q, :, 4 * cols : 4 * cols + LANES] = jnp.concatenate(lefts + [rest], axis=1)
                    ref[q, :, 4 * cols + LANES : 4 * cols + 2 * LANES] = jnp.concatenate(
                        rights + [rest], axis=1
                    )


def edges_out(info, ref, send_a, send_b, count):
    size = ref.shape[-2]
    lead = (slice(None),) * (len(ref.shape) - 2)

    def put(top_to, bottom_to):
        top_to[lead + (slice(0, count),)] = ref[lead + (slice(0, count),)]
        bottom_to[lead + (slice(0, count),)] = ref[lead + (slice(size - count, size),)]

    pl.when(info[EVEN_PAIR] == 1)(lambda: put(send_b, send_a))
    pl.when(info[EVEN_PAIR] == 0)(lambda: put(send_a, send_b))


def join_tables_kernel(edge, info, mine, got_hi, got_side, got_both, whole, send_a, send_b):
    strip = mine.shape[1]
    for s in range(2):
        near = jnp.where(info[HI] == s, mine[...], got_hi[...])
        far = jnp.where(info[HI] == s, got_side[...], got_both[...])
        first = info[SIDE] == 0
        whole[s, :, 0:strip, :] = jnp.where(first, near, far)
        whole[s, :, strip : 2 * strip, :] = jnp.where(first, far, near)
        edges_out(info, whole.at[s], send_a.at[s], send_b.at[s], edge)


def join_fields_kernel(halo, info, mine, got, whole, send_a, send_b):
    strip = mine.shape[0]
    first = info[SIDE] == 0
    whole[0:strip, :] = jnp.where(first, mine[...], got[...])
    whole[strip : 2 * strip, :] = jnp.where(first, got[...], mine[...])
    edges_out(info, whole, send_a, send_b, halo)


def columns_kernel(halo, info, mid, got_a, got_b, send_a, send_b):
    even = info[EVEN_PAIR] == 1
    cols = mid.shape[1] // 4
    lefts, rights = [], []
    for p in range(4):
        for start, out in ((p * cols, lefts), ((p + 1) * cols - LANES, rights)):
            lanes = slice(start, start + LANES)
            a, b, m = got_a[:, lanes], got_b[:, lanes], mid[:, lanes]
            top = jnp.where(info[FIRST_PAIR] == 1, 0.0, jnp.where(even, b, a))
            bottom = jnp.where(info[LAST_PAIR] == 1, 0.0, jnp.where(even, a, b))
            rows = jnp.concatenate([top, m, bottom], axis=0)
            out.append(rows[:, :halo] if out is lefts else rows[:, LANES - halo :])
    rest = jnp.zeros((lefts[0].shape[0], LANES - 4 * halo), f32)
    left = jnp.concatenate(lefts + [rest], axis=1)
    right = jnp.concatenate(rights + [rest], axis=1)
    inner = info[BLOCK] % 2 == 0
    send_a[...] = jnp.where(inner, right, left)
    send_b[...] = jnp.where(inner, left, right)


def tables_kernel(
    cols, edge, windows, info, whole_m, whole_o, a_m, a_o, b_m, b_o, out
):
    half = whole_m.shape[0]
    levels, held = out.shape[:2]
    even = info[EVEN_PAIR] == 1
    for v in range(levels):
        own = info[CORE] == v // half
        i = v % half
        a = jnp.where(own, a_m[i], a_o[i])[:edge]
        b = jnp.where(own, b_m[i], b_o[i])[:edge]
        w = jnp.where(own, whole_m[i], whole_o[i])
        top = jnp.where(info[FIRST_PAIR] == 1, 0, jnp.where(even, b, a))
        bottom = jnp.where(info[LAST_PAIR] == 1, 0, jnp.where(even, a, b))
        x = jnp.concatenate([top, w, bottom], axis=0)
        s = 2 * cols
        z = jnp.concatenate([x[:, s : s + edge], x[:, :cols], x[:, s + edge : s + 2 * edge]], 1)
        s += 2 * edge
        w = jnp.concatenate(
            [x[:, s : s + edge], x[:, cols : 2 * cols], x[:, s + edge : s + 2 * edge]], 1
        )
        t = (z - OFF).astype(f32) + w.astype(f32) * (1.0 / BLEND)
        h = x.shape[0] - SPAN * v
        t = t[HALF * v : HALF * v + h]
        for b in range(windows):
            out[v, 0:h, b * LANES : (b + 1) * LANES] = window(t, HALF * v, b)
        out[v, h:held, :] = jnp.full((held - h, windows * LANES), -8.0, f32)


def stage_kernel(
    levels, halo, windows, blocks, refs, first, last, carried, *args
):
    args = list(args)
    info = args.pop(0)
    mid, got_a, got_b = args[:3]
    del args[:3]
    if not first:
        got_y, got_m = args[:2]
        del args[:2]
    tw_ref, a_ref, c_ref = args[:3]
    del args[:3]
    if carried:
        before = args.pop(0)
    img_ref = args.pop(0)
    if not last:
        out_ref, send_a, send_b = args[:3]
        del args[:3]
    cur_ref, y_ref, im_ref = args
    rows = mid.shape[0]
    cols = img_ref.shape[2]
    height = rows + 2 * halo
    held = cur_ref.shape[2]
    each = 2 * windows
    lanes = windows * LANES

    even = info[EVEN_PAIR] == 1
    inner = info[BLOCK] % 2 == 0

    def rows_of(lane):
        a, b = got_a[:, lane], got_b[:, lane]
        top = jnp.where(info[FIRST_PAIR] == 1, 0.0, jnp.where(even, b, a))
        bottom = jnp.where(info[LAST_PAIR] == 1, 0.0, jnp.where(even, a, b))
        return jnp.concatenate([top, mid[:, lane], bottom], axis=0)

    if first:
        left = rows_of(slice(4 * cols, 4 * cols + LANES))
        right = rows_of(slice(4 * cols + LANES, 4 * cols + 2 * LANES))
    else:
        left = jnp.where(info[BLOCK] == 0, 0.0, jnp.where(inner, got_m[...], got_y[...]))
        right = jnp.where(info[BLOCK] == 3, 0.0, jnp.where(inner, got_y[...], got_m[...]))
    for f in range(2):
        for p in range(2):
            n = 2 * f + p
            x = jnp.concatenate(
                [
                    left[:, n * halo : (n + 1) * halo],
                    rows_of(slice(n * cols, (n + 1) * cols)),
                    right[:, n * halo : (n + 1) * halo],
                ],
                axis=1,
            )
            for b in range(windows):
                high, low = split(window(x, 0, b))
                at = (f * windows + b) * LANES
                cur_ref[p, 0, 0:height, at : at + LANES] = high
                cur_ref[p, 1, 0:height, at : at + LANES] = low
    if held > height:
        cur_ref[:, :, height:held, :] = jnp.zeros((2, 2, held - height, 2 * lanes), bf16)
    lane = lax.broadcasted_iota(jnp.int32, (BLK, LANES), 1)

    def chunk(l, base, blocks):
        for k in range(blocks):
            r = pl.ds(base + BLK * k, 2 * BLK)
            rhi, rlo = cur_ref[0, 0, r, :], cur_ref[0, 1, r, :]
            ihi, ilo = cur_ref[1, 0, r, :], cur_ref[1, 1, r, :]
            rhs = jnp.concatenate([rhi, ihi, rlo, ilo, rhi, ihi], axis=0)
            g = jnp.dot(a_ref[...], rhs, preferred_element_type=f32)
            high, low = split(g)
            for j in range(refs):
                for p in range(2):
                    s = (2 * j + p) * BLK
                    for q in range(each):
                        rr = (k * each + q) * BLK
                        at = q * LANES
                        y_ref[j, rr : rr + BLK, p * LANES : (p + 1) * LANES] = high[
                            s : s + BLK, at : at + LANES
                        ]
                        y_ref[j, rr : rr + BLK, (2 + p) * LANES : (3 + p) * LANES] = low[
                            s : s + BLK, at : at + LANES
                        ]
        t = tw_ref[l, pl.ds(base, BLK * blocks), :]
        acc = None
        for j in range(refs):
            y = y_ref[j, : blocks * each * BLK]
            full = jnp.dot(
                jnp.concatenate([y, y[:, : 2 * LANES]], axis=1),
                c_ref[j],
                preferred_element_type=f32,
            )
            w = jnp.maximum(1.0 - jnp.abs(t - float(j)), 0.0)
            new = []
            for k in range(blocks):
                for f in range(2):
                    for b in range(windows):
                        rr = (k * each + f * windows + b) * BLK
                        wk = w[BLK * k : BLK * (k + 1), b * LANES : (b + 1) * LANES]
                        new.append(
                            (wk * full[rr : rr + BLK, :LANES], wk * full[rr : rr + BLK, LANES:])
                        )
            if acc is None:
                acc = new
            else:
                acc = [(a0 + b0, a1 + b1) for (a0, a1), (b0, b1) in zip(acc, new)]
        for k in range(blocks):
            r = pl.ds(base + BLK * k, BLK)
            for b in range(windows):
                s = acc[k * each + b]
                q = acc[k * each + windows + b]
                im_ref[l, r, b * LANES : (b + 1) * LANES] = s[0] * q[0] - s[1] * q[1]
            for f in range(2):
                for b in range(windows):
                    at = (f * windows + b) * LANES
                    for p in range(2):
                        v = acc[k * each + f * windows + b][p]
                        if b + 1 < windows:
                            after = pltpu.roll(acc[k * each + f * windows + b + 1][p], WIN, 1)
                            v = jnp.where(lane < WIN, v, after)
                        high, low = split(v)
                        cur_ref[p, 0, r, at : at + LANES] = high
                        cur_ref[p, 1, r, at : at + LANES] = low

    for l in range(levels):
        need = cdiv(height - SPAN * (l + 1), BLK)
        parts = cdiv(need, blocks)
        at = 0
        for i in range(parts):
            n = cdiv(need - at, parts - i)
            chunk(l, at * BLK, n)
            at += n
    if not last:
        for f in range(2):
            for p in range(2):

                def get(b):
                    at = (f * windows + b) * LANES
                    return cur_ref[p, 0, 0:rows, at : at + LANES].astype(f32) + cur_ref[
                        p, 1, 0:rows, at : at + LANES
                    ].astype(f32)

                n = 2 * f + p
                out_ref[:, n * cols : (n + 1) * cols] = dense(get, 0, cols)
        edges_out(info, out_ref, send_a, send_b, halo)
    for l in range(levels):
        o = HALF * (levels - 1 - l)
        part = dense(
            lambda b: im_ref[l, o : o + rows, b * LANES : (b + 1) * LANES], o, cols
        )
        img_ref[l] = part + before[l] if carried else part


def call(body, out_shape, info, *args, **more):
    specs = [pl.BlockSpec(memory_space=pltpu.SMEM)] + [pl.BlockSpec(memory_space=pltpu.VMEM)] * len(args)
    return pl.pallas_call(
        body,
        in_specs=specs,
        out_specs=jax.tree.map(lambda _: pl.BlockSpec(memory_space=pltpu.VMEM), out_shape),
        out_shape=out_shape,
        compiler_params=pltpu.CompilerParams(vmem_limit_bytes=40 * 2**20),
        **more,
    )(info, *args)


def shape(*dims, dtype=f32):
    return jax.ShapeDtypeStruct(dims, dtype)


def local(source_field, receiver_field, zone_index, blend_weight, ref_velocity, frequencies):
    depth, lat = lax.axis_size("depth"), lax.axis_size("lat")
    d, l = lax.axis_index("depth"), lax.axis_index("lat")
    hi, core = d // 2, d % 2
    pair, side = l // 2, l % 2
    if depth != 4 or lat % 4:
        raise ValueError("mesh")
    levels, strip, width = zone_index.shape
    freq_count, refs = frequencies.shape[0], ref_velocity.shape[0]
    per_core = freq_count // 2
    rows, cols = 2 * strip, width // 4
    halo = HALF * levels
    edge = halo - HALF
    half = levels // 2
    windows = cdiv(cols + SPAN * (levels - 1), WIN)
    blocks = 4
    held = cdiv(rows + 2 * halo - SPAN, BLK) * BLK + BLK

    def permutation(move):
        out = []
        for i in range(depth * lat):
            dd, ll = divmod(i, lat)
            h, c, p, s = dd // 2, dd % 2, ll // 2, ll % 2
            target = move(h, c, p, s)
            if target is None or not 0 <= target[2] < lat // 2:
                target = (h, 1 - c, p, s)
            h, c, p, s = target
            out.append((i, (h * 2 + c) * lat + p * 2 + s))
        return out

    across_hi = permutation(lambda h, c, p, s: (1 - h, c, p, s))
    across_side = permutation(lambda h, c, p, s: (h, c, p, 1 - s))
    across_both = permutation(lambda h, c, p, s: (1 - h, c, p, 1 - s))
    across_core = permutation(lambda h, c, p, s: (h, 1 - c, p, s))
    pairs_even = permutation(lambda h, c, p, s: (h, c, p + 1 - 2 * (p % 2), s))
    pairs_odd = permutation(lambda h, c, p, s: (h, c, p - 1 + 2 * (p % 2), s))
    middle = permutation(lambda h, c, p, s: (1 - h, c, p, s) if s == 1 else None)

    def move(x, pairs):
        return lax.ppermute(x, AXES, pairs)

    def place(h, s):
        return 2 * h + jnp.where(h == 0, s, 1 - s)

    block = place(hi, side)
    rel = []
    for k in range(4):
        kh = k // 2
        ks = k % 2 if kh == 0 else 1 - k % 2
        rel.append(jnp.where(hi == kh, 0, 1) + jnp.where(side == ks, 0, 2))
    info = jnp.stack(
        [
            core,
            hi,
            side,
            (pair % 2 == 0).astype(jnp.int32),
            (pair == 0).astype(jnp.int32),
            (pair == lat // 2 - 1).astype(jnp.int32),
            block,
        ]
        + rel
    ).astype(jnp.int32)

    lane_t = 2 * cols + LANES
    lane_f = 4 * cols + 2 * LANES
    packed = shape(4, half, strip, lane_t, dtype=jnp.int32)
    keep, give, mine, send = call(
        functools.partial(pack_kernel, halo, edge),
        [packed, packed] + [shape(per_core, strip, lane_f)] * 2,
        info,
        source_field,
        receiver_field,
        zone_index,
        blend_weight,
    )
    swapped = move(give, across_core)
    got = [move(send[q], across_side) for q in range(per_core)]

    def spread(k):
        own = jnp.where(core == k, keep, swapped)
        return (
            own[0],
            move(own[1], across_hi),
            move(own[2], across_side),
            move(own[3], across_both),
        )

    def join(parts):
        return call(
            functools.partial(join_tables_kernel, edge),
            [shape(2, half, rows, lane_t, dtype=jnp.int32)]
            + [shape(2, half, cdiv(edge, 8) * 8, lane_t, dtype=jnp.int32)] * 2,
            info,
            *parts,
        )

    def finish(whole, send_a, send_b):
        got_a, got_b = move(send_a, pairs_even), move(send_b, pairs_odd)
        return call(
            functools.partial(tables_kernel, cols, edge, windows),
            shape(levels, held, windows * LANES),
            info,
            whole,
            move(whole, across_core),
            got_a,
            move(got_a, across_core),
            got_b,
            move(got_b, across_core),
        )

    tables = [None] * 4
    joined = [join(spread(0)), None]
    tables[0] = finish(*[x[0] for x in joined[0]])

    state = []
    for q in range(per_core):
        whole, send_a, send_b = call(
            functools.partial(join_fields_kernel, halo),
            [shape(rows, lane_f), shape(halo, lane_f), shape(halo, lane_f)],
            info,
            mine[q],
            got[q],
        )
        state.append((whole, move(send_a, pairs_even), move(send_b, pairs_odd)))

    taps = kernels(frequencies, ref_velocity)
    taps = [lax.dynamic_slice_in_dim(x, core * per_core, per_core, 0) for x in taps]
    by_rows, by_cols = operators(*taps)

    area = levels * (rows + halo) * windows * LANES
    images = []
    for s in range(4):
        image = []
        for q in range(per_core):
            out_shape = [shape(levels, rows, cols)]
            if s < 3:
                out_shape += [shape(rows, 4 * cols)] + [shape(halo, 4 * cols)] * 2
            image, *fields = call(
                functools.partial(
                    stage_kernel, levels, halo, windows, blocks, refs, s == 0, s == 3, q > 0
                ),
                out_shape,
                info,
                *state[q],
                tables[s],
                by_rows[q],
                by_cols[q],
                *([image] if q else []),
                scratch_shapes=[
                    pltpu.VMEM((2, 2, held, 2 * windows * LANES), bf16),
                    pltpu.VMEM((refs, blocks * 2 * windows * BLK, 4 * LANES), bf16),
                    pltpu.VMEM((levels, held, windows * LANES), f32),
                ],
                cost_estimate=pl.CostEstimate(
                    flops=area * 2 * refs * 2 * 3 * 512, bytes_accessed=2**21, transcendentals=0
                ),
            )
            if s < 3:
                field, send_a, send_b = fields
                got_a, got_b = move(send_a, pairs_even), move(send_b, pairs_odd)
                side_a, side_b = call(
                    functools.partial(columns_kernel, halo),
                    [shape(rows + 2 * halo, LANES)] * 2,
                    info,
                    field,
                    got_a,
                    got_b,
                )
                state[q] = (
                    field, got_a, got_b, move(side_a, across_side), move(side_b, middle),
                )
            if s == 0 and q == 0:
                keep, swapped, _ = lax.optimization_barrier((keep, swapped, image))
                joined[1] = join(spread(1))
                tables[1] = finish(*[x[0] for x in joined[1]])
                tables[2] = finish(*[x[1] for x in joined[0]])
                tables[3] = finish(*[x[1] for x in joined[1]])
        images.append(image)

    sums = [x + move(x, across_core) for x in images]
    sets = [jnp.where(core == 0, sums[2 * s], sums[2 * s + 1]) for s in range(2)]
    here = jnp.where(hi == 0, sets[0], sets[1])
    there = jnp.where(hi == 0, sets[1], sets[0])

    def strip_of(x, s):
        return lax.dynamic_slice_in_dim(x, s * strip, strip, 1)

    mine = strip_of(here, side)
    got_hi = move(strip_of(there, side), across_hi)
    got_side = move(strip_of(here, 1 - side), across_side)
    got_both = move(strip_of(there, 1 - side), across_both)
    pieces = []
    for k in range(4):
        piece = jnp.where(
            block == k,
            mine,
            jnp.where(
                place(1 - hi, side) == k,
                got_hi,
                jnp.where(place(hi, 1 - side) == k, got_side, got_both),
            ),
        )
        pieces.append(piece)
    return jnp.concatenate(pieces, axis=2) * (1.0 / freq_count)


def solution(mesh):
    in_specs = (
        P(None, None, "lat", None),
        P(None, None, "lat", None),
        P("depth", "lat", None),
        P("depth", "lat", None),
        P(),
        P(),
    )
    out_specs = P("depth", "lat", None)
    return jax.shard_map(local, mesh=mesh, in_specs=in_specs, out_specs=out_specs, check_vma=False)
```

```python
import functools
import math

import jax
import jax.numpy as jnp
from jax import lax
from jax.experimental import pallas as pl
from jax.experimental.pallas import tpu as pltpu
from jax.sharding import PartitionSpec as P

HALF = 7
BLEND = 16
TAPS = 2 * HALF + 1
SPAN = 2 * HALF
LANES = 128
WIN = LANES - SPAN
BLK = 16
AXES = ("depth", "lat")
OFF = 8

cell_width = 5.0
depth_step = 10.0
taper_width = 16.0

f32 = jnp.float32
bf16 = jnp.bfloat16


def cdiv(a, b):
    return -(-a // b)


def kernels(frequencies, ref_velocity):
    offsets = jnp.arange(-HALF, HALF + 1, dtype=jnp.int32).astype(jnp.float32)
    wavenumber = 2.0 * math.pi * frequencies.astype(jnp.float32)[:, None] / ref_velocity[None, :]
    curvature = wavenumber * (cell_width * cell_width / (2.0 * depth_step))
    phase_turn = wavenumber * depth_step
    chirp_angle = curvature[:, :, None] * (offsets * offsets)[None, None, :]
    envelope = jnp.exp(-offsets * offsets / taper_width)
    raw_re = envelope * jnp.cos(chirp_angle)
    raw_im = envelope * jnp.sin(chirp_angle)
    magnitude = jnp.sqrt(jnp.sum(raw_re, axis=-1) ** 2 + jnp.sum(raw_im, axis=-1) ** 2)[:, :, None]
    return (raw_re / magnitude, raw_im / magnitude, jnp.cos(phase_turn), jnp.sin(phase_turn))


def operators(tap_re, tap_im, turn_cos, turn_sin):
    ph_re = tap_re * turn_cos[..., None] - tap_im * turn_sin[..., None]
    ph_im = tap_re * turn_sin[..., None] + tap_im * turn_cos[..., None]
    lines = jnp.stack([tap_re, tap_im, ph_re, ph_im], axis=2)
    return jnp.pad(lines, ((0, 0),) * 3 + ((0, LANES - TAPS),))


def split(v):
    high = v.astype(bf16)
    return high, (v - high.astype(f32)).astype(bf16)


def window(x, start, b):
    low = start + WIN * b
    high = min(low + LANES, x.shape[1])
    part = x[:, low:high]
    if high - low < LANES:
        part = jnp.concatenate(
            [part, jnp.zeros((x.shape[0], LANES - (high - low)), x.dtype)], axis=1
        )
    return part


def dense(get, start, count):
    pieces = []
    n = start
    while n < start + count:
        b = n // WIN
        end = min(WIN * (b + 1), start + count)
        pieces.append(get(b)[:, n - WIN * b : end - WIN * b])
        n = end
    return jnp.concatenate(pieces, axis=1)


CORE, HI, SIDE, EVEN_PAIR, FIRST_PAIR, LAST_PAIR, BLOCK, REL = range(8)


def edge_lanes(x, k, cols, n):
    none = jnp.zeros((x.shape[0], n), x.dtype)
    left = x[:, cols * k - n : cols * k] if k > 0 else none
    right = x[:, cols * (k + 1) : cols * (k + 1) + n] if k < 3 else none
    return left, right


def pack_tables_kernel(edge, info, zone, blend, keep, give):
    strip, width = zone.shape[1:]
    cols = width // 4
    half = zone.shape[0] // 2
    core = info[CORE]
    rest = jnp.zeros((strip, LANES - 4 * edge), jnp.int32)
    for k in range(4):
        slot = info[REL + k]
        for v in range(half):
            for ref, h in ((keep, core), (give, 1 - core)):
                z = zone[h * half + v] + OFF
                w = blend[h * half + v]
                zl, zr = edge_lanes(z, k, cols, edge)
                wl, wr = edge_lanes(w, k, cols, edge)
                ref[slot, v, :, 0:cols] = z[:, cols * k : cols * (k + 1)]
                ref[slot, v, :, cols : 2 * cols] = w[:, cols * k : cols * (k + 1)]
                ref[slot, v, :, 2 * cols : 2 * cols + LANES] = jnp.concatenate(
                    [zl, zr, wl, wr, rest], axis=1
                )


def pack_fields_kernel(q, halo, per_core, info, src, rcv, mine, send):
    at = info[CORE] * per_core + q
    strip, width = src.shape[2:]
    cols = width // 4
    rest = jnp.zeros((strip, LANES - 4 * halo), f32)
    for k in range(4):
        slot = info[REL + k]
        for place, ref in ((0, mine), (2, send)):

            @pl.when(slot == place)
            def _():
                lefts, rights = [], []
                for p in range(4):
                    x = (src if p < 2 else rcv)[p % 2, at]
                    if p == 3:
                        x = -x
                    ref[:, p * cols : (p + 1) * cols] = x[:, cols * k : cols * (k + 1)]
                    left, right = edge_lanes(x, k, cols, halo)
                    lefts.append(left)
                    rights.append(right)
                ref[:, 4 * cols : 4 * cols + LANES] = jnp.concatenate(lefts + [rest], axis=1)
                ref[:, 4 * cols + LANES : 4 * cols + 2 * LANES] = jnp.concatenate(
                    rights + [rest], axis=1
                )


def operators_kernel(info, lines, *outs):
    count, refs = lines.shape[:2]
    lane = lax.broadcasted_iota(jnp.int32, (LANES, LANES), 1)
    for q in range(count):
        by_rows, by_cols = outs[2 * q : 2 * q + 2]
        for j in range(refs):
            re, im, ph_re, ph_im = (lines[q, j, n : n + 1, :] for n in range(4))
            for p, line in enumerate(
                (re - pltpu.roll(im, 2 * BLK, 1), im + pltpu.roll(re, 2 * BLK, 1))
            ):
                x = pltpu.roll(
                    jnp.broadcast_to(line, (BLK, LANES)), 0, 1, stride=1, stride_axis=0
                )
                high, low = split(x)
                high, low = high[:, : 4 * BLK], low[:, : 4 * BLK]
                at = (2 * j + p) * BLK
                by_rows[at : at + BLK, :] = jnp.concatenate([high, high, low], axis=1)
            bands = []
            for line in (ph_re, ph_im):
                x = pltpu.roll(
                    jnp.broadcast_to(pltpu.roll(line, WIN, 1), (LANES, LANES)),
                    0,
                    1,
                    stride=1,
                    stride_axis=0,
                )
                bands.append(split(jnp.where(lane < WIN, x, 0.0)))
            for n, kind in enumerate((0, 0, 1)):
                x, y = bands[0][kind], bands[1][kind]
                at = 2 * LANES * n
                by_cols[j, at : at + LANES, 0:LANES] = x
                by_cols[j, at : at + LANES, LANES : 2 * LANES] = y
                by_cols[j, at + LANES : at + 2 * LANES, 0:LANES] = -y
                by_cols[j, at + LANES : at + 2 * LANES, LANES : 2 * LANES] = x


def edges_out(info, ref, send_a, send_b, count):
    size = ref.shape[-2]
    lead = (slice(None),) * (len(ref.shape) - 2)

    def put(top_to, bottom_to):
        top_to[lead + (slice(0, count),)] = ref[lead + (slice(0, count),)]
        bottom_to[lead + (slice(0, count),)] = ref[lead + (slice(size - count, size),)]

    pl.when(info[EVEN_PAIR] == 1)(lambda: put(send_b, send_a))
    pl.when(info[EVEN_PAIR] == 0)(lambda: put(send_a, send_b))


def join_tables_kernel(edge, sets, info, *refs):
    count = len(sets)
    whole, send_a, send_b = refs[4 * count :]
    first = info[SIDE] == 0
    for n, s in enumerate(sets):
        mine, got_hi, got_side, got_both = refs[4 * n : 4 * n + 4]
        strip = mine.shape[1]
        near = jnp.where(info[HI] == s, mine[...], got_hi[...])
        far = jnp.where(info[HI] == s, got_side[...], got_both[...])
        whole[n, :, 0:strip, :] = jnp.where(first, near, far)
        whole[n, :, strip : 2 * strip, :] = jnp.where(first, far, near)
        edges_out(info, whole.at[n], send_a.at[n], send_b.at[n], edge)


def join_fields_kernel(halo, info, mine, got, whole, send_a, send_b):
    strip = mine.shape[0]
    first = info[SIDE] == 0
    whole[0:strip, :] = jnp.where(first, mine[...], got[...])
    whole[strip : 2 * strip, :] = jnp.where(first, got[...], mine[...])
    edges_out(info, whole, send_a, send_b, halo)


def columns_kernel(halo, info, mid, got_a, got_b, *refs):
    send_a, send_b = refs[-2:]
    even = info[EVEN_PAIR] == 1
    cols = mid.shape[1] // 4
    lefts, rights = [], []
    for p in range(4):
        for start, out in ((p * cols, lefts), ((p + 1) * cols - LANES, rights)):
            lanes = slice(start, start + LANES)
            a, b, m = got_a[:, lanes], got_b[:, lanes], mid[:, lanes]
            top = jnp.where(info[FIRST_PAIR] == 1, 0.0, jnp.where(even, b, a))
            bottom = jnp.where(info[LAST_PAIR] == 1, 0.0, jnp.where(even, a, b))
            rows = jnp.concatenate([top, m, bottom], axis=0)
            out.append(rows[:, :halo] if out is lefts else rows[:, LANES - halo :])
    rest = jnp.zeros((lefts[0].shape[0], LANES - 4 * halo), f32)
    left = jnp.concatenate(lefts + [rest], axis=1)
    right = jnp.concatenate(rights + [rest], axis=1)
    inner = info[BLOCK] % 2 == 0
    send_a[...] = jnp.where(inner, right, left)
    send_b[...] = jnp.where(inner, left, right)


def tables_kernel(
    cols, edge, windows, n, info, whole_m, whole_o, a_m, a_o, b_m, b_o, out
):
    whole_m, whole_o, a_m, a_o, b_m, b_o = (
        x.at[n] for x in (whole_m, whole_o, a_m, a_o, b_m, b_o)
    )
    half = whole_m.shape[0]
    levels, held = out.shape[:2]
    even = info[EVEN_PAIR] == 1
    for v in range(levels):
        own = info[CORE] == v // half
        i = v % half
        a = jnp.where(own, a_m[i], a_o[i])[:edge]
        b = jnp.where(own, b_m[i], b_o[i])[:edge]
        w = jnp.where(own, whole_m[i], whole_o[i])
        top = jnp.where(info[FIRST_PAIR] == 1, 0, jnp.where(even, b, a))
        bottom = jnp.where(info[LAST_PAIR] == 1, 0, jnp.where(even, a, b))
        x = jnp.concatenate([top, w, bottom], axis=0)
        s = 2 * cols
        z = jnp.concatenate([x[:, s : s + edge], x[:, :cols], x[:, s + edge : s + 2 * edge]], 1)
        s += 2 * edge
        w = jnp.concatenate(
            [x[:, s : s + edge], x[:, cols : 2 * cols], x[:, s + edge : s + 2 * edge]], 1
        )
        t = (z - OFF).astype(f32) + w.astype(f32) * (1.0 / BLEND)
        h = x.shape[0] - SPAN * v
        t = t[HALF * v : HALF * v + h]
        for b in range(windows):
            out[v, 0:h, b * LANES : (b + 1) * LANES] = window(t, HALF * v, b)
        out[v, h:held, :] = jnp.full((held - h, windows * LANES), -8.0, f32)


def stage_kernel(
    levels, halo, windows, blocks, refs, first, last, *args
):
    args = list(args)
    info = args.pop(0)
    mid, got_a, got_b = args[:3]
    del args[:3]
    if not first:
        got_y, got_m = args[:2]
        del args[:2]
    tw_ref, a_ref, c_ref = args[:3]
    del args[:3]
    img_ref = args.pop(0)
    if not last:
        out_ref, send_a, send_b = args[:3]
        del args[:3]
    cur_ref, y_ref, im_ref = args
    rows = mid.shape[0]
    cols = img_ref.shape[2]
    height = rows + 2 * halo
    held = cur_ref.shape[2]
    each = 2 * windows
    lanes = windows * LANES

    even = info[EVEN_PAIR] == 1
    inner = info[BLOCK] % 2 == 0

    def rows_of(lane):
        a, b = got_a[:, lane], got_b[:, lane]
        top = jnp.where(info[FIRST_PAIR] == 1, 0.0, jnp.where(even, b, a))
        bottom = jnp.where(info[LAST_PAIR] == 1, 0.0, jnp.where(even, a, b))
        return jnp.concatenate([top, mid[:, lane], bottom], axis=0)

    if first:
        left = rows_of(slice(4 * cols, 4 * cols + LANES))
        right = rows_of(slice(4 * cols + LANES, 4 * cols + 2 * LANES))
    else:
        left = jnp.where(info[BLOCK] == 0, 0.0, jnp.where(inner, got_m[...], got_y[...]))
        right = jnp.where(info[BLOCK] == 3, 0.0, jnp.where(inner, got_y[...], got_m[...]))
    for f in range(2):
        for p in range(2):
            n = 2 * f + p
            x = jnp.concatenate(
                [
                    left[:, n * halo : (n + 1) * halo],
                    rows_of(slice(n * cols, (n + 1) * cols)),
                    right[:, n * halo : (n + 1) * halo],
                ],
                axis=1,
            )
            for b in range(windows):
                high, low = split(window(x, 0, b))
                at = (f * windows + b) * LANES
                cur_ref[p, 0, 0:height, at : at + LANES] = high
                cur_ref[p, 1, 0:height, at : at + LANES] = low
    if held > height:
        cur_ref[:, :, height:held, :] = jnp.zeros((2, 2, held - height, 2 * lanes), bf16)
    lane = lax.broadcasted_iota(jnp.int32, (BLK, LANES), 1)

    def chunk(l, base, blocks):
        for k in range(blocks):
            r = pl.ds(base + BLK * k, 2 * BLK)
            rhi, rlo = cur_ref[0, 0, r, :], cur_ref[0, 1, r, :]
            ihi, ilo = cur_ref[1, 0, r, :], cur_ref[1, 1, r, :]
            rhs = jnp.concatenate([rhi, ihi, rlo, ilo, rhi, ihi], axis=0)
            g = jnp.dot(a_ref[...], rhs, preferred_element_type=f32)
            high, low = split(g)
            for j in range(refs):
                for p in range(2):
                    s = (2 * j + p) * BLK
                    for q in range(each):
                        rr = (k * each + q) * BLK
                        at = q * LANES
                        y_ref[j, rr : rr + BLK, p * LANES : (p + 1) * LANES] = high[
                            s : s + BLK, at : at + LANES
                        ]
                        y_ref[j, rr : rr + BLK, (2 + p) * LANES : (3 + p) * LANES] = low[
                            s : s + BLK, at : at + LANES
                        ]
        t = tw_ref[l, pl.ds(base, BLK * blocks), :]
        acc = None
        for j in range(refs):
            y = y_ref[j, : blocks * each * BLK]
            full = jnp.dot(
                jnp.concatenate([y, y[:, : 2 * LANES]], axis=1),
                c_ref[j],
                preferred_element_type=f32,
            )
            w = jnp.maximum(1.0 - jnp.abs(t - float(j)), 0.0)
            new = []
            for k in range(blocks):
                for f in range(2):
                    for b in range(windows):
                        rr = (k * each + f * windows + b) * BLK
                        wk = w[BLK * k : BLK * (k + 1), b * LANES : (b + 1) * LANES]
                        new.append(
                            (wk * full[rr : rr + BLK, :LANES], wk * full[rr : rr + BLK, LANES:])
                        )
            if acc is None:
                acc = new
            else:
                acc = [(a0 + b0, a1 + b1) for (a0, a1), (b0, b1) in zip(acc, new)]
        for k in range(blocks):
            r = pl.ds(base + BLK * k, BLK)
            for b in range(windows):
                s = acc[k * each + b]
                q = acc[k * each + windows + b]
                im_ref[l, r, b * LANES : (b + 1) * LANES] = s[0] * q[0] - s[1] * q[1]
            for f in range(2):
                for b in range(windows):
                    at = (f * windows + b) * LANES
                    for p in range(2):
                        v = acc[k * each + f * windows + b][p]
                        if b + 1 < windows:
                            after = pltpu.roll(acc[k * each + f * windows + b + 1][p], WIN, 1)
                            v = jnp.where(lane < WIN, v, after)
                        high, low = split(v)
                        cur_ref[p, 0, r, at : at + LANES] = high
                        cur_ref[p, 1, r, at : at + LANES] = low

    for l in range(levels):
        need = cdiv(height - SPAN * (l + 1), BLK)
        parts = cdiv(need, blocks)
        at = 0
        for i in range(parts):
            n = cdiv(need - at, parts - i)
            chunk(l, at * BLK, n)
            at += n
    if not last:
        for f in range(2):
            for p in range(2):

                def get(b):
                    at = (f * windows + b) * LANES
                    return cur_ref[p, 0, 0:rows, at : at + LANES].astype(f32) + cur_ref[
                        p, 1, 0:rows, at : at + LANES
                    ].astype(f32)

                n = 2 * f + p
                out_ref[:, n * cols : (n + 1) * cols] = dense(get, 0, cols)
        edges_out(info, out_ref, send_a, send_b, halo)
    for l in range(levels):
        o = HALF * (levels - 1 - l)
        img_ref[l] = dense(
            lambda b: im_ref[l, o : o + rows, b * LANES : (b + 1) * LANES], o, cols
        )


def call(body, out_shape, info, *args, after=(), hand=(), **more):
    near = [pl.BlockSpec(memory_space=pltpu.VMEM)] * len(args)
    far = [pl.BlockSpec(memory_space=pl.ANY)]
    count = 1 + len(args)
    skip = count + len(after) + 2 * len(hand)

    def run(*refs):
        body(*refs[:count], *refs[skip:])

    out_specs = jax.tree.map(lambda _: pl.BlockSpec(memory_space=pltpu.VMEM), out_shape)
    if hand:
        out_shape = [shape(*x.shape, dtype=x.dtype) for x in hand] + out_shape
        out_specs = far * len(hand) + out_specs
        first = count + len(after)
        more["input_output_aliases"] = {first + n: n for n in range(len(hand))}
    return pl.pallas_call(
        run,
        in_specs=[pl.BlockSpec(memory_space=pltpu.SMEM)] + near + far * (len(after) + len(hand)),
        out_specs=out_specs,
        out_shape=out_shape,
        compiler_params=pltpu.CompilerParams(vmem_limit_bytes=40 * 2**20),
        **more,
    )(info, *args, *after, *hand)


def shape(*dims, dtype=f32):
    return jax.ShapeDtypeStruct(dims, dtype)


def local(source_field, receiver_field, zone_index, blend_weight, ref_velocity, frequencies):
    depth, lat = lax.axis_size("depth"), lax.axis_size("lat")
    d, l = lax.axis_index("depth"), lax.axis_index("lat")
    hi, core = d // 2, d % 2
    pair, side = l // 2, l % 2
    if depth != 4 or lat % 4:
        raise ValueError("mesh")
    levels, strip, width = zone_index.shape
    freq_count, refs = frequencies.shape[0], ref_velocity.shape[0]
    per_core = freq_count // 2
    rows, cols = 2 * strip, width // 4
    halo = HALF * levels
    edge = halo - HALF
    half = levels // 2
    windows = cdiv(cols + SPAN * (levels - 1), WIN)
    blocks = cdiv(rows + 2 * halo - SPAN, BLK)
    held = cdiv(rows + 2 * halo - SPAN, BLK) * BLK + BLK

    def permutation(move):
        out = []
        for i in range(depth * lat):
            dd, ll = divmod(i, lat)
            h, c, p, s = dd // 2, dd % 2, ll // 2, ll % 2
            target = move(h, c, p, s)
            if target is None or not 0 <= target[2] < lat // 2:
                target = (h, 1 - c, p, s)
            h, c, p, s = target
            out.append((i, (h * 2 + c) * lat + p * 2 + s))
        return out

    across_hi = permutation(lambda h, c, p, s: (1 - h, c, p, s))
    across_side = permutation(lambda h, c, p, s: (h, c, p, 1 - s))
    across_both = permutation(lambda h, c, p, s: (1 - h, c, p, 1 - s))
    across_core = permutation(lambda h, c, p, s: (h, 1 - c, p, s))
    pairs_even = permutation(lambda h, c, p, s: (h, c, p + 1 - 2 * (p % 2), s))
    pairs_odd = permutation(lambda h, c, p, s: (h, c, p - 1 + 2 * (p % 2), s))
    middle = permutation(lambda h, c, p, s: (1 - h, c, p, s) if s == 1 else None)

    def move(x, pairs):
        return lax.ppermute(x, AXES, pairs)

    def place(h, s):
        return 2 * h + jnp.where(h == 0, s, 1 - s)

    block = place(hi, side)
    rel = []
    for k in range(4):
        kh = k // 2
        ks = k % 2 if kh == 0 else 1 - k % 2
        rel.append(jnp.where(hi == kh, 0, 1) + jnp.where(side == ks, 0, 2))
    info = jnp.stack(
        [
            core,
            hi,
            side,
            (pair % 2 == 0).astype(jnp.int32),
            (pair == 0).astype(jnp.int32),
            (pair == lat // 2 - 1).astype(jnp.int32),
            block,
        ]
        + rel
    ).astype(jnp.int32)

    lane_t = 2 * cols + LANES
    lane_f = 4 * cols + 2 * LANES
    packed = shape(4, half, strip, lane_t, dtype=jnp.int32)
    keep, give = call(
        functools.partial(pack_tables_kernel, edge),
        [packed, packed],
        info,
        zone_index,
        blend_weight,
    )
    swapped = move(give, across_core)

    def pack_fields(q, after):
        mine, send = call(
            functools.partial(pack_fields_kernel, q, halo, per_core),
            [shape(strip, lane_f)] * 2,
            info,
            source_field,
            receiver_field,
            after=after,
        )
        return mine, move(send, across_side)

    def spread(own):
        return (
            own[0],
            move(own[1], across_hi),
            move(own[2], across_side),
            move(own[3], across_both),
        )

    def join(sets, parts, after):
        edges = shape(len(sets), half, cdiv(edge, 8) * 8, lane_t, dtype=jnp.int32)
        whole, send_a, send_b = call(
            functools.partial(join_tables_kernel, edge, sets),
            [shape(len(sets), half, rows, lane_t, dtype=jnp.int32), edges, edges],
            info,
            *parts,
            after=after,
        )
        return (
            whole,
            move(whole, across_core),
            move(send_a, pairs_even),
            move(send_b, pairs_odd),
        )

    def finish(whole, other, got_a, got_b):
        swap_a, swap_b = move(got_a, across_core), move(got_b, across_core)
        return [
            call(
                functools.partial(tables_kernel, cols, edge, windows, n),
                shape(levels, held, windows * LANES),
                info,
                whole,
                other,
                got_a,
                swap_a,
                got_b,
                swap_b,
            )
            for n in range(whole.shape[0])
        ]

    parts = [spread(jnp.where(core == 0, keep, swapped)), None]

    taps = kernels(frequencies, ref_velocity)
    taps = [lax.dynamic_slice_in_dim(x, core * per_core, per_core, 0) for x in taps]
    matrices = call(
        operators_kernel,
        [
            shape(refs * 2 * BLK, 12 * BLK, dtype=bf16),
            shape(refs, 6 * LANES, 2 * LANES, dtype=bf16),
        ]
        * per_core,
        info,
        operators(*taps),
        after=[give],
    )

    def join_fields(mine, got, after):
        whole, send_a, send_b = call(
            functools.partial(join_fields_kernel, halo),
            [shape(rows, lane_f), shape(halo, lane_f), shape(halo, lane_f)],
            info,
            mine,
            got,
            after=after,
        )
        return whole, move(send_a, pairs_even), move(send_b, pairs_odd)

    ahead = join_fields(*pack_fields(0, [give]), [matrices[0]])
    later = [pack_fields(q, [ahead[0]]) for q in range(1, per_core)]
    joined = join((0,), parts[0], [ahead[0]] + [x[0] for x in later])
    tables = finish(*joined)
    state = [ahead] + [join_fields(*x, [joined[0]]) for x in later]
    parts[1] = spread(jnp.where(core == 1, keep, swapped))

    area = levels * (rows + halo) * windows * LANES
    images = []
    before = [parts[1][0]]
    for s in range(4):
        image, results = [], []
        for q in range(per_core):
            out_shape = [shape(levels, rows, cols)]
            if s < 3:
                out_shape += [shape(rows, 4 * cols)] + [shape(halo, 4 * cols)] * 2
            part, *fields = call(
                functools.partial(
                    stage_kernel, levels, halo, windows, blocks, refs, s == 0, s == 3
                ),
                out_shape,
                info,
                *state[q],
                tables[s],
                matrices[2 * q],
                matrices[2 * q + 1],
                after=before,
                scratch_shapes=[
                    pltpu.VMEM((2, 2, held, 2 * windows * LANES), bf16),
                    pltpu.VMEM((refs, blocks * 2 * windows * BLK, 4 * LANES), bf16),
                    pltpu.VMEM((levels, held, windows * LANES), f32),
                ],
                cost_estimate=pl.CostEstimate(
                    flops=area * 4 * refs * 2 * 3 * 512, bytes_accessed=2**21, transcendentals=0
                ),
            )
            image.append(part)
            if s < 3:
                results.append(fields)
            before = []
            if q == 0 and s < 2:
                sets, arrays = ((0,), parts[1]) if s == 0 else ((1, 1), parts[0] + parts[1])
                joined = join(sets, arrays, [part])
                before = [joined[0]]
        images.append(image)
        sends = [None] * per_core
        arrived = []
        for q in range(len(results)):
            field, *edges = results[q]
            sends[q] = edges if q == 0 else sends[q]
            got = [move(sends[q][0], pairs_even), move(sends[q][1], pairs_odd)]
            hand = results[q + 1][1:] if q + 1 < per_core else []
            if q == 0 and s < 2:
                hand = hand + list(joined[2:])
            *handed, side_a, side_b = call(
                functools.partial(columns_kernel, halo),
                [shape(rows + 2 * halo, LANES)] * 2,
                info,
                field,
                *got,
                after=arrived,
                hand=hand,
            )
            if q + 1 < per_core:
                sends[q + 1] = handed[:2]
            if q == 0 and s < 2:
                tables += finish(*joined[:2], *handed[-2:])
            arrived = [move(side_a, across_side), move(side_b, middle), tables[s + 1]]
            state[q] = (field, *got, *arrived[:2])
            before = [side_a]

    sums = [sum(x) for x in images]
    sums = [x + move(x, across_core) for x in sums]
    sets = [jnp.where(core == 0, sums[2 * s], sums[2 * s + 1]) for s in range(2)]
    here = jnp.where(hi == 0, sets[0], sets[1])
    there = jnp.where(hi == 0, sets[1], sets[0])

    def strip_of(x, s):
        return lax.dynamic_slice_in_dim(x, s * strip, strip, 1)

    mine = strip_of(here, side)
    got_hi = move(strip_of(there, side), across_hi)
    got_side = move(strip_of(here, 1 - side), across_side)
    got_both = move(strip_of(there, 1 - side), across_both)
    pieces = []
    for k in range(4):
        piece = jnp.where(
            block == k,
            mine,
            jnp.where(
                place(1 - hi, side) == k,
                got_hi,
                jnp.where(place(hi, 1 - side) == k, got_side, got_both),
            ),
        )
        pieces.append(piece)
    return jnp.concatenate(pieces, axis=2) * (1.0 / freq_count)


def solution(mesh):
    in_specs = (
        P(None, None, "lat", None),
        P(None, None, "lat", None),
        P("depth", "lat", None),
        P("depth", "lat", None),
        P(),
        P(),
    )
    out_specs = P("depth", "lat", None)
    return jax.shard_map(local, mesh=mesh, in_specs=in_specs, out_specs=out_specs, check_vma=False)
```

```python
import functools
import math

import jax
import jax.numpy as jnp
from jax import lax
from jax.experimental import pallas as pl
from jax.experimental.pallas import tpu as pltpu
from jax.sharding import PartitionSpec as P

HALF = 7
BLEND = 16
TAPS = 2 * HALF + 1
SPAN = 2 * HALF
LANES = 128
WIN = LANES - SPAN
BLK = 16
AXES = ("depth", "lat")
OFF = 8

cell_width = 5.0
depth_step = 10.0
taper_width = 16.0

f32 = jnp.float32
bf16 = jnp.bfloat16


def cdiv(a, b):
    return -(-a // b)


def kernels(frequencies, ref_velocity):
    offsets = jnp.arange(-HALF, HALF + 1, dtype=jnp.int32).astype(jnp.float32)
    wavenumber = 2.0 * math.pi * frequencies.astype(jnp.float32)[:, None] / ref_velocity[None, :]
    curvature = wavenumber * (cell_width * cell_width / (2.0 * depth_step))
    phase_turn = wavenumber * depth_step
    chirp_angle = curvature[:, :, None] * (offsets * offsets)[None, None, :]
    envelope = jnp.exp(-offsets * offsets / taper_width)
    raw_re = envelope * jnp.cos(chirp_angle)
    raw_im = envelope * jnp.sin(chirp_angle)
    magnitude = jnp.sqrt(jnp.sum(raw_re, axis=-1) ** 2 + jnp.sum(raw_im, axis=-1) ** 2)[:, :, None]
    return (raw_re / magnitude, raw_im / magnitude, jnp.cos(phase_turn), jnp.sin(phase_turn))


def operators(tap_re, tap_im, turn_cos, turn_sin):
    ph_re = tap_re * turn_cos[..., None] - tap_im * turn_sin[..., None]
    ph_im = tap_re * turn_sin[..., None] + tap_im * turn_cos[..., None]
    lines = jnp.stack([tap_re, tap_im, ph_re, ph_im], axis=2)
    return jnp.pad(lines, ((0, 0),) * 3 + ((0, LANES - TAPS),))


def split(v):
    high = v.astype(bf16)
    return high, (v - high.astype(f32)).astype(bf16)


def window(x, start, b):
    low = start + WIN * b
    high = min(low + LANES, x.shape[1])
    part = x[:, low:high]
    if high - low < LANES:
        part = jnp.concatenate(
            [part, jnp.zeros((x.shape[0], LANES - (high - low)), x.dtype)], axis=1
        )
    return part


def dense(get, start, count):
    pieces = []
    n = start
    while n < start + count:
        b = n // WIN
        end = min(WIN * (b + 1), start + count)
        pieces.append(get(b)[:, n - WIN * b : end - WIN * b])
        n = end
    return jnp.concatenate(pieces, axis=1)


CORE, HI, SIDE, EVEN_PAIR, FIRST_PAIR, LAST_PAIR, BLOCK, REL = range(8)


def edge_lanes(x, k, cols, n):
    none = jnp.zeros((x.shape[0], n), x.dtype)
    left = x[:, cols * k - n : cols * k] if k > 0 else none
    right = x[:, cols * (k + 1) : cols * (k + 1) + n] if k < 3 else none
    return left, right


def pack_tables_kernel(edge, info, zone, blend, keep, give):
    strip, width = zone.shape[1:]
    cols = width // 4
    half = zone.shape[0] // 2
    core = info[CORE]
    rest = jnp.zeros((strip, LANES - 4 * edge), jnp.int32)
    for k in range(4):
        slot = info[REL + k]
        for v in range(half):
            for ref, h in ((keep, core), (give, 1 - core)):
                z = zone[h * half + v] + OFF
                w = blend[h * half + v]
                zl, zr = edge_lanes(z, k, cols, edge)
                wl, wr = edge_lanes(w, k, cols, edge)
                ref[slot, v, :, 0:cols] = z[:, cols * k : cols * (k + 1)]
                ref[slot, v, :, cols : 2 * cols] = w[:, cols * k : cols * (k + 1)]
                ref[slot, v, :, 2 * cols : 2 * cols + LANES] = jnp.concatenate(
                    [zl, zr, wl, wr, rest], axis=1
                )


def pack_fields_kernel(halo, info, src, rcv, mine, send):
    per_core = mine.shape[0]
    strip, width = src.shape[2:]
    cols = width // 4
    rest = jnp.zeros((strip, LANES - 4 * halo), f32)
    for k in range(4):
        slot = info[REL + k]
        for place, ref in ((0, mine), (2, send)):

            @pl.when(slot == place)
            def _():
                for q in range(per_core):
                    at = info[CORE] * per_core + q
                    lefts, rights = [], []
                    for p in range(4):
                        x = (src if p < 2 else rcv)[p % 2, at]
                        if p == 3:
                            x = -x
                        ref[q, :, p * cols : (p + 1) * cols] = x[:, cols * k : cols * (k + 1)]
                        left, right = edge_lanes(x, k, cols, halo)
                        lefts.append(left)
                        rights.append(right)
                    ref[q, :, 4 * cols : 4 * cols + LANES] = jnp.concatenate(
                        lefts + [rest], axis=1
                    )
                    ref[q, :, 4 * cols + LANES : 4 * cols + 2 * LANES] = jnp.concatenate(
                        rights + [rest], axis=1
                    )


def operators_kernel(info, lines, rows_out, cols_out):
    count, refs = lines.shape[:2]
    lane = lax.broadcasted_iota(jnp.int32, (LANES, LANES), 1)
    for q in range(count):
        by_rows, by_cols = rows_out.at[q], cols_out.at[q]
        for j in range(refs):
            re, im, ph_re, ph_im = (lines[q, j, n : n + 1, :] for n in range(4))
            for p, line in enumerate(
                (re - pltpu.roll(im, 2 * BLK, 1), im + pltpu.roll(re, 2 * BLK, 1))
            ):
                x = pltpu.roll(
                    jnp.broadcast_to(line, (BLK, LANES)), 0, 1, stride=1, stride_axis=0
                )
                high, low = split(x)
                high, low = high[:, : 4 * BLK], low[:, : 4 * BLK]
                at = (2 * j + p) * BLK
                by_rows[at : at + BLK, :] = jnp.concatenate([high, high, low], axis=1)
            bands = []
            for line in (ph_re, ph_im):
                x = pltpu.roll(
                    jnp.broadcast_to(pltpu.roll(line, WIN, 1), (LANES, LANES)),
                    0,
                    1,
                    stride=1,
                    stride_axis=0,
                )
                bands.append(split(jnp.where(lane < WIN, x, 0.0)))
            for n, kind in enumerate((0, 0, 1)):
                x, y = bands[0][kind], bands[1][kind]
                at = 2 * LANES * n
                by_cols[j, at : at + LANES, 0:LANES] = x
                by_cols[j, at : at + LANES, LANES : 2 * LANES] = y
                by_cols[j, at + LANES : at + 2 * LANES, 0:LANES] = -y
                by_cols[j, at + LANES : at + 2 * LANES, LANES : 2 * LANES] = x


def edges_out(info, ref, send_a, send_b, count):
    size = ref.shape[-2]
    lead = (slice(None),) * (len(ref.shape) - 2)

    def put(top_to, bottom_to):
        top_to[lead + (slice(0, count),)] = ref[lead + (slice(0, count),)]
        bottom_to[lead + (slice(0, count),)] = ref[lead + (slice(size - count, size),)]

    pl.when(info[EVEN_PAIR] == 1)(lambda: put(send_b, send_a))
    pl.when(info[EVEN_PAIR] == 0)(lambda: put(send_a, send_b))


def join_tables_kernel(edge, sets, info, *refs):
    count = len(sets)
    whole, send_a, send_b, token = refs[4 * count :]
    token[...] = jnp.zeros_like(token)
    first = info[SIDE] == 0
    for n, s in enumerate(sets):
        mine, got_hi, got_side, got_both = refs[4 * n : 4 * n + 4]
        strip = mine.shape[1]
        near = jnp.where(info[HI] == s, mine[...], got_hi[...])
        far = jnp.where(info[HI] == s, got_side[...], got_both[...])
        whole[n, :, 0:strip, :] = jnp.where(first, near, far)
        whole[n, :, strip : 2 * strip, :] = jnp.where(first, far, near)
        edges_out(info, whole.at[n], send_a.at[n], send_b.at[n], edge)


def join_fields_kernel(halo, info, mine, got, whole, send_a, send_b, token):
    token[...] = jnp.zeros_like(token)
    strip = mine.shape[1]
    first = info[SIDE] == 0
    whole[:, 0:strip, :] = jnp.where(first, mine[...], got[...])
    whole[:, strip : 2 * strip, :] = jnp.where(first, got[...], mine[...])
    edges_out(info, whole, send_a, send_b, halo)


def columns_kernel(halo, info, mid, got_a, got_b, *refs):
    send_a, send_b, token = refs
    token[...] = jnp.zeros_like(token)
    even = info[EVEN_PAIR] == 1
    inner = info[BLOCK] % 2 == 0
    cols = mid.shape[2] // 4
    for q in range(mid.shape[0]):
        lefts, rights = [], []
        for p in range(4):
            for start, out in ((p * cols, lefts), ((p + 1) * cols - LANES, rights)):
                lanes = slice(start, start + LANES)
                a, b, m = got_a[q, :, lanes], got_b[q, :, lanes], mid[q, :, lanes]
                top = jnp.where(info[FIRST_PAIR] == 1, 0.0, jnp.where(even, b, a))
                bottom = jnp.where(info[LAST_PAIR] == 1, 0.0, jnp.where(even, a, b))
                rows = jnp.concatenate([top, m, bottom], axis=0)
                out.append(rows[:, :halo] if out is lefts else rows[:, LANES - halo :])
        rest = jnp.zeros((lefts[0].shape[0], LANES - 4 * halo), f32)
        left = jnp.concatenate(lefts + [rest], axis=1)
        right = jnp.concatenate(rights + [rest], axis=1)
        send_a[q] = jnp.where(inner, right, left)
        send_b[q] = jnp.where(inner, left, right)


def tables_kernel(
    cols, edge, windows, n, info, whole_m, whole_o, a_m, a_o, b_m, b_o, out
):
    whole_m, whole_o, a_m, a_o, b_m, b_o = (
        x.at[n] for x in (whole_m, whole_o, a_m, a_o, b_m, b_o)
    )
    half = whole_m.shape[0]
    levels, held = out.shape[:2]
    even = info[EVEN_PAIR] == 1
    for v in range(levels):
        own = info[CORE] == v // half
        i = v % half
        a = jnp.where(own, a_m[i], a_o[i])[:edge]
        b = jnp.where(own, b_m[i], b_o[i])[:edge]
        w = jnp.where(own, whole_m[i], whole_o[i])
        top = jnp.where(info[FIRST_PAIR] == 1, 0, jnp.where(even, b, a))
        bottom = jnp.where(info[LAST_PAIR] == 1, 0, jnp.where(even, a, b))
        x = jnp.concatenate([top, w, bottom], axis=0)
        s = 2 * cols
        z = jnp.concatenate([x[:, s : s + edge], x[:, :cols], x[:, s + edge : s + 2 * edge]], 1)
        s += 2 * edge
        w = jnp.concatenate(
            [x[:, s : s + edge], x[:, cols : 2 * cols], x[:, s + edge : s + 2 * edge]], 1
        )
        t = (z - OFF).astype(f32) + w.astype(f32) * (1.0 / BLEND)
        h = x.shape[0] - SPAN * v
        t = t[HALF * v : HALF * v + h]
        for b in range(windows):
            out[v, 0:h, b * LANES : (b + 1) * LANES] = window(t, HALF * v, b)
        out[v, h:held, :] = jnp.full((held - h, windows * LANES), -8.0, f32)


def stage_kernel(levels, halo, windows, blocks, refs, first, last, *args):
    args = list(args)
    info, token = args[:2]
    count = 3 if first else 5
    fields = args[2 : 2 + count]
    tw_ref, a_ref, c_ref = args[2 + count : 5 + count]
    img_ref = args[5 + count]
    outs = args[6 + count : 6 + count + (0 if last else 3)]
    scratch = args[6 + count + len(outs) :]

    def one(q, carry):
        stage_one(
            levels, halo, windows, blocks, refs, first, last, q,
            info, *(x.at[q] for x in fields), tw_ref, a_ref.at[q], c_ref.at[q], img_ref,
            *(x.at[q] for x in outs), *scratch,
        )
        return carry

    lax.fori_loop(0, fields[0].shape[0], one, 0)


def stage_one(levels, halo, windows, blocks, refs, first, last, freq, *args):
    args = list(args)
    info = args.pop(0)
    mid, got_a, got_b = args[:3]
    del args[:3]
    if not first:
        got_y, got_m = args[:2]
        del args[:2]
    tw_ref, a_ref, c_ref = args[:3]
    del args[:3]
    img_ref = args.pop(0)
    if not last:
        out_ref, send_a, send_b = args[:3]
        del args[:3]
    cur_ref, y_ref, im_ref = args
    rows = mid.shape[0]
    cols = img_ref.shape[2]
    height = rows + 2 * halo
    held = cur_ref.shape[2]
    each = 2 * windows
    lanes = windows * LANES

    even = info[EVEN_PAIR] == 1
    inner = info[BLOCK] % 2 == 0

    def rows_of(lane):
        a, b = got_a[:, lane], got_b[:, lane]
        top = jnp.where(info[FIRST_PAIR] == 1, 0.0, jnp.where(even, b, a))
        bottom = jnp.where(info[LAST_PAIR] == 1, 0.0, jnp.where(even, a, b))
        return jnp.concatenate([top, mid[:, lane], bottom], axis=0)

    if first:
        left = rows_of(slice(4 * cols, 4 * cols + LANES))
        right = rows_of(slice(4 * cols + LANES, 4 * cols + 2 * LANES))
    else:
        left = jnp.where(info[BLOCK] == 0, 0.0, jnp.where(inner, got_m[...], got_y[...]))
        right = jnp.where(info[BLOCK] == 3, 0.0, jnp.where(inner, got_y[...], got_m[...]))
    for f in range(2):
        for p in range(2):
            n = 2 * f + p
            x = jnp.concatenate(
                [
                    left[:, n * halo : (n + 1) * halo],
                    rows_of(slice(n * cols, (n + 1) * cols)),
                    right[:, n * halo : (n + 1) * halo],
                ],
                axis=1,
            )
            for b in range(windows):
                high, low = split(window(x, 0, b))
                at = (f * windows + b) * LANES
                cur_ref[p, 0, 0:height, at : at + LANES] = high
                cur_ref[p, 1, 0:height, at : at + LANES] = low
    if held > height:
        cur_ref[:, :, height:held, :] = jnp.zeros((2, 2, held - height, 2 * lanes), bf16)
    lane = lax.broadcasted_iota(jnp.int32, (BLK, LANES), 1)

    def chunk(l, base, blocks):
        for k in range(blocks):
            r = pl.ds(base + BLK * k, 2 * BLK)
            rhi, rlo = cur_ref[0, 0, r, :], cur_ref[0, 1, r, :]
            ihi, ilo = cur_ref[1, 0, r, :], cur_ref[1, 1, r, :]
            rhs = jnp.concatenate([rhi, ihi, rlo, ilo, rhi, ihi], axis=0)
            g = jnp.dot(a_ref[...], rhs, preferred_element_type=f32)
            high, low = split(g)
            for j in range(refs):
                for p in range(2):
                    s = (2 * j + p) * BLK
                    for q in range(each):
                        rr = (k * each + q) * BLK
                        at = q * LANES
                        y_ref[j, rr : rr + BLK, p * LANES : (p + 1) * LANES] = high[
                            s : s + BLK, at : at + LANES
                        ]
                        y_ref[j, rr : rr + BLK, (2 + p) * LANES : (3 + p) * LANES] = low[
                            s : s + BLK, at : at + LANES
                        ]
        t = tw_ref[l, pl.ds(base, BLK * blocks), :]
        acc = None
        for j in range(refs):
            y = y_ref[j, : blocks * each * BLK]
            full = jnp.dot(
                jnp.concatenate([y, y[:, : 2 * LANES]], axis=1),
                c_ref[j],
                preferred_element_type=f32,
            )
            w = jnp.maximum(1.0 - jnp.abs(t - float(j)), 0.0)
            new = []
            for k in range(blocks):
                for f in range(2):
                    for b in range(windows):
                        rr = (k * each + f * windows + b) * BLK
                        wk = w[BLK * k : BLK * (k + 1), b * LANES : (b + 1) * LANES]
                        new.append(
                            (wk * full[rr : rr + BLK, :LANES], wk * full[rr : rr + BLK, LANES:])
                        )
            if acc is None:
                acc = new
            else:
                acc = [(a0 + b0, a1 + b1) for (a0, a1), (b0, b1) in zip(acc, new)]
        for k in range(blocks):
            r = pl.ds(base + BLK * k, BLK)
            for b in range(windows):
                s = acc[k * each + b]
                q = acc[k * each + windows + b]
                im_ref[l, r, b * LANES : (b + 1) * LANES] = s[0] * q[0] - s[1] * q[1]
            for f in range(2):
                for b in range(windows):
                    at = (f * windows + b) * LANES
                    for p in range(2):
                        v = acc[k * each + f * windows + b][p]
                        if b + 1 < windows:
                            after = pltpu.roll(acc[k * each + f * windows + b + 1][p], WIN, 1)
                            v = jnp.where(lane < WIN, v, after)
                        high, low = split(v)
                        cur_ref[p, 0, r, at : at + LANES] = high
                        cur_ref[p, 1, r, at : at + LANES] = low

    for l in range(levels):
        need = cdiv(height - SPAN * (l + 1), BLK)
        parts = cdiv(need, blocks)
        at = 0
        for i in range(parts):
            n = cdiv(need - at, parts - i)
            chunk(l, at * BLK, n)
            at += n
    if not last:
        for f in range(2):
            for p in range(2):

                def get(b):
                    at = (f * windows + b) * LANES
                    return cur_ref[p, 0, 0:rows, at : at + LANES].astype(f32) + cur_ref[
                        p, 1, 0:rows, at : at + LANES
                    ].astype(f32)

                n = 2 * f + p
                out_ref[:, n * cols : (n + 1) * cols] = dense(get, 0, cols)
        edges_out(info, out_ref, send_a, send_b, halo)
    for l in range(levels):
        o = HALF * (levels - 1 - l)
        part = dense(
            lambda b: im_ref[l, o : o + rows, b * LANES : (b + 1) * LANES], o, cols
        )
        img_ref[l] = jnp.where(freq == 0, part, img_ref[l] + part)


def call(body, out_shape, info, *args, after=(), hand=(), **more):
    near = [pl.BlockSpec(memory_space=pltpu.VMEM)] * len(args)
    far = [pl.BlockSpec(memory_space=pl.ANY)]
    count = 1 + len(args)
    skip = count + len(after) + 2 * len(hand)

    def run(*refs):
        body(*refs[:count], *refs[skip:])

    out_specs = jax.tree.map(lambda _: pl.BlockSpec(memory_space=pltpu.VMEM), out_shape)
    if hand:
        out_shape = [shape(*x.shape, dtype=x.dtype) for x in hand] + out_shape
        out_specs = far * len(hand) + out_specs
        first = count + len(after)
        more["input_output_aliases"] = {first + n: n for n in range(len(hand))}
    return pl.pallas_call(
        run,
        in_specs=[pl.BlockSpec(memory_space=pltpu.SMEM)] + near + far * (len(after) + len(hand)),
        out_specs=out_specs,
        out_shape=out_shape,
        compiler_params=pltpu.CompilerParams(vmem_limit_bytes=40 * 2**20),
        **more,
    )(info, *args, *after, *hand)


def shape(*dims, dtype=f32):
    return jax.ShapeDtypeStruct(dims, dtype)


def local(source_field, receiver_field, zone_index, blend_weight, ref_velocity, frequencies):
    depth, lat = lax.axis_size("depth"), lax.axis_size("lat")
    d, l = lax.axis_index("depth"), lax.axis_index("lat")
    hi, core = d // 2, d % 2
    pair, side = l // 2, l % 2
    if depth != 4 or lat % 4:
        raise ValueError("mesh")
    levels, strip, width = zone_index.shape
    freq_count, refs = frequencies.shape[0], ref_velocity.shape[0]
    per_core = freq_count // 2
    rows, cols = 2 * strip, width // 4
    halo = HALF * levels
    edge = halo - HALF
    half = levels // 2
    windows = cdiv(cols + SPAN * (levels - 1), WIN)
    blocks = cdiv(rows + 2 * halo - SPAN, BLK)
    held = cdiv(rows + 2 * halo - SPAN, BLK) * BLK + BLK

    def permutation(move):
        out = []
        for i in range(depth * lat):
            dd, ll = divmod(i, lat)
            h, c, p, s = dd // 2, dd % 2, ll // 2, ll % 2
            target = move(h, c, p, s)
            if target is None or not 0 <= target[2] < lat // 2:
                target = (h, 1 - c, p, s)
            h, c, p, s = target
            out.append((i, (h * 2 + c) * lat + p * 2 + s))
        return out

    across_hi = permutation(lambda h, c, p, s: (1 - h, c, p, s))
    across_side = permutation(lambda h, c, p, s: (h, c, p, 1 - s))
    across_both = permutation(lambda h, c, p, s: (1 - h, c, p, 1 - s))
    across_core = permutation(lambda h, c, p, s: (h, 1 - c, p, s))
    pairs_even = permutation(lambda h, c, p, s: (h, c, p + 1 - 2 * (p % 2), s))
    pairs_odd = permutation(lambda h, c, p, s: (h, c, p - 1 + 2 * (p % 2), s))
    middle = permutation(lambda h, c, p, s: (1 - h, c, p, s) if s == 1 else None)

    def move(x, pairs):
        return lax.ppermute(x, AXES, pairs)

    def place(h, s):
        return 2 * h + jnp.where(h == 0, s, 1 - s)

    block = place(hi, side)
    rel = []
    for k in range(4):
        kh = k // 2
        ks = k % 2 if kh == 0 else 1 - k % 2
        rel.append(jnp.where(hi == kh, 0, 1) + jnp.where(side == ks, 0, 2))
    info = jnp.stack(
        [
            core,
            hi,
            side,
            (pair % 2 == 0).astype(jnp.int32),
            (pair == 0).astype(jnp.int32),
            (pair == lat // 2 - 1).astype(jnp.int32),
            block,
        ]
        + rel
    ).astype(jnp.int32)

    mark = shape(8, LANES)
    lane_t = 2 * cols + LANES
    lane_f = 4 * cols + 2 * LANES
    packed = shape(4, half, strip, lane_t, dtype=jnp.int32)
    keep, give = call(
        functools.partial(pack_tables_kernel, edge),
        [packed, packed],
        info,
        zone_index,
        blend_weight,
    )
    swapped = move(give, across_core)

    mine, send = call(
        functools.partial(pack_fields_kernel, halo),
        [shape(per_core, strip, lane_f)] * 2,
        info,
        source_field,
        receiver_field,
        after=[give],
    )
    got = move(send, across_side)

    def spread(own):
        return (
            own[0],
            move(own[1], across_hi),
            move(own[2], across_side),
            move(own[3], across_both),
        )

    def join(sets, parts, after):
        edges = shape(len(sets), half, cdiv(edge, 8) * 8, lane_t, dtype=jnp.int32)
        whole, send_a, send_b, token = call(
            functools.partial(join_tables_kernel, edge, sets),
            [shape(len(sets), half, rows, lane_t, dtype=jnp.int32), edges, edges, mark],
            info,
            *parts,
            after=after,
        )
        return (
            whole,
            move(whole, across_core),
            move(send_a, pairs_even),
            move(send_b, pairs_odd),
            token,
        )

    def finish(whole, other, got_a, got_b):
        swap_a, swap_b = move(got_a, across_core), move(got_b, across_core)
        return [
            call(
                functools.partial(tables_kernel, cols, edge, windows, n),
                shape(levels, held, windows * LANES),
                info,
                whole,
                other,
                got_a,
                swap_a,
                got_b,
                swap_b,
            )
            for n in range(whole.shape[0])
        ]

    parts = [spread(jnp.where(core == 0, keep, swapped)), None]

    taps = kernels(frequencies, ref_velocity)
    taps = [lax.dynamic_slice_in_dim(x, core * per_core, per_core, 0) for x in taps]
    matrices = call(
        operators_kernel,
        [
            shape(per_core, refs * 2 * BLK, 12 * BLK, dtype=bf16),
            shape(per_core, refs, 6 * LANES, 2 * LANES, dtype=bf16),
        ],
        info,
        operators(*taps),
        after=[give],
    )

    *joined, token = join((0,), parts[0], [matrices[0]])
    tables = finish(*joined)
    parts[1] = spread(jnp.where(core == 1, keep, swapped))
    whole, send_a, send_b, token = call(
        functools.partial(join_fields_kernel, halo),
        [shape(per_core, rows, lane_f)] + [shape(per_core, halo, lane_f)] * 2 + [mark],
        info,
        mine,
        got,
        after=[joined[0]],
    )
    state = (whole, move(send_a, pairs_even), move(send_b, pairs_odd))

    area = levels * (rows + halo) * windows * LANES
    images = []
    for s in range(4):
        out_shape = [shape(levels, rows, cols)]
        if s < 3:
            out_shape += [shape(per_core, rows, 4 * cols)] + [shape(per_core, halo, 4 * cols)] * 2
        image, *fields = call(
            functools.partial(
                stage_kernel, levels, halo, windows, blocks, refs, s == 0, s == 3
            ),
            out_shape,
            info,
            token,
            *state,
            tables[s],
            *matrices,
            scratch_shapes=[
                pltpu.VMEM((2, 2, held, 2 * windows * LANES), bf16),
                pltpu.VMEM((refs, blocks * 2 * windows * BLK, 4 * LANES), bf16),
                pltpu.VMEM((levels, held, windows * LANES), f32),
            ],
            cost_estimate=pl.CostEstimate(
                flops=area * 8 * refs * 2 * 3 * 512, bytes_accessed=2**21, transcendentals=0
            ),
        )
        images.append(image)
        if s == 3:
            break
        if s == 0:
            *joined, _ = join((0,), parts[1], [image])
        field, send_a, send_b = fields
        got = [move(send_a, pairs_even), move(send_b, pairs_odd)]
        *handed, side_a, side_b, token = call(
            functools.partial(columns_kernel, halo),
            [shape(per_core, rows + 2 * halo, LANES)] * 2 + [mark],
            info,
            field,
            *got,
            hand=list(joined[2:]) if s < 2 else [],
        )
        state = (field, *got, move(side_a, across_side), move(side_b, middle))
        if s < 2:
            tables += finish(*joined[:2], *handed)
        if s == 0:
            *joined, token = join((1, 1), parts[0] + parts[1], [token])

    sums = [x + move(x, across_core) for x in images]
    sets = [jnp.where(core == 0, sums[2 * s], sums[2 * s + 1]) for s in range(2)]
    here = jnp.where(hi == 0, sets[0], sets[1])
    there = jnp.where(hi == 0, sets[1], sets[0])

    def strip_of(x, s):
        return lax.dynamic_slice_in_dim(x, s * strip, strip, 1)

    mine = strip_of(here, side)
    got_hi = move(strip_of(there, side), across_hi)
    got_side = move(strip_of(here, 1 - side), across_side)
    got_both = move(strip_of(there, 1 - side), across_both)
    pieces = []
    for k in range(4):
        piece = jnp.where(
            block == k,
            mine,
            jnp.where(
                place(1 - hi, side) == k,
                got_hi,
                jnp.where(place(hi, 1 - side) == k, got_side, got_both),
            ),
        )
        pieces.append(piece)
    return jnp.concatenate(pieces, axis=2) * (1.0 / freq_count)


def solution(mesh):
    in_specs = (
        P(None, None, "lat", None),
        P(None, None, "lat", None),
        P("depth", "lat", None),
        P("depth", "lat", None),
        P(),
        P(),
    )
    out_specs = P("depth", "lat", None)
    return jax.shard_map(local, mesh=mesh, in_specs=in_specs, out_specs=out_specs, check_vma=False)
```

```python
import functools
import math

import jax
import jax.numpy as jnp
from jax import lax
from jax.experimental import pallas as pl
from jax.experimental.pallas import tpu as pltpu
from jax.sharding import PartitionSpec as P

HALF = 7
BLEND = 16
TAPS = 2 * HALF + 1
SPAN = 2 * HALF
LANES = 128
WIN = LANES - SPAN
BLK = 16
AXES = ("depth", "lat")
OFF = 8

cell_width = 5.0
depth_step = 10.0
taper_width = 16.0

f32 = jnp.float32
bf16 = jnp.bfloat16


def cdiv(a, b):
    return -(-a // b)


def kernels(frequencies, ref_velocity):
    offsets = jnp.arange(-HALF, HALF + 1, dtype=jnp.int32).astype(jnp.float32)
    wavenumber = 2.0 * math.pi * frequencies.astype(jnp.float32)[:, None] / ref_velocity[None, :]
    curvature = wavenumber * (cell_width * cell_width / (2.0 * depth_step))
    phase_turn = wavenumber * depth_step
    chirp_angle = curvature[:, :, None] * (offsets * offsets)[None, None, :]
    envelope = jnp.exp(-offsets * offsets / taper_width)
    raw_re = envelope * jnp.cos(chirp_angle)
    raw_im = envelope * jnp.sin(chirp_angle)
    magnitude = jnp.sqrt(jnp.sum(raw_re, axis=-1) ** 2 + jnp.sum(raw_im, axis=-1) ** 2)[:, :, None]
    return (raw_re / magnitude, raw_im / magnitude, jnp.cos(phase_turn), jnp.sin(phase_turn))


def operators(tap_re, tap_im, turn_cos, turn_sin):
    ph_re = tap_re * turn_cos[..., None] - tap_im * turn_sin[..., None]
    ph_im = tap_re * turn_sin[..., None] + tap_im * turn_cos[..., None]
    lines = jnp.stack([tap_re, tap_im, ph_re, ph_im], axis=2)
    return jnp.pad(lines, ((0, 0),) * 3 + ((0, LANES - TAPS),))


def split(v):
    high = v.astype(bf16)
    return high, (v - high.astype(f32)).astype(bf16)


def window(x, start, b):
    low = start + WIN * b
    high = min(low + LANES, x.shape[1])
    part = x[:, low:high]
    if high - low < LANES:
        part = jnp.concatenate(
            [part, jnp.zeros((x.shape[0], LANES - (high - low)), x.dtype)], axis=1
        )
    return part


def dense(get, start, count):
    pieces = []
    n = start
    while n < start + count:
        b = n // WIN
        end = min(WIN * (b + 1), start + count)
        pieces.append(get(b)[:, n - WIN * b : end - WIN * b])
        n = end
    return jnp.concatenate(pieces, axis=1)


CORE, HI, SIDE, EVEN_PAIR, FIRST_PAIR, LAST_PAIR, BLOCK, REL = range(8)


def edge_lanes(x, k, cols, n):
    none = jnp.zeros((x.shape[0], n), x.dtype)
    left = x[:, cols * k - n : cols * k] if k > 0 else none
    right = x[:, cols * (k + 1) : cols * (k + 1) + n] if k < 3 else none
    return left, right


def pack_tables_kernel(edge, info, zone, blend, keep, give):
    strip, width = zone.shape[1:]
    cols = width // 4
    half = zone.shape[0] // 2
    core = info[CORE]
    rest = jnp.zeros((strip, LANES - 4 * edge), jnp.int32)
    for k in range(4):
        slot = info[REL + k]
        for v in range(half):
            for ref, h in ((keep, core), (give, 1 - core)):
                z = zone[h * half + v] + OFF
                w = blend[h * half + v]
                zl, zr = edge_lanes(z, k, cols, edge)
                wl, wr = edge_lanes(w, k, cols, edge)
                ref[slot, v, :, 0:cols] = z[:, cols * k : cols * (k + 1)]
                ref[slot, v, :, cols : 2 * cols] = w[:, cols * k : cols * (k + 1)]
                ref[slot, v, :, 2 * cols : 2 * cols + LANES] = jnp.concatenate(
                    [zl, zr, wl, wr, rest], axis=1
                )


def pack_fields_kernel(halo, info, src, rcv, mine, send):
    per_core = mine.shape[0]
    strip, width = src.shape[2:]
    cols = width // 4
    rest = jnp.zeros((strip, LANES - 4 * halo), f32)
    for k in range(4):
        slot = info[REL + k]
        for place, ref in ((0, mine), (2, send)):

            @pl.when(slot == place)
            def _():
                for q in range(per_core):
                    at = info[CORE] * per_core + q
                    lefts, rights = [], []
                    for p in range(4):
                        x = (src if p < 2 else rcv)[p % 2, at]
                        if p == 3:
                            x = -x
                        ref[q, :, p * cols : (p + 1) * cols] = x[:, cols * k : cols * (k + 1)]
                        left, right = edge_lanes(x, k, cols, halo)
                        lefts.append(left)
                        rights.append(right)
                    ref[q, :, 4 * cols : 4 * cols + LANES] = jnp.concatenate(
                        lefts + [rest], axis=1
                    )
                    ref[q, :, 4 * cols + LANES : 4 * cols + 2 * LANES] = jnp.concatenate(
                        rights + [rest], axis=1
                    )


def operators_kernel(info, lines, rows_out, cols_out):
    count, refs = lines.shape[:2]
    lane = lax.broadcasted_iota(jnp.int32, (LANES, LANES), 1)
    for q in range(count):
        by_rows, by_cols = rows_out.at[q], cols_out.at[q]
        for j in range(refs):
            re, im, ph_re, ph_im = (lines[q, j, n : n + 1, :] for n in range(4))
            for p, line in enumerate(
                (re - pltpu.roll(im, 2 * BLK, 1), im + pltpu.roll(re, 2 * BLK, 1))
            ):
                x = pltpu.roll(
                    jnp.broadcast_to(line, (BLK, LANES)), 0, 1, stride=1, stride_axis=0
                )
                high, low = split(x)
                high, low = high[:, : 4 * BLK], low[:, : 4 * BLK]
                at = (2 * j + p) * BLK
                by_rows[at : at + BLK, :] = jnp.concatenate([high, high, low], axis=1)
            bands = []
            for line in (ph_re, ph_im):
                x = pltpu.roll(
                    jnp.broadcast_to(pltpu.roll(line, WIN, 1), (LANES, LANES)),
                    0,
                    1,
                    stride=1,
                    stride_axis=0,
                )
                bands.append(split(jnp.where(lane < WIN, x, 0.0)))
            for n, kind in enumerate((0, 0, 1)):
                x, y = bands[0][kind], bands[1][kind]
                at = 2 * LANES * n
                by_cols[j, at : at + LANES, 0:LANES] = x
                by_cols[j, at : at + LANES, LANES : 2 * LANES] = y
                by_cols[j, at + LANES : at + 2 * LANES, 0:LANES] = -y
                by_cols[j, at + LANES : at + 2 * LANES, LANES : 2 * LANES] = x


def edges_out(info, ref, send_a, send_b, count):
    size = ref.shape[-2]
    lead = (slice(None),) * (len(ref.shape) - 2)

    def put(top_to, bottom_to):
        top_to[lead + (slice(0, count),)] = ref[lead + (slice(0, count),)]
        bottom_to[lead + (slice(0, count),)] = ref[lead + (slice(size - count, size),)]

    pl.when(info[EVEN_PAIR] == 1)(lambda: put(send_b, send_a))
    pl.when(info[EVEN_PAIR] == 0)(lambda: put(send_a, send_b))


def join_tables_kernel(edge, sets, info, *refs):
    count = len(sets)
    whole, send_a, send_b, token = refs[4 * count :]
    token[...] = jnp.zeros_like(token)
    first = info[SIDE] == 0
    for n, s in enumerate(sets):
        mine, got_hi, got_side, got_both = refs[4 * n : 4 * n + 4]
        strip = mine.shape[1]
        near = jnp.where(info[HI] == s, mine[...], got_hi[...])
        far = jnp.where(info[HI] == s, got_side[...], got_both[...])
        whole[n, :, 0:strip, :] = jnp.where(first, near, far)
        whole[n, :, strip : 2 * strip, :] = jnp.where(first, far, near)
        edges_out(info, whole.at[n], send_a.at[n], send_b.at[n], edge)


def join_fields_kernel(halo, info, mine, got, whole, send_a, send_b, token):
    token[...] = jnp.zeros_like(token)
    strip = mine.shape[1]
    first = info[SIDE] == 0
    whole[:, 0:strip, :] = jnp.where(first, mine[...], got[...])
    whole[:, strip : 2 * strip, :] = jnp.where(first, got[...], mine[...])
    edges_out(info, whole, send_a, send_b, halo)


def mark_kernel(info, token):
    token[...] = jnp.zeros_like(token)


def columns_kernel(halo, info, mid, got_a, got_b, *refs):
    send_a, send_b, token = refs
    token[...] = jnp.zeros_like(token)
    even = info[EVEN_PAIR] == 1
    inner = info[BLOCK] % 2 == 0
    cols = mid.shape[2] // 4
    for q in range(mid.shape[0]):
        lefts, rights = [], []
        for p in range(4):
            for start, out in ((p * cols, lefts), ((p + 1) * cols - LANES, rights)):
                lanes = slice(start, start + LANES)
                a, b, m = got_a[q, :, lanes], got_b[q, :, lanes], mid[q, :, lanes]
                top = jnp.where(info[FIRST_PAIR] == 1, 0.0, jnp.where(even, b, a))
                bottom = jnp.where(info[LAST_PAIR] == 1, 0.0, jnp.where(even, a, b))
                rows = jnp.concatenate([top, m, bottom], axis=0)
                out.append(rows[:, :halo] if out is lefts else rows[:, LANES - halo :])
        rest = jnp.zeros((lefts[0].shape[0], LANES - 4 * halo), f32)
        left = jnp.concatenate(lefts + [rest], axis=1)
        right = jnp.concatenate(rights + [rest], axis=1)
        send_a[q] = jnp.where(inner, right, left)
        send_b[q] = jnp.where(inner, left, right)


def tables_kernel(
    cols, edge, windows, n, info, whole_m, whole_o, a_m, a_o, b_m, b_o, out
):
    whole_m, whole_o, a_m, a_o, b_m, b_o = (
        x.at[n] for x in (whole_m, whole_o, a_m, a_o, b_m, b_o)
    )
    half = whole_m.shape[0]
    levels, held = out.shape[:2]
    even = info[EVEN_PAIR] == 1
    for v in range(levels):
        own = info[CORE] == v // half
        i = v % half
        a = jnp.where(own, a_m[i], a_o[i])[:edge]
        b = jnp.where(own, b_m[i], b_o[i])[:edge]
        w = jnp.where(own, whole_m[i], whole_o[i])
        top = jnp.where(info[FIRST_PAIR] == 1, 0, jnp.where(even, b, a))
        bottom = jnp.where(info[LAST_PAIR] == 1, 0, jnp.where(even, a, b))
        x = jnp.concatenate([top, w, bottom], axis=0)
        s = 2 * cols
        z = jnp.concatenate([x[:, s : s + edge], x[:, :cols], x[:, s + edge : s + 2 * edge]], 1)
        s += 2 * edge
        w = jnp.concatenate(
            [x[:, s : s + edge], x[:, cols : 2 * cols], x[:, s + edge : s + 2 * edge]], 1
        )
        t = (z - OFF).astype(f32) + w.astype(f32) * (1.0 / BLEND)
        h = x.shape[0] - SPAN * v
        t = t[HALF * v : HALF * v + h]
        for b in range(windows):
            out[v, 0:h, b * LANES : (b + 1) * LANES] = window(t, HALF * v, b)
        out[v, h:held, :] = jnp.full((held - h, windows * LANES), -8.0, f32)


def stage_kernel(levels, halo, windows, blocks, refs, first, last, *args):
    args = list(args)
    info, token = args[:2]
    count = 3 if first else 5
    fields = args[2 : 2 + count]
    tw_ref, a_ref, c_ref = args[2 + count : 5 + count]
    img_ref = args[5 + count]
    outs = args[6 + count : 6 + count + (0 if last else 3)]
    scratch = args[6 + count + len(outs) :]

    def one(q, carry):
        stage_one(
            levels, halo, windows, blocks, refs, first, last, q,
            info, *(x.at[q] for x in fields), tw_ref, a_ref.at[q], c_ref.at[q], img_ref,
            *(x.at[q] for x in outs), *scratch,
        )
        return carry

    lax.fori_loop(0, fields[0].shape[0], one, 0)


def stage_one(levels, halo, windows, blocks, refs, first, last, freq, *args):
    args = list(args)
    info = args.pop(0)
    mid, got_a, got_b = args[:3]
    del args[:3]
    if not first:
        got_y, got_m = args[:2]
        del args[:2]
    tw_ref, a_ref, c_ref = args[:3]
    del args[:3]
    img_ref = args.pop(0)
    if not last:
        out_ref, send_a, send_b = args[:3]
        del args[:3]
    cur_ref, y_ref, im_ref = args
    rows = mid.shape[0]
    cols = img_ref.shape[2]
    height = rows + 2 * halo
    held = cur_ref.shape[2]
    each = 2 * windows
    lanes = windows * LANES

    even = info[EVEN_PAIR] == 1
    inner = info[BLOCK] % 2 == 0

    def rows_of(lane):
        a, b = got_a[:, lane], got_b[:, lane]
        top = jnp.where(info[FIRST_PAIR] == 1, 0.0, jnp.where(even, b, a))
        bottom = jnp.where(info[LAST_PAIR] == 1, 0.0, jnp.where(even, a, b))
        return jnp.concatenate([top, mid[:, lane], bottom], axis=0)

    if first:
        left = rows_of(slice(4 * cols, 4 * cols + LANES))
        right = rows_of(slice(4 * cols + LANES, 4 * cols + 2 * LANES))
    else:
        left = jnp.where(info[BLOCK] == 0, 0.0, jnp.where(inner, got_m[...], got_y[...]))
        right = jnp.where(info[BLOCK] == 3, 0.0, jnp.where(inner, got_y[...], got_m[...]))
    for f in range(2):
        for p in range(2):
            n = 2 * f + p
            x = jnp.concatenate(
                [
                    left[:, n * halo : (n + 1) * halo],
                    rows_of(slice(n * cols, (n + 1) * cols)),
                    right[:, n * halo : (n + 1) * halo],
                ],
                axis=1,
            )
            for b in range(windows):
                high, low = split(window(x, 0, b))
                at = (f * windows + b) * LANES
                cur_ref[p, 0, 0:height, at : at + LANES] = high
                cur_ref[p, 1, 0:height, at : at + LANES] = low
    if held > height:
        cur_ref[:, :, height:held, :] = jnp.zeros((2, 2, held - height, 2 * lanes), bf16)
    lane = lax.broadcasted_iota(jnp.int32, (BLK, LANES), 1)

    def chunk(l, base, blocks):
        for k in range(blocks):
            r = pl.ds(base + BLK * k, 2 * BLK)
            rhi, rlo = cur_ref[0, 0, r, :], cur_ref[0, 1, r, :]
            ihi, ilo = cur_ref[1, 0, r, :], cur_ref[1, 1, r, :]
            rhs = jnp.concatenate([rhi, ihi, rlo, ilo, rhi, ihi], axis=0)
            g = jnp.dot(a_ref[...], rhs, preferred_element_type=f32)
            high, low = split(g)
            for j in range(refs):
                for p in range(2):
                    s = (2 * j + p) * BLK
                    for q in range(each):
                        rr = (k * each + q) * BLK
                        at = q * LANES
                        y_ref[j, rr : rr + BLK, p * LANES : (p + 1) * LANES] = high[
                            s : s + BLK, at : at + LANES
                        ]
                        y_ref[j, rr : rr + BLK, (2 + p) * LANES : (3 + p) * LANES] = low[
                            s : s + BLK, at : at + LANES
                        ]
        t = tw_ref[l, pl.ds(base, BLK * blocks), :]
        acc = None
        for j in range(refs):
            y = y_ref[j, : blocks * each * BLK]
            full = jnp.dot(
                jnp.concatenate([y, y[:, : 2 * LANES]], axis=1),
                c_ref[j],
                preferred_element_type=f32,
            )
            w = jnp.maximum(1.0 - jnp.abs(t - float(j)), 0.0)
            new = []
            for k in range(blocks):
                for f in range(2):
                    for b in range(windows):
                        rr = (k * each + f * windows + b) * BLK
                        wk = w[BLK * k : BLK * (k + 1), b * LANES : (b + 1) * LANES]
                        new.append(
                            (wk * full[rr : rr + BLK, :LANES], wk * full[rr : rr + BLK, LANES:])
                        )
            if acc is None:
                acc = new
            else:
                acc = [(a0 + b0, a1 + b1) for (a0, a1), (b0, b1) in zip(acc, new)]
        for k in range(blocks):
            r = pl.ds(base + BLK * k, BLK)
            for b in range(windows):
                s = acc[k * each + b]
                q = acc[k * each + windows + b]
                im_ref[l, r, b * LANES : (b + 1) * LANES] = s[0] * q[0] - s[1] * q[1]
            for f in range(2):
                for b in range(windows):
                    at = (f * windows + b) * LANES
                    for p in range(2):
                        v = acc[k * each + f * windows + b][p]
                        if b + 1 < windows:
                            after = pltpu.roll(acc[k * each + f * windows + b + 1][p], WIN, 1)
                            v = jnp.where(lane < WIN, v, after)
                        high, low = split(v)
                        cur_ref[p, 0, r, at : at + LANES] = high
                        cur_ref[p, 1, r, at : at + LANES] = low

    for l in range(levels):
        need = cdiv(height - SPAN * (l + 1), BLK)
        parts = cdiv(need, blocks)
        at = 0
        for i in range(parts):
            n = cdiv(need - at, parts - i)
            chunk(l, at * BLK, n)
            at += n
    if not last:
        for f in range(2):
            for p in range(2):

                def get(b):
                    at = (f * windows + b) * LANES
                    return cur_ref[p, 0, 0:rows, at : at + LANES].astype(f32) + cur_ref[
                        p, 1, 0:rows, at : at + LANES
                    ].astype(f32)

                n = 2 * f + p
                out_ref[:, n * cols : (n + 1) * cols] = dense(get, 0, cols)
        edges_out(info, out_ref, send_a, send_b, halo)
    for l in range(levels):
        o = HALF * (levels - 1 - l)
        part = dense(
            lambda b: im_ref[l, o : o + rows, b * LANES : (b + 1) * LANES], o, cols
        )
        img_ref[l] = jnp.where(freq == 0, part, img_ref[l] + part)


def call(body, out_shape, info, *args, after=(), hand=(), **more):
    near = [pl.BlockSpec(memory_space=pltpu.VMEM)] * len(args)
    far = [pl.BlockSpec(memory_space=pl.ANY)]
    count = 1 + len(args)
    skip = count + len(after) + 2 * len(hand)

    def run(*refs):
        body(*refs[:count], *refs[skip:])

    out_specs = jax.tree.map(lambda _: pl.BlockSpec(memory_space=pltpu.VMEM), out_shape)
    if hand:
        out_shape = [shape(*x.shape, dtype=x.dtype) for x in hand] + out_shape
        out_specs = far * len(hand) + out_specs
        first = count + len(after)
        more["input_output_aliases"] = {first + n: n for n in range(len(hand))}
    return pl.pallas_call(
        run,
        in_specs=[pl.BlockSpec(memory_space=pltpu.SMEM)] + near + far * (len(after) + len(hand)),
        out_specs=out_specs,
        out_shape=out_shape,
        compiler_params=pltpu.CompilerParams(vmem_limit_bytes=40 * 2**20),
        **more,
    )(info, *args, *after, *hand)


def shape(*dims, dtype=f32):
    return jax.ShapeDtypeStruct(dims, dtype)


def local(source_field, receiver_field, zone_index, blend_weight, ref_velocity, frequencies):
    depth, lat = lax.axis_size("depth"), lax.axis_size("lat")
    d, l = lax.axis_index("depth"), lax.axis_index("lat")
    hi, core = d // 2, d % 2
    pair, side = l // 2, l % 2
    if depth != 4 or lat % 4:
        raise ValueError("mesh")
    levels, strip, width = zone_index.shape
    freq_count, refs = frequencies.shape[0], ref_velocity.shape[0]
    per_core = freq_count // 2
    rows, cols = 2 * strip, width // 4
    halo = HALF * levels
    edge = halo - HALF
    half = levels // 2
    windows = cdiv(cols + SPAN * (levels - 1), WIN)
    blocks = cdiv(rows + 2 * halo - SPAN, BLK)
    held = cdiv(rows + 2 * halo - SPAN, BLK) * BLK + BLK

    def permutation(move):
        out = []
        for i in range(depth * lat):
            dd, ll = divmod(i, lat)
            h, c, p, s = dd // 2, dd % 2, ll // 2, ll % 2
            target = move(h, c, p, s)
            if target is None or not 0 <= target[2] < lat // 2:
                target = (h, 1 - c, p, s)
            h, c, p, s = target
            out.append((i, (h * 2 + c) * lat + p * 2 + s))
        return out

    across_hi = permutation(lambda h, c, p, s: (1 - h, c, p, s))
    across_side = permutation(lambda h, c, p, s: (h, c, p, 1 - s))
    across_both = permutation(lambda h, c, p, s: (1 - h, c, p, 1 - s))
    across_core = permutation(lambda h, c, p, s: (h, 1 - c, p, s))
    pairs_even = permutation(lambda h, c, p, s: (h, c, p + 1 - 2 * (p % 2), s))
    pairs_odd = permutation(lambda h, c, p, s: (h, c, p - 1 + 2 * (p % 2), s))
    middle = permutation(lambda h, c, p, s: (1 - h, c, p, s) if s == 1 else None)

    def move(x, pairs):
        return lax.ppermute(x, AXES, pairs)

    def place(h, s):
        return 2 * h + jnp.where(h == 0, s, 1 - s)

    block = place(hi, side)
    rel = []
    for k in range(4):
        kh = k // 2
        ks = k % 2 if kh == 0 else 1 - k % 2
        rel.append(jnp.where(hi == kh, 0, 1) + jnp.where(side == ks, 0, 2))
    info = jnp.stack(
        [
            core,
            hi,
            side,
            (pair % 2 == 0).astype(jnp.int32),
            (pair == 0).astype(jnp.int32),
            (pair == lat // 2 - 1).astype(jnp.int32),
            block,
        ]
        + rel
    ).astype(jnp.int32)

    mark = shape(8, LANES)
    lane_t = 2 * cols + LANES
    lane_f = 4 * cols + 2 * LANES
    packed = shape(4, half, strip, lane_t, dtype=jnp.int32)
    mine, send = call(
        functools.partial(pack_fields_kernel, halo),
        [shape(per_core, strip, lane_f)] * 2,
        info,
        source_field,
        receiver_field,
    )
    got = move(send, across_side)
    keep, give = call(
        functools.partial(pack_tables_kernel, edge),
        [packed, packed],
        info,
        zone_index,
        blend_weight,
        after=[send],
    )
    swapped = move(give, across_core)

    def spread(own):
        return (
            own[0],
            move(own[1], across_hi),
            move(own[2], across_side),
            move(own[3], across_both),
        )

    def join(sets, parts, after):
        edges = shape(len(sets), half, cdiv(edge, 8) * 8, lane_t, dtype=jnp.int32)
        whole, send_a, send_b, token = call(
            functools.partial(join_tables_kernel, edge, sets),
            [shape(len(sets), half, rows, lane_t, dtype=jnp.int32), edges, edges, mark],
            info,
            *parts,
            after=after,
        )
        return (
            whole,
            move(whole, across_core),
            move(send_a, pairs_even),
            move(send_b, pairs_odd),
            token,
        )

    def finish(whole, other, got_a, got_b):
        swap_a, swap_b = move(got_a, across_core), move(got_b, across_core)
        return [
            call(
                functools.partial(tables_kernel, cols, edge, windows, n),
                shape(levels, held, windows * LANES),
                info,
                whole,
                other,
                got_a,
                swap_a,
                got_b,
                swap_b,
            )
            for n in range(whole.shape[0])
        ]

    parts = [spread(jnp.where(core == 0, keep, swapped)), None]

    taps = kernels(frequencies, ref_velocity)
    taps = [lax.dynamic_slice_in_dim(x, core * per_core, per_core, 0) for x in taps]
    matrices = call(
        operators_kernel,
        [
            shape(per_core, refs * 2 * BLK, 12 * BLK, dtype=bf16),
            shape(per_core, refs, 6 * LANES, 2 * LANES, dtype=bf16),
        ],
        info,
        operators(*taps),
        after=[give],
    )

    whole, send_a, send_b, _ = call(
        functools.partial(join_fields_kernel, halo),
        [shape(per_core, rows, lane_f)] + [shape(per_core, halo, lane_f)] * 2 + [mark],
        info,
        mine,
        got,
        after=[matrices[0]],
    )
    state = (whole, move(send_a, pairs_even), move(send_b, pairs_odd))
    *joined, token = join((0,), parts[0], [whole])
    tables = finish(*joined)
    parts[1] = spread(jnp.where(core == 1, keep, swapped))

    area = levels * (rows + halo) * windows * LANES
    images = []
    for s in range(4):
        out_shape = [shape(levels, rows, cols)]
        if s < 3:
            out_shape += [shape(per_core, rows, 4 * cols)] + [shape(per_core, halo, 4 * cols)] * 2
        image, *fields = call(
            functools.partial(
                stage_kernel, levels, halo, windows, blocks, refs, s == 0, s == 3
            ),
            out_shape,
            info,
            token,
            *state,
            tables[s],
            *matrices,
            scratch_shapes=[
                pltpu.VMEM((2, 2, held, 2 * windows * LANES), bf16),
                pltpu.VMEM((refs, blocks * 2 * windows * BLK, 4 * LANES), bf16),
                pltpu.VMEM((levels, held, windows * LANES), f32),
            ],
            cost_estimate=pl.CostEstimate(
                flops=area * 8 * refs * 2 * 3 * 512, bytes_accessed=2**21, transcendentals=0
            ),
        )
        images.append(image)
        if s == 3:
            break
        if s == 0:
            *joined, _ = join((0,), parts[1], [image])
        field, send_a, send_b = fields
        got = [move(send_a, pairs_even), move(send_b, pairs_odd)]
        if s == 1:
            *handed, _ = call(mark_kernel, [mark], info, after=[image], hand=list(joined[2:]))
            tables += finish(*joined[:2], *handed)
        *handed, side_a, side_b, token = call(
            functools.partial(columns_kernel, halo),
            [shape(per_core, rows + 2 * halo, LANES)] * 2 + [mark],
            info,
            field,
            *got,
            after=tables[2:] if s == 1 else [],
            hand=list(joined[2:]) if s == 0 else [],
        )
        state = (field, *got, move(side_a, across_side), move(side_b, middle))
        if s == 0:
            tables += finish(*joined[:2], *handed)
            *joined, token = join((1, 1), parts[0] + parts[1], [token])

    sums = [x + move(x, across_core) for x in images]
    sets = [jnp.where(core == 0, sums[2 * s], sums[2 * s + 1]) for s in range(2)]
    here = jnp.where(hi == 0, sets[0], sets[1])
    there = jnp.where(hi == 0, sets[1], sets[0])

    def strip_of(x, s):
        return lax.dynamic_slice_in_dim(x, s * strip, strip, 1)

    mine = strip_of(here, side)
    got_hi = move(strip_of(there, side), across_hi)
    got_side = move(strip_of(here, 1 - side), across_side)
    got_both = move(strip_of(there, 1 - side), across_both)
    pieces = []
    for k in range(4):
        piece = jnp.where(
            block == k,
            mine,
            jnp.where(
                place(1 - hi, side) == k,
                got_hi,
                jnp.where(place(hi, 1 - side) == k, got_side, got_both),
            ),
        )
        pieces.append(piece)
    return jnp.concatenate(pieces, axis=2) * (1.0 / freq_count)


def solution(mesh):
    in_specs = (
        P(None, None, "lat", None),
        P(None, None, "lat", None),
        P("depth", "lat", None),
        P("depth", "lat", None),
        P(),
        P(),
    )
    out_specs = P("depth", "lat", None)
    return jax.shard_map(local, mesh=mesh, in_specs=in_specs, out_specs=out_specs, check_vma=False)
```

```python
import functools
import math

import jax
import jax.numpy as jnp
from jax import lax
from jax.experimental import pallas as pl
from jax.experimental.pallas import tpu as pltpu
from jax.sharding import PartitionSpec as P

HALF = 7
BLEND = 16
TAPS = 2 * HALF + 1
SPAN = 2 * HALF
LANES = 128
WIN = LANES - SPAN
BLK = 16
AXES = ("depth", "lat")
OFF = 8

cell_width = 5.0
depth_step = 10.0
taper_width = 16.0

f32 = jnp.float32
bf16 = jnp.bfloat16


def cdiv(a, b):
    return -(-a // b)


def kernels(frequencies, ref_velocity):
    offsets = jnp.arange(-HALF, HALF + 1, dtype=jnp.int32).astype(jnp.float32)
    wavenumber = 2.0 * math.pi * frequencies.astype(jnp.float32)[:, None] / ref_velocity[None, :]
    curvature = wavenumber * (cell_width * cell_width / (2.0 * depth_step))
    phase_turn = wavenumber * depth_step
    chirp_angle = curvature[:, :, None] * (offsets * offsets)[None, None, :]
    envelope = jnp.exp(-offsets * offsets / taper_width)
    raw_re = envelope * jnp.cos(chirp_angle)
    raw_im = envelope * jnp.sin(chirp_angle)
    magnitude = jnp.sqrt(jnp.sum(raw_re, axis=-1) ** 2 + jnp.sum(raw_im, axis=-1) ** 2)[:, :, None]
    return (raw_re / magnitude, raw_im / magnitude, jnp.cos(phase_turn), jnp.sin(phase_turn))


def operators(tap_re, tap_im, turn_cos, turn_sin):
    ph_re = tap_re * turn_cos[..., None] - tap_im * turn_sin[..., None]
    ph_im = tap_re * turn_sin[..., None] + tap_im * turn_cos[..., None]
    lines = jnp.stack([tap_re, tap_im, ph_re, ph_im], axis=2)
    return jnp.pad(lines, ((0, 0),) * 3 + ((0, LANES - TAPS),))


def split(v):
    high = v.astype(bf16)
    return high, (v - high.astype(f32)).astype(bf16)


def window(x, start, b):
    low = start + WIN * b
    high = min(low + LANES, x.shape[1])
    part = x[:, low:high]
    if high - low < LANES:
        part = jnp.concatenate(
            [part, jnp.zeros((x.shape[0], LANES - (high - low)), x.dtype)], axis=1
        )
    return part


def dense(get, start, count):
    pieces = []
    n = start
    while n < start + count:
        b = n // WIN
        end = min(WIN * (b + 1), start + count)
        pieces.append(get(b)[:, n - WIN * b : end - WIN * b])
        n = end
    return jnp.concatenate(pieces, axis=1)


CORE, HI, SIDE, EVEN_PAIR, FIRST_PAIR, LAST_PAIR, BLOCK, REL = range(8)


def edge_lanes(x, k, cols, n):
    none = jnp.zeros((x.shape[0], n), x.dtype)
    left = x[:, cols * k - n : cols * k] if k > 0 else none
    right = x[:, cols * (k + 1) : cols * (k + 1) + n] if k < 3 else none
    return left, right


def pack_tables_kernel(edge, info, zone, blend, keep, give):
    strip, width = zone.shape[1:]
    cols = width // 4
    half = zone.shape[0] // 2
    core = info[CORE]
    rest = jnp.zeros((strip, LANES - 4 * edge), jnp.int32)
    for k in range(4):
        slot = info[REL + k]
        for v in range(half):
            for ref, h in ((keep, core), (give, 1 - core)):
                z = zone[h * half + v] + OFF
                w = blend[h * half + v]
                zl, zr = edge_lanes(z, k, cols, edge)
                wl, wr = edge_lanes(w, k, cols, edge)
                ref[slot, v, :, 0:cols] = z[:, cols * k : cols * (k + 1)]
                ref[slot, v, :, cols : 2 * cols] = w[:, cols * k : cols * (k + 1)]
                ref[slot, v, :, 2 * cols : 2 * cols + LANES] = jnp.concatenate(
                    [zl, zr, wl, wr, rest], axis=1
                )


def pack_fields_kernel(halo, info, src, rcv, mine, send):
    per_core = mine.shape[0]
    strip, width = src.shape[2:]
    cols = width // 4
    rest = jnp.zeros((strip, LANES - 4 * halo), f32)
    for k in range(4):
        slot = info[REL + k]
        for place, ref in ((0, mine), (2, send)):

            @pl.when(slot == place)
            def _():
                for q in range(per_core):
                    at = info[CORE] * per_core + q
                    lefts, rights = [], []
                    for p in range(4):
                        x = (src if p < 2 else rcv)[p % 2, at]
                        if p == 3:
                            x = -x
                        ref[q, :, p * cols : (p + 1) * cols] = x[:, cols * k : cols * (k + 1)]
                        left, right = edge_lanes(x, k, cols, halo)
                        lefts.append(left)
                        rights.append(right)
                    ref[q, :, 4 * cols : 4 * cols + LANES] = jnp.concatenate(
                        lefts + [rest], axis=1
                    )
                    ref[q, :, 4 * cols + LANES : 4 * cols + 2 * LANES] = jnp.concatenate(
                        rights + [rest], axis=1
                    )


def operators_kernel(info, lines, rows_out, cols_out):
    count, refs = lines.shape[:2]
    lane = lax.broadcasted_iota(jnp.int32, (LANES, LANES), 1)
    for q in range(count):
        by_rows, by_cols = rows_out.at[q], cols_out.at[q]
        for j in range(refs):
            re, im, ph_re, ph_im = (lines[q, j, n : n + 1, :] for n in range(4))
            for p, line in enumerate(
                (re - pltpu.roll(im, 2 * BLK, 1), im + pltpu.roll(re, 2 * BLK, 1))
            ):
                x = pltpu.roll(
                    jnp.broadcast_to(line, (BLK, LANES)), 0, 1, stride=1, stride_axis=0
                )
                high, low = split(x)
                high, low = high[:, : 4 * BLK], low[:, : 4 * BLK]
                at = (2 * j + p) * BLK
                by_rows[at : at + BLK, :] = jnp.concatenate([high, high, low], axis=1)
            bands = []
            for line in (ph_re, ph_im):
                x = pltpu.roll(
                    jnp.broadcast_to(pltpu.roll(line, WIN, 1), (LANES, LANES)),
                    0,
                    1,
                    stride=1,
                    stride_axis=0,
                )
                bands.append(split(jnp.where(lane < WIN, x, 0.0)))
            for n, kind in enumerate((0, 0, 1)):
                x, y = bands[0][kind], bands[1][kind]
                at = 2 * LANES * n
                by_cols[j, at : at + LANES, 0:LANES] = x
                by_cols[j, at : at + LANES, LANES : 2 * LANES] = y
                by_cols[j, at + LANES : at + 2 * LANES, 0:LANES] = -y
                by_cols[j, at + LANES : at + 2 * LANES, LANES : 2 * LANES] = x


def edges_out(info, ref, send_a, send_b, count):
    size = ref.shape[-2]
    lead = (slice(None),) * (len(ref.shape) - 2)

    def put(top_to, bottom_to):
        top_to[lead + (slice(0, count),)] = ref[lead + (slice(0, count),)]
        bottom_to[lead + (slice(0, count),)] = ref[lead + (slice(size - count, size),)]

    pl.when(info[EVEN_PAIR] == 1)(lambda: put(send_b, send_a))
    pl.when(info[EVEN_PAIR] == 0)(lambda: put(send_a, send_b))


def join_tables_kernel(edge, sets, info, *refs):
    count = len(sets)
    whole, send_a, send_b, token = refs[4 * count :]
    token[...] = jnp.zeros_like(token)
    first = info[SIDE] == 0
    for n, s in enumerate(sets):
        mine, got_hi, got_side, got_both = refs[4 * n : 4 * n + 4]
        strip = mine.shape[1]
        near = jnp.where(info[HI] == s, mine[...], got_hi[...])
        far = jnp.where(info[HI] == s, got_side[...], got_both[...])
        whole[n, :, 0:strip, :] = jnp.where(first, near, far)
        whole[n, :, strip : 2 * strip, :] = jnp.where(first, far, near)
        edges_out(info, whole.at[n], send_a.at[n], send_b.at[n], edge)


def join_fields_kernel(halo, info, mine, got, whole, send_a, send_b, token):
    token[...] = jnp.zeros_like(token)
    strip = mine.shape[1]
    first = info[SIDE] == 0
    whole[:, 0:strip, :] = jnp.where(first, mine[...], got[...])
    whole[:, strip : 2 * strip, :] = jnp.where(first, got[...], mine[...])
    edges_out(info, whole, send_a, send_b, halo)


def mark_kernel(info, token):
    token[...] = jnp.zeros_like(token)


def columns_kernel(halo, info, mid, got_a, got_b, *refs):
    send_a, send_b, token = refs
    token[...] = jnp.zeros_like(token)
    even = info[EVEN_PAIR] == 1
    inner = info[BLOCK] % 2 == 0
    cols = mid.shape[2] // 4
    for q in range(mid.shape[0]):
        lefts, rights = [], []
        for p in range(4):
            for start, out in ((p * cols, lefts), ((p + 1) * cols - LANES, rights)):
                lanes = slice(start, start + LANES)
                a, b, m = got_a[q, :, lanes], got_b[q, :, lanes], mid[q, :, lanes]
                top = jnp.where(info[FIRST_PAIR] == 1, 0.0, jnp.where(even, b, a))
                bottom = jnp.where(info[LAST_PAIR] == 1, 0.0, jnp.where(even, a, b))
                rows = jnp.concatenate([top, m, bottom], axis=0)
                out.append(rows[:, :halo] if out is lefts else rows[:, LANES - halo :])
        rest = jnp.zeros((lefts[0].shape[0], LANES - 4 * halo), f32)
        left = jnp.concatenate(lefts + [rest], axis=1)
        right = jnp.concatenate(rights + [rest], axis=1)
        send_a[q] = jnp.where(inner, right, left)
        send_b[q] = jnp.where(inner, left, right)


def tables_kernel(
    cols, edge, windows, n, info, whole_m, whole_o, a_m, a_o, b_m, b_o, out
):
    whole_m, whole_o, a_m, a_o, b_m, b_o = (
        x.at[n] for x in (whole_m, whole_o, a_m, a_o, b_m, b_o)
    )
    half = whole_m.shape[0]
    levels, held = out.shape[:2]
    even = info[EVEN_PAIR] == 1
    for v in range(levels):
        own = info[CORE] == v // half
        i = v % half
        a = jnp.where(own, a_m[i], a_o[i])[:edge]
        b = jnp.where(own, b_m[i], b_o[i])[:edge]
        w = jnp.where(own, whole_m[i], whole_o[i])
        top = jnp.where(info[FIRST_PAIR] == 1, 0, jnp.where(even, b, a))
        bottom = jnp.where(info[LAST_PAIR] == 1, 0, jnp.where(even, a, b))
        x = jnp.concatenate([top, w, bottom], axis=0)
        s = 2 * cols
        z = jnp.concatenate([x[:, s : s + edge], x[:, :cols], x[:, s + edge : s + 2 * edge]], 1)
        s += 2 * edge
        w = jnp.concatenate(
            [x[:, s : s + edge], x[:, cols : 2 * cols], x[:, s + edge : s + 2 * edge]], 1
        )
        t = (z - OFF).astype(f32) + w.astype(f32) * (1.0 / BLEND)
        h = x.shape[0] - SPAN * v
        t = t[HALF * v : HALF * v + h]
        for b in range(windows):
            out[v, 0:h, b * LANES : (b + 1) * LANES] = window(t, HALF * v, b)
        out[v, h:held, :] = jnp.full((held - h, windows * LANES), -8.0, f32)


def stage_kernel(levels, halo, windows, blocks, refs, first, last, *args):
    args = list(args)
    info, token = args[:2]
    count = 3 if first else 5
    fields = args[2 : 2 + count]
    tw_ref, a_ref, c_ref = args[2 + count : 5 + count]
    img_ref = args[5 + count]
    outs = args[6 + count : 6 + count + (0 if last else 3)]
    scratch = args[6 + count + len(outs) :]

    def one(q, carry):
        stage_one(
            levels, halo, windows, blocks, refs, first, last, q,
            info, *(x.at[q] for x in fields), tw_ref, a_ref.at[q], c_ref.at[q], img_ref,
            *(x.at[q] for x in outs), *scratch,
        )
        return carry

    lax.fori_loop(0, fields[0].shape[0], one, 0)


def stage_one(levels, halo, windows, blocks, refs, first, last, freq, *args):
    args = list(args)
    info = args.pop(0)
    mid, got_a, got_b = args[:3]
    del args[:3]
    if not first:
        got_y, got_m = args[:2]
        del args[:2]
    tw_ref, a_ref, c_ref = args[:3]
    del args[:3]
    img_ref = args.pop(0)
    if not last:
        out_ref, send_a, send_b = args[:3]
        del args[:3]
    cur_ref, y_ref, im_ref = args
    rows = mid.shape[0]
    cols = img_ref.shape[2]
    height = rows + 2 * halo
    held = cur_ref.shape[2]
    each = 2 * windows
    lanes = windows * LANES

    even = info[EVEN_PAIR] == 1
    inner = info[BLOCK] % 2 == 0

    def rows_of(lane):
        a, b = got_a[:, lane], got_b[:, lane]
        top = jnp.where(info[FIRST_PAIR] == 1, 0.0, jnp.where(even, b, a))
        bottom = jnp.where(info[LAST_PAIR] == 1, 0.0, jnp.where(even, a, b))
        return jnp.concatenate([top, mid[:, lane], bottom], axis=0)

    if first:
        left = rows_of(slice(4 * cols, 4 * cols + LANES))
        right = rows_of(slice(4 * cols + LANES, 4 * cols + 2 * LANES))
    else:
        left = jnp.where(info[BLOCK] == 0, 0.0, jnp.where(inner, got_m[...], got_y[...]))
        right = jnp.where(info[BLOCK] == 3, 0.0, jnp.where(inner, got_y[...], got_m[...]))
    for f in range(2):
        for p in range(2):
            n = 2 * f + p
            x = jnp.concatenate(
                [
                    left[:, n * halo : (n + 1) * halo],
                    rows_of(slice(n * cols, (n + 1) * cols)),
                    right[:, n * halo : (n + 1) * halo],
                ],
                axis=1,
            )
            if held > height:
                x = jnp.concatenate([x, jnp.zeros((held - height, x.shape[1]), f32)], axis=0)
            for b in range(windows):
                high, low = split(window(x, 0, b))
                at = (f * windows + b) * LANES
                cur_ref[p, 0, :, at : at + LANES] = high
                cur_ref[p, 1, :, at : at + LANES] = low
    lane = lax.broadcasted_iota(jnp.int32, (BLK, LANES), 1)

    def chunk(l, base, blocks):
        for k in range(blocks):
            r = pl.ds(base + BLK * k, 2 * BLK)
            rhi, rlo = cur_ref[0, 0, r, :], cur_ref[0, 1, r, :]
            ihi, ilo = cur_ref[1, 0, r, :], cur_ref[1, 1, r, :]
            rhs = jnp.concatenate([rhi, ihi, rlo, ilo, rhi, ihi], axis=0)
            g = jnp.dot(a_ref[...], rhs, preferred_element_type=f32)
            high, low = split(g)
            for j in range(refs):
                for p in range(2):
                    s = (2 * j + p) * BLK
                    for q in range(each):
                        rr = (k * each + q) * BLK
                        at = q * LANES
                        y_ref[j, rr : rr + BLK, p * LANES : (p + 1) * LANES] = high[
                            s : s + BLK, at : at + LANES
                        ]
                        y_ref[j, rr : rr + BLK, (2 + p) * LANES : (3 + p) * LANES] = low[
                            s : s + BLK, at : at + LANES
                        ]
        t = tw_ref[l, pl.ds(base, BLK * blocks), :]
        acc = None
        for j in range(refs):
            y = y_ref[j, : blocks * each * BLK]
            full = jnp.dot(
                jnp.concatenate([y, y[:, : 2 * LANES]], axis=1),
                c_ref[j],
                preferred_element_type=f32,
            )
            w = jnp.maximum(1.0 - jnp.abs(t - float(j)), 0.0)
            new = []
            for k in range(blocks):
                for f in range(2):
                    for b in range(windows):
                        rr = (k * each + f * windows + b) * BLK
                        wk = w[BLK * k : BLK * (k + 1), b * LANES : (b + 1) * LANES]
                        new.append(
                            (wk * full[rr : rr + BLK, :LANES], wk * full[rr : rr + BLK, LANES:])
                        )
            if acc is None:
                acc = new
            else:
                acc = [(a0 + b0, a1 + b1) for (a0, a1), (b0, b1) in zip(acc, new)]
        for k in range(blocks):
            r = pl.ds(base + BLK * k, BLK)
            for b in range(windows):
                s = acc[k * each + b]
                q = acc[k * each + windows + b]
                im_ref[l, r, b * LANES : (b + 1) * LANES] = s[0] * q[0] - s[1] * q[1]
            for f in range(2):
                for b in range(windows):
                    at = (f * windows + b) * LANES
                    for p in range(2):
                        v = acc[k * each + f * windows + b][p]
                        if b + 1 < windows:
                            after = pltpu.roll(acc[k * each + f * windows + b + 1][p], WIN, 1)
                            v = jnp.where(lane < WIN, v, after)
                        high, low = split(v)
                        cur_ref[p, 0, r, at : at + LANES] = high
                        cur_ref[p, 1, r, at : at + LANES] = low

    for l in range(levels):
        need = cdiv(height - SPAN * (l + 1), BLK)
        parts = cdiv(need, blocks)
        at = 0
        for i in range(parts):
            n = cdiv(need - at, parts - i)
            chunk(l, at * BLK, n)
            at += n
    if not last:
        for f in range(2):
            for p in range(2):

                def get(b):
                    at = (f * windows + b) * LANES
                    return cur_ref[p, 0, 0:rows, at : at + LANES].astype(f32) + cur_ref[
                        p, 1, 0:rows, at : at + LANES
                    ].astype(f32)

                n = 2 * f + p
                out_ref[:, n * cols : (n + 1) * cols] = dense(get, 0, cols)
        edges_out(info, out_ref, send_a, send_b, halo)
    for l in range(levels):
        o = HALF * (levels - 1 - l)
        part = dense(
            lambda b: im_ref[l, o : o + rows, b * LANES : (b + 1) * LANES], o, cols
        )
        img_ref[l] = jnp.where(freq == 0, part, img_ref[l] + part)


def call(body, out_shape, info, *args, after=(), hand=(), **more):
    near = [pl.BlockSpec(memory_space=pltpu.VMEM)] * len(args)
    far = [pl.BlockSpec(memory_space=pl.ANY)]
    count = 1 + len(args)
    skip = count + len(after) + 2 * len(hand)

    def run(*refs):
        body(*refs[:count], *refs[skip:])

    out_specs = jax.tree.map(lambda _: pl.BlockSpec(memory_space=pltpu.VMEM), out_shape)
    if hand:
        out_shape = [shape(*x.shape, dtype=x.dtype) for x in hand] + out_shape
        out_specs = far * len(hand) + out_specs
        first = count + len(after)
        more["input_output_aliases"] = {first + n: n for n in range(len(hand))}
    return pl.pallas_call(
        run,
        in_specs=[pl.BlockSpec(memory_space=pltpu.SMEM)] + near + far * (len(after) + len(hand)),
        out_specs=out_specs,
        out_shape=out_shape,
        compiler_params=pltpu.CompilerParams(vmem_limit_bytes=40 * 2**20),
        **more,
    )(info, *args, *after, *hand)


def shape(*dims, dtype=f32):
    return jax.ShapeDtypeStruct(dims, dtype)


def local(source_field, receiver_field, zone_index, blend_weight, ref_velocity, frequencies):
    depth, lat = lax.axis_size("depth"), lax.axis_size("lat")
    d, l = lax.axis_index("depth"), lax.axis_index("lat")
    hi, core = d // 2, d % 2
    pair, side = l // 2, l % 2
    if depth != 4 or lat % 4:
        raise ValueError("mesh")
    levels, strip, width = zone_index.shape
    freq_count, refs = frequencies.shape[0], ref_velocity.shape[0]
    per_core = freq_count // 2
    rows, cols = 2 * strip, width // 4
    halo = HALF * levels
    edge = halo - HALF
    half = levels // 2
    windows = cdiv(cols + SPAN * (levels - 1), WIN)
    blocks = cdiv(rows + 2 * halo - SPAN, BLK)
    held = cdiv(rows + 2 * halo - SPAN, BLK) * BLK + BLK

    def permutation(move):
        out = []
        for i in range(depth * lat):
            dd, ll = divmod(i, lat)
            h, c, p, s = dd // 2, dd % 2, ll // 2, ll % 2
            target = move(h, c, p, s)
            if target is None or not 0 <= target[2] < lat // 2:
                target = (h, 1 - c, p, s)
            h, c, p, s = target
            out.append((i, (h * 2 + c) * lat + p * 2 + s))
        return out

    across_hi = permutation(lambda h, c, p, s: (1 - h, c, p, s))
    across_side = permutation(lambda h, c, p, s: (h, c, p, 1 - s))
    across_both = permutation(lambda h, c, p, s: (1 - h, c, p, 1 - s))
    across_core = permutation(lambda h, c, p, s: (h, 1 - c, p, s))
    pairs_even = permutation(lambda h, c, p, s: (h, c, p + 1 - 2 * (p % 2), s))
    pairs_odd = permutation(lambda h, c, p, s: (h, c, p - 1 + 2 * (p % 2), s))
    middle = permutation(lambda h, c, p, s: (1 - h, c, p, s) if s == 1 else None)

    def move(x, pairs):
        return lax.ppermute(x, AXES, pairs)

    def place(h, s):
        return 2 * h + jnp.where(h == 0, s, 1 - s)

    block = place(hi, side)
    rel = []
    for k in range(4):
        kh = k // 2
        ks = k % 2 if kh == 0 else 1 - k % 2
        rel.append(jnp.where(hi == kh, 0, 1) + jnp.where(side == ks, 0, 2))
    info = jnp.stack(
        [
            core,
            hi,
            side,
            (pair % 2 == 0).astype(jnp.int32),
            (pair == 0).astype(jnp.int32),
            (pair == lat // 2 - 1).astype(jnp.int32),
            block,
        ]
        + rel
    ).astype(jnp.int32)

    mark = shape(8, LANES)
    lane_t = 2 * cols + LANES
    lane_f = 4 * cols + 2 * LANES
    packed = shape(4, half, strip, lane_t, dtype=jnp.int32)
    mine, send = call(
        functools.partial(pack_fields_kernel, halo),
        [shape(per_core, strip, lane_f)] * 2,
        info,
        source_field,
        receiver_field,
    )
    got = move(send, across_side)
    keep, give = call(
        functools.partial(pack_tables_kernel, edge),
        [packed, packed],
        info,
        zone_index,
        blend_weight,
        after=[send],
    )
    swapped = move(give, across_core)

    def spread(own):
        return (
            own[0],
            move(own[1], across_hi),
            move(own[2], across_side),
            move(own[3], across_both),
        )

    def join(sets, parts, after):
        edges = shape(len(sets), half, cdiv(edge, 8) * 8, lane_t, dtype=jnp.int32)
        whole, send_a, send_b, token = call(
            functools.partial(join_tables_kernel, edge, sets),
            [shape(len(sets), half, rows, lane_t, dtype=jnp.int32), edges, edges, mark],
            info,
            *parts,
            after=after,
        )
        return (
            whole,
            move(whole, across_core),
            move(send_a, pairs_even),
            move(send_b, pairs_odd),
            token,
        )

    def finish(whole, other, got_a, got_b):
        swap_a, swap_b = move(got_a, across_core), move(got_b, across_core)
        return [
            call(
                functools.partial(tables_kernel, cols, edge, windows, n),
                shape(levels, held, windows * LANES),
                info,
                whole,
                other,
                got_a,
                swap_a,
                got_b,
                swap_b,
            )
            for n in range(whole.shape[0])
        ]

    parts = [spread(jnp.where(core == 0, keep, swapped)), None]

    taps = kernels(frequencies, ref_velocity)
    taps = [lax.dynamic_slice_in_dim(x, core * per_core, per_core, 0) for x in taps]
    matrices = call(
        operators_kernel,
        [
            shape(per_core, refs * 2 * BLK, 12 * BLK, dtype=bf16),
            shape(per_core, refs, 6 * LANES, 2 * LANES, dtype=bf16),
        ],
        info,
        operators(*taps),
        after=[give],
    )

    whole, send_a, send_b, _ = call(
        functools.partial(join_fields_kernel, halo),
        [shape(per_core, rows, lane_f)] + [shape(per_core, halo, lane_f)] * 2 + [mark],
        info,
        mine,
        got,
        after=[matrices[0]],
    )
    state = (whole, move(send_a, pairs_even), move(send_b, pairs_odd))
    *joined, token = join((0,), parts[0], [whole])
    tables = finish(*joined)
    parts[1] = spread(jnp.where(core == 1, keep, swapped))

    area = levels * (rows + halo) * windows * LANES
    images = []
    for s in range(4):
        out_shape = [shape(levels, rows, cols)]
        if s < 3:
            out_shape += [shape(per_core, rows, 4 * cols)] + [shape(per_core, halo, 4 * cols)] * 2
        image, *fields = call(
            functools.partial(
                stage_kernel, levels, halo, windows, blocks, refs, s == 0, s == 3
            ),
            out_shape,
            info,
            token,
            *state,
            tables[s],
            *matrices,
            scratch_shapes=[
                pltpu.VMEM((2, 2, held, 2 * windows * LANES), bf16),
                pltpu.VMEM((refs, blocks * 2 * windows * BLK, 4 * LANES), bf16),
                pltpu.VMEM((levels, held, windows * LANES), f32),
            ],
            cost_estimate=pl.CostEstimate(
                flops=area * 8 * refs * 2 * 3 * 512, bytes_accessed=2**21, transcendentals=0
            ),
        )
        images.append(image)
        if s == 3:
            break
        if s == 0:
            *joined, _ = join((0,), parts[1], [image])
        field, send_a, send_b = fields
        got = [move(send_a, pairs_even), move(send_b, pairs_odd)]
        if s == 1:
            *handed, _ = call(mark_kernel, [mark], info, after=[image], hand=list(joined[2:]))
            tables += finish(*joined[:2], *handed)
        *handed, side_a, side_b, token = call(
            functools.partial(columns_kernel, halo),
            [shape(per_core, rows + 2 * halo, LANES)] * 2 + [mark],
            info,
            field,
            *got,
            after=tables[2:] if s == 1 else [],
            hand=list(joined[2:]) if s == 0 else [],
        )
        state = (field, *got, move(side_a, across_side), move(side_b, middle))
        if s == 0:
            tables += finish(*joined[:2], *handed)
            *joined, token = join((1, 1), parts[0] + parts[1], [token])

    sums = [x + move(x, across_core) for x in images]
    sets = [jnp.where(core == 0, sums[2 * s], sums[2 * s + 1]) for s in range(2)]
    here = jnp.where(hi == 0, sets[0], sets[1])
    there = jnp.where(hi == 0, sets[1], sets[0])

    def strip_of(x, s):
        return lax.dynamic_slice_in_dim(x, s * strip, strip, 1)

    mine = strip_of(here, side)
    got_hi = move(strip_of(there, side), across_hi)
    got_side = move(strip_of(here, 1 - side), across_side)
    got_both = move(strip_of(there, 1 - side), across_both)
    pieces = []
    for k in range(4):
        piece = jnp.where(
            block == k,
            mine,
            jnp.where(
                place(1 - hi, side) == k,
                got_hi,
                jnp.where(place(hi, 1 - side) == k, got_side, got_both),
            ),
        )
        pieces.append(piece)
    return jnp.concatenate(pieces, axis=2) * (1.0 / freq_count)


def solution(mesh):
    in_specs = (
        P(None, None, "lat", None),
        P(None, None, "lat", None),
        P("depth", "lat", None),
        P("depth", "lat", None),
        P(),
        P(),
    )
    out_specs = P("depth", "lat", None)
    return jax.shard_map(local, mesh=mesh, in_specs=in_specs, out_specs=out_specs, check_vma=False)
```

```python
import functools
import math

import jax
import jax.numpy as jnp
from jax import lax
from jax.experimental import pallas as pl
from jax.experimental.pallas import tpu as pltpu
from jax.sharding import PartitionSpec as P

HALF = 7
BLEND = 16
TAPS = 2 * HALF + 1
SPAN = 2 * HALF
LANES = 128
WIN = LANES - SPAN
BLK = 16
AXES = ("depth", "lat")
OFF = 8

cell_width = 5.0
depth_step = 10.0
taper_width = 16.0

f32 = jnp.float32
bf16 = jnp.bfloat16


def cdiv(a, b):
    return -(-a // b)


def kernels(frequencies, ref_velocity):
    offsets = jnp.arange(-HALF, HALF + 1, dtype=jnp.int32).astype(jnp.float32)
    wavenumber = 2.0 * math.pi * frequencies.astype(jnp.float32)[:, None] / ref_velocity[None, :]
    curvature = wavenumber * (cell_width * cell_width / (2.0 * depth_step))
    phase_turn = wavenumber * depth_step
    chirp_angle = curvature[:, :, None] * (offsets * offsets)[None, None, :]
    envelope = jnp.exp(-offsets * offsets / taper_width)
    raw_re = envelope * jnp.cos(chirp_angle)
    raw_im = envelope * jnp.sin(chirp_angle)
    magnitude = jnp.sqrt(jnp.sum(raw_re, axis=-1) ** 2 + jnp.sum(raw_im, axis=-1) ** 2)[:, :, None]
    return (raw_re / magnitude, raw_im / magnitude, jnp.cos(phase_turn), jnp.sin(phase_turn))


def operators(tap_re, tap_im, turn_cos, turn_sin):
    ph_re = tap_re * turn_cos[..., None] - tap_im * turn_sin[..., None]
    ph_im = tap_re * turn_sin[..., None] + tap_im * turn_cos[..., None]
    lines = jnp.stack([tap_re, tap_im, ph_re, ph_im], axis=2)
    return jnp.pad(lines, ((0, 0),) * 3 + ((0, LANES - TAPS),))


def split(v):
    high = v.astype(bf16)
    return high, (v - high.astype(f32)).astype(bf16)


def window(x, start, b):
    low = start + WIN * b
    high = min(low + LANES, x.shape[1])
    part = x[:, low:high]
    if high - low < LANES:
        part = jnp.concatenate(
            [part, jnp.zeros((x.shape[0], LANES - (high - low)), x.dtype)], axis=1
        )
    return part


def dense(get, start, count):
    pieces = []
    n = start
    while n < start + count:
        b = n // WIN
        end = min(WIN * (b + 1), start + count)
        pieces.append(get(b)[:, n - WIN * b : end - WIN * b])
        n = end
    return jnp.concatenate(pieces, axis=1)


CORE, HI, SIDE, EVEN_PAIR, FIRST_PAIR, LAST_PAIR, BLOCK, REL = range(8)


def edge_lanes(x, k, cols, n):
    none = jnp.zeros((x.shape[0], n), x.dtype)
    left = x[:, cols * k - n : cols * k] if k > 0 else none
    right = x[:, cols * (k + 1) : cols * (k + 1) + n] if k < 3 else none
    return left, right


def pack_tables_kernel(edge, info, zone, blend, keep, give):
    strip, width = zone.shape[1:]
    cols = width // 4
    half = zone.shape[0] // 2
    core = info[CORE]
    rest = jnp.zeros((strip, LANES - 4 * edge), jnp.int32)
    for k in range(4):
        slot = info[REL + k]
        for v in range(half):
            for ref, h in ((keep, core), (give, 1 - core)):
                z = zone[h * half + v] + OFF
                w = blend[h * half + v]
                zl, zr = edge_lanes(z, k, cols, edge)
                wl, wr = edge_lanes(w, k, cols, edge)
                ref[slot, v, :, 0:cols] = z[:, cols * k : cols * (k + 1)]
                ref[slot, v, :, cols : 2 * cols] = w[:, cols * k : cols * (k + 1)]
                ref[slot, v, :, 2 * cols : 2 * cols + LANES] = jnp.concatenate(
                    [zl, zr, wl, wr, rest], axis=1
                )


def pack_fields_kernel(halo, info, src, rcv, mine, send):
    per_core = mine.shape[0]
    strip, width = src.shape[2:]
    cols = width // 4
    rest = jnp.zeros((strip, LANES - 4 * halo), f32)
    for k in range(4):
        slot = info[REL + k]
        for place, ref in ((0, mine), (2, send)):

            @pl.when(slot == place)
            def _():
                for q in range(per_core):
                    at = info[CORE] * per_core + q
                    lefts, rights = [], []
                    for p in range(4):
                        x = (src if p < 2 else rcv)[p % 2, at]
                        if p == 3:
                            x = -x
                        ref[q, :, p * cols : (p + 1) * cols] = x[:, cols * k : cols * (k + 1)]
                        left, right = edge_lanes(x, k, cols, halo)
                        lefts.append(left)
                        rights.append(right)
                    ref[q, :, 4 * cols : 4 * cols + LANES] = jnp.concatenate(
                        lefts + [rest], axis=1
                    )
                    ref[q, :, 4 * cols + LANES : 4 * cols + 2 * LANES] = jnp.concatenate(
                        rights + [rest], axis=1
                    )


def operators_kernel(info, lines, rows_out, cols_out):
    count, refs = lines.shape[:2]
    lane = lax.broadcasted_iota(jnp.int32, (LANES, LANES), 1)
    for q in range(count):
        by_rows, by_cols = rows_out.at[q], cols_out.at[q]
        for j in range(refs):
            re, im, ph_re, ph_im = (lines[q, j, n : n + 1, :] for n in range(4))
            for p, line in enumerate(
                (re - pltpu.roll(im, 2 * BLK, 1), im + pltpu.roll(re, 2 * BLK, 1))
            ):
                x = pltpu.roll(
                    jnp.broadcast_to(line, (BLK, LANES)), 0, 1, stride=1, stride_axis=0
                )
                high, low = split(x)
                high, low = high[:, : 4 * BLK], low[:, : 4 * BLK]
                at = (2 * j + p) * BLK
                by_rows[at : at + BLK, :] = jnp.concatenate([high, high, low], axis=1)
            bands = []
            for line in (ph_re, ph_im):
                x = pltpu.roll(
                    jnp.broadcast_to(pltpu.roll(line, WIN, 1), (LANES, LANES)),
                    0,
                    1,
                    stride=1,
                    stride_axis=0,
                )
                bands.append(split(jnp.where(lane < WIN, x, 0.0)))
            for n, kind in enumerate((0, 0, 1)):
                x, y = bands[0][kind], bands[1][kind]
                at = 2 * LANES * n
                by_cols[j, at : at + LANES, 0:LANES] = x
                by_cols[j, at : at + LANES, LANES : 2 * LANES] = y
                by_cols[j, at + LANES : at + 2 * LANES, 0:LANES] = -y
                by_cols[j, at + LANES : at + 2 * LANES, LANES : 2 * LANES] = x


def edges_out(info, ref, send_a, send_b, count):
    size = ref.shape[-2]
    lead = (slice(None),) * (len(ref.shape) - 2)

    def put(top_to, bottom_to):
        top_to[lead + (slice(0, count),)] = ref[lead + (slice(0, count),)]
        bottom_to[lead + (slice(0, count),)] = ref[lead + (slice(size - count, size),)]

    pl.when(info[EVEN_PAIR] == 1)(lambda: put(send_b, send_a))
    pl.when(info[EVEN_PAIR] == 0)(lambda: put(send_a, send_b))


def join_tables_kernel(edge, sets, info, *refs):
    count = len(sets)
    whole, send_a, send_b, token = refs[4 * count :]
    token[...] = jnp.zeros_like(token)
    first = info[SIDE] == 0
    for n, s in enumerate(sets):
        mine, got_hi, got_side, got_both = refs[4 * n : 4 * n + 4]
        strip = mine.shape[1]
        near = jnp.where(info[HI] == s, mine[...], got_hi[...])
        far = jnp.where(info[HI] == s, got_side[...], got_both[...])
        whole[n, :, 0:strip, :] = jnp.where(first, near, far)
        whole[n, :, strip : 2 * strip, :] = jnp.where(first, far, near)
        edges_out(info, whole.at[n], send_a.at[n], send_b.at[n], edge)


def join_fields_kernel(halo, info, mine, got, whole, send_a, send_b, token):
    token[...] = jnp.zeros_like(token)
    strip = mine.shape[1]
    first = info[SIDE] == 0
    whole[:, 0:strip, :] = jnp.where(first, mine[...], got[...])
    whole[:, strip : 2 * strip, :] = jnp.where(first, got[...], mine[...])
    edges_out(info, whole, send_a, send_b, halo)


def mark_kernel(info, token):
    token[...] = jnp.zeros_like(token)


def columns_kernel(halo, info, mid, got_a, got_b, *refs):
    send_a, send_b, token = refs
    token[...] = jnp.zeros_like(token)
    even = info[EVEN_PAIR] == 1
    inner = info[BLOCK] % 2 == 0
    cols = mid.shape[2] // 4
    for q in range(mid.shape[0]):
        lefts, rights = [], []
        for p in range(4):
            for start, out in ((p * cols, lefts), ((p + 1) * cols - LANES, rights)):
                lanes = slice(start, start + LANES)
                a, b, m = got_a[q, :, lanes], got_b[q, :, lanes], mid[q, :, lanes]
                top = jnp.where(info[FIRST_PAIR] == 1, 0.0, jnp.where(even, b, a))
                bottom = jnp.where(info[LAST_PAIR] == 1, 0.0, jnp.where(even, a, b))
                rows = jnp.concatenate([top, m, bottom], axis=0)
                out.append(rows[:, :halo] if out is lefts else rows[:, LANES - halo :])
        rest = jnp.zeros((lefts[0].shape[0], LANES - 4 * halo), f32)
        left = jnp.concatenate(lefts + [rest], axis=1)
        right = jnp.concatenate(rights + [rest], axis=1)
        send_a[q] = jnp.where(inner, right, left)
        send_b[q] = jnp.where(inner, left, right)


def tables_kernel(
    cols, edge, windows, n, info, whole_m, whole_o, a_m, a_o, b_m, b_o, out
):
    whole_m, whole_o, a_m, a_o, b_m, b_o = (
        x.at[n] for x in (whole_m, whole_o, a_m, a_o, b_m, b_o)
    )
    half = whole_m.shape[0]
    levels, held = out.shape[:2]
    even = info[EVEN_PAIR] == 1
    for v in range(levels):
        own = info[CORE] == v // half
        i = v % half
        a = jnp.where(own, a_m[i], a_o[i])[:edge]
        b = jnp.where(own, b_m[i], b_o[i])[:edge]
        w = jnp.where(own, whole_m[i], whole_o[i])
        top = jnp.where(info[FIRST_PAIR] == 1, 0, jnp.where(even, b, a))
        bottom = jnp.where(info[LAST_PAIR] == 1, 0, jnp.where(even, a, b))
        x = jnp.concatenate([top, w, bottom], axis=0)
        s = 2 * cols
        z = jnp.concatenate([x[:, s : s + edge], x[:, :cols], x[:, s + edge : s + 2 * edge]], 1)
        s += 2 * edge
        w = jnp.concatenate(
            [x[:, s : s + edge], x[:, cols : 2 * cols], x[:, s + edge : s + 2 * edge]], 1
        )
        t = (z - OFF).astype(f32) + w.astype(f32) * (1.0 / BLEND)
        h = x.shape[0] - SPAN * v
        t = t[HALF * v : HALF * v + h]
        for b in range(windows):
            out[v, 0:h, b * LANES : (b + 1) * LANES] = window(t, HALF * v, b)
        out[v, h:held, :] = jnp.full((held - h, windows * LANES), -8.0, f32)


def stage_kernel(levels, halo, windows, blocks, refs, first, last, *args):
    args = list(args)
    info, token = args[:2]
    count = 3 if first else 5
    fields = args[2 : 2 + count]
    tw_ref, a_ref, c_ref = args[2 + count : 5 + count]
    img_ref = args[5 + count]
    outs = args[6 + count : 6 + count + (0 if last else 3)]
    scratch = args[6 + count + len(outs) :]

    def one(q, carry):
        stage_one(
            levels, halo, windows, blocks, refs, first, last, q,
            info, *(x.at[q] for x in fields), tw_ref, a_ref.at[q], c_ref.at[q], img_ref,
            *(x.at[q] for x in outs), *scratch,
        )
        return carry

    lax.fori_loop(0, fields[0].shape[0], one, 0)


def stage_one(levels, halo, windows, blocks, refs, first, last, freq, *args):
    args = list(args)
    info = args.pop(0)
    mid, got_a, got_b = args[:3]
    del args[:3]
    if not first:
        got_y, got_m = args[:2]
        del args[:2]
    tw_ref, a_ref, c_ref = args[:3]
    del args[:3]
    img_ref = args.pop(0)
    if not last:
        out_ref, send_a, send_b = args[:3]
        del args[:3]
    cur_ref, y_ref, im_ref = args
    rows = mid.shape[0]
    cols = img_ref.shape[2]
    height = rows + 2 * halo
    held = cur_ref.shape[2]
    each = 2 * windows
    lanes = windows * LANES

    even = info[EVEN_PAIR] == 1
    inner = info[BLOCK] % 2 == 0

    def rows_of(lane):
        a, b = got_a[:, lane], got_b[:, lane]
        top = jnp.where(info[FIRST_PAIR] == 1, 0.0, jnp.where(even, b, a))
        bottom = jnp.where(info[LAST_PAIR] == 1, 0.0, jnp.where(even, a, b))
        return jnp.concatenate([top, mid[:, lane], bottom], axis=0)

    if first:
        left = rows_of(slice(4 * cols, 4 * cols + LANES))
        right = rows_of(slice(4 * cols + LANES, 4 * cols + 2 * LANES))
    else:
        left = jnp.where(info[BLOCK] == 0, 0.0, jnp.where(inner, got_m[...], got_y[...]))
        right = jnp.where(info[BLOCK] == 3, 0.0, jnp.where(inner, got_y[...], got_m[...]))
    for f in range(2):
        for p in range(2):
            n = 2 * f + p
            x = jnp.concatenate(
                [
                    left[:, n * halo : (n + 1) * halo],
                    rows_of(slice(n * cols, (n + 1) * cols)),
                    right[:, n * halo : (n + 1) * halo],
                ],
                axis=1,
            )
            if held > height:
                x = jnp.concatenate([x, jnp.zeros((held - height, x.shape[1]), f32)], axis=0)
            for b in range(windows):
                high, low = split(window(x, 0, b))
                at = (f * windows + b) * LANES
                cur_ref[p, 0, :, at : at + LANES] = high
                cur_ref[p, 1, :, at : at + LANES] = low
    lane = lax.broadcasted_iota(jnp.int32, (BLK, LANES), 1)

    def chunk(l, base, blocks):
        for k in range(blocks):
            r = pl.ds(base + BLK * k, 2 * BLK)
            rhi, rlo = cur_ref[0, 0, r, :], cur_ref[0, 1, r, :]
            ihi, ilo = cur_ref[1, 0, r, :], cur_ref[1, 1, r, :]
            rhs = jnp.concatenate([rhi, ihi, rlo, ilo, rhi, ihi], axis=0)
            g = jnp.dot(a_ref[...], rhs, preferred_element_type=f32)
            high, low = split(g)
            for j in range(refs):
                for p in range(2):
                    s = (2 * j + p) * BLK
                    for q in range(each):
                        rr = (k * each + q) * BLK
                        at = q * LANES
                        y_ref[j, rr : rr + BLK, p * LANES : (p + 1) * LANES] = high[
                            s : s + BLK, at : at + LANES
                        ]
                        y_ref[j, rr : rr + BLK, (2 + p) * LANES : (3 + p) * LANES] = low[
                            s : s + BLK, at : at + LANES
                        ]
        t = tw_ref[l, pl.ds(base, BLK * blocks), :]
        acc = None
        for j in range(refs):
            y = y_ref[j, : blocks * each * BLK]
            full = jnp.dot(
                jnp.concatenate([y, y[:, : 2 * LANES]], axis=1),
                c_ref[j],
                preferred_element_type=f32,
            )
            w = jnp.maximum(1.0 - jnp.abs(t - float(j)), 0.0)
            new = []
            for k in range(blocks):
                for f in range(2):
                    for b in range(windows):
                        rr = (k * each + f * windows + b) * BLK
                        wk = w[BLK * k : BLK * (k + 1), b * LANES : (b + 1) * LANES]
                        new.append(
                            (wk * full[rr : rr + BLK, :LANES], wk * full[rr : rr + BLK, LANES:])
                        )
            if acc is None:
                acc = new
            else:
                acc = [(a0 + b0, a1 + b1) for (a0, a1), (b0, b1) in zip(acc, new)]
        for k in range(blocks):
            r = pl.ds(base + BLK * k, BLK)
            for b in range(windows):
                s = acc[k * each + b]
                q = acc[k * each + windows + b]
                im_ref[l, r, b * LANES : (b + 1) * LANES] = s[0] * q[0] - s[1] * q[1]
            if last and l == levels - 1:
                continue
            for f in range(2):
                for b in range(windows):
                    at = (f * windows + b) * LANES
                    for p in range(2):
                        v = acc[k * each + f * windows + b][p]
                        if b + 1 < windows:
                            after = pltpu.roll(acc[k * each + f * windows + b + 1][p], WIN, 1)
                            v = jnp.where(lane < WIN, v, after)
                        high, low = split(v)
                        cur_ref[p, 0, r, at : at + LANES] = high
                        cur_ref[p, 1, r, at : at + LANES] = low

    for l in range(levels):
        need = cdiv(height - SPAN * (l + 1), BLK)
        parts = cdiv(need, blocks)
        at = 0
        for i in range(parts):
            n = cdiv(need - at, parts - i)
            chunk(l, at * BLK, n)
            at += n
    if not last:
        for f in range(2):
            for p in range(2):

                def get(b):
                    at = (f * windows + b) * LANES
                    return cur_ref[p, 0, 0:rows, at : at + LANES].astype(f32) + cur_ref[
                        p, 1, 0:rows, at : at + LANES
                    ].astype(f32)

                n = 2 * f + p
                out_ref[:, n * cols : (n + 1) * cols] = dense(get, 0, cols)
        edges_out(info, out_ref, send_a, send_b, halo)
    for l in range(levels):
        o = HALF * (levels - 1 - l)
        part = dense(
            lambda b: im_ref[l, o : o + rows, b * LANES : (b + 1) * LANES], o, cols
        )
        img_ref[l] = jnp.where(freq == 0, part, img_ref[l] + part)


def call(body, out_shape, info, *args, after=(), hand=(), **more):
    near = [pl.BlockSpec(memory_space=pltpu.VMEM)] * len(args)
    far = [pl.BlockSpec(memory_space=pl.ANY)]
    count = 1 + len(args)
    skip = count + len(after) + 2 * len(hand)

    def run(*refs):
        body(*refs[:count], *refs[skip:])

    out_specs = jax.tree.map(lambda _: pl.BlockSpec(memory_space=pltpu.VMEM), out_shape)
    if hand:
        out_shape = [shape(*x.shape, dtype=x.dtype) for x in hand] + out_shape
        out_specs = far * len(hand) + out_specs
        first = count + len(after)
        more["input_output_aliases"] = {first + n: n for n in range(len(hand))}
    return pl.pallas_call(
        run,
        in_specs=[pl.BlockSpec(memory_space=pltpu.SMEM)] + near + far * (len(after) + len(hand)),
        out_specs=out_specs,
        out_shape=out_shape,
        compiler_params=pltpu.CompilerParams(vmem_limit_bytes=40 * 2**20),
        **more,
    )(info, *args, *after, *hand)


def shape(*dims, dtype=f32):
    return jax.ShapeDtypeStruct(dims, dtype)


def local(source_field, receiver_field, zone_index, blend_weight, ref_velocity, frequencies):
    depth, lat = lax.axis_size("depth"), lax.axis_size("lat")
    d, l = lax.axis_index("depth"), lax.axis_index("lat")
    hi, core = d // 2, d % 2
    pair, side = l // 2, l % 2
    if depth != 4 or lat % 4:
        raise ValueError("mesh")
    levels, strip, width = zone_index.shape
    freq_count, refs = frequencies.shape[0], ref_velocity.shape[0]
    per_core = freq_count // 2
    rows, cols = 2 * strip, width // 4
    halo = HALF * levels
    edge = halo - HALF
    half = levels // 2
    windows = cdiv(cols + SPAN * (levels - 1), WIN)
    blocks = cdiv(rows + 2 * halo - SPAN, BLK)
    held = cdiv(rows + 2 * halo - SPAN, BLK) * BLK + BLK

    def permutation(move):
        out = []
        for i in range(depth * lat):
            dd, ll = divmod(i, lat)
            h, c, p, s = dd // 2, dd % 2, ll // 2, ll % 2
            target = move(h, c, p, s)
            if target is None or not 0 <= target[2] < lat // 2:
                target = (h, 1 - c, p, s)
            h, c, p, s = target
            out.append((i, (h * 2 + c) * lat + p * 2 + s))
        return out

    across_hi = permutation(lambda h, c, p, s: (1 - h, c, p, s))
    across_side = permutation(lambda h, c, p, s: (h, c, p, 1 - s))
    across_both = permutation(lambda h, c, p, s: (1 - h, c, p, 1 - s))
    across_core = permutation(lambda h, c, p, s: (h, 1 - c, p, s))
    pairs_even = permutation(lambda h, c, p, s: (h, c, p + 1 - 2 * (p % 2), s))
    pairs_odd = permutation(lambda h, c, p, s: (h, c, p - 1 + 2 * (p % 2), s))
    middle = permutation(lambda h, c, p, s: (1 - h, c, p, s) if s == 1 else None)

    def move(x, pairs):
        return lax.ppermute(x, AXES, pairs)

    def place(h, s):
        return 2 * h + jnp.where(h == 0, s, 1 - s)

    block = place(hi, side)
    rel = []
    for k in range(4):
        kh = k // 2
        ks = k % 2 if kh == 0 else 1 - k % 2
        rel.append(jnp.where(hi == kh, 0, 1) + jnp.where(side == ks, 0, 2))
    info = jnp.stack(
        [
            core,
            hi,
            side,
            (pair % 2 == 0).astype(jnp.int32),
            (pair == 0).astype(jnp.int32),
            (pair == lat // 2 - 1).astype(jnp.int32),
            block,
        ]
        + rel
    ).astype(jnp.int32)

    mark = shape(8, LANES)
    lane_t = 2 * cols + LANES
    lane_f = 4 * cols + 2 * LANES
    packed = shape(4, half, strip, lane_t, dtype=jnp.int32)
    mine, send = call(
        functools.partial(pack_fields_kernel, halo),
        [shape(per_core, strip, lane_f)] * 2,
        info,
        source_field,
        receiver_field,
    )
    got = move(send, across_side)
    keep, give = call(
        functools.partial(pack_tables_kernel, edge),
        [packed, packed],
        info,
        zone_index,
        blend_weight,
        after=[send],
    )
    swapped = move(give, across_core)

    def spread(own):
        return (
            own[0],
            move(own[1], across_hi),
            move(own[2], across_side),
            move(own[3], across_both),
        )

    def join(sets, parts, after):
        edges = shape(len(sets), half, cdiv(edge, 8) * 8, lane_t, dtype=jnp.int32)
        whole, send_a, send_b, token = call(
            functools.partial(join_tables_kernel, edge, sets),
            [shape(len(sets), half, rows, lane_t, dtype=jnp.int32), edges, edges, mark],
            info,
            *parts,
            after=after,
        )
        return (
            whole,
            move(whole, across_core),
            move(send_a, pairs_even),
            move(send_b, pairs_odd),
            token,
        )

    def finish(whole, other, got_a, got_b):
        swap_a, swap_b = move(got_a, across_core), move(got_b, across_core)
        return [
            call(
                functools.partial(tables_kernel, cols, edge, windows, n),
                shape(levels, held, windows * LANES),
                info,
                whole,
                other,
                got_a,
                swap_a,
                got_b,
                swap_b,
            )
            for n in range(whole.shape[0])
        ]

    parts = [spread(jnp.where(core == 0, keep, swapped)), None]

    taps = kernels(frequencies, ref_velocity)
    taps = [lax.dynamic_slice_in_dim(x, core * per_core, per_core, 0) for x in taps]
    matrices = call(
        operators_kernel,
        [
            shape(per_core, refs * 2 * BLK, 12 * BLK, dtype=bf16),
            shape(per_core, refs, 6 * LANES, 2 * LANES, dtype=bf16),
        ],
        info,
        operators(*taps),
        after=[give],
    )

    whole, send_a, send_b, _ = call(
        functools.partial(join_fields_kernel, halo),
        [shape(per_core, rows, lane_f)] + [shape(per_core, halo, lane_f)] * 2 + [mark],
        info,
        mine,
        got,
        after=[matrices[0]],
    )
    state = (whole, move(send_a, pairs_even), move(send_b, pairs_odd))
    *joined, token = join((0,), parts[0], [whole])
    tables = finish(*joined)
    parts[1] = spread(jnp.where(core == 1, keep, swapped))

    area = levels * (rows + halo) * windows * LANES
    images = []
    for s in range(4):
        out_shape = [shape(levels, rows, cols)]
        if s < 3:
            out_shape += [shape(per_core, rows, 4 * cols)] + [shape(per_core, halo, 4 * cols)] * 2
        image, *fields = call(
            functools.partial(
                stage_kernel, levels, halo, windows, blocks, refs, s == 0, s == 3
            ),
            out_shape,
            info,
            token,
            *state,
            tables[s],
            *matrices,
            scratch_shapes=[
                pltpu.VMEM((2, 2, held, 2 * windows * LANES), bf16),
                pltpu.VMEM((refs, blocks * 2 * windows * BLK, 4 * LANES), bf16),
                pltpu.VMEM((levels, held, windows * LANES), f32),
            ],
            cost_estimate=pl.CostEstimate(
                flops=area * 8 * refs * 2 * 3 * 512, bytes_accessed=2**21, transcendentals=0
            ),
        )
        images.append(image)
        if s == 3:
            break
        if s == 0:
            *joined, _ = join((0,), parts[1], [image])
        field, send_a, send_b = fields
        got = [move(send_a, pairs_even), move(send_b, pairs_odd)]
        if s == 1:
            *handed, _ = call(mark_kernel, [mark], info, after=[image], hand=list(joined[2:]))
            tables += finish(*joined[:2], *handed)
        *handed, side_a, side_b, token = call(
            functools.partial(columns_kernel, halo),
            [shape(per_core, rows + 2 * halo, LANES)] * 2 + [mark],
            info,
            field,
            *got,
            after=tables[2:] if s == 1 else [],
            hand=list(joined[2:]) if s == 0 else [],
        )
        state = (field, *got, move(side_a, across_side), move(side_b, middle))
        if s == 0:
            tables += finish(*joined[:2], *handed)
            *joined, token = join((1, 1), parts[0] + parts[1], [token])

    sums = [x + move(x, across_core) for x in images]
    sets = [jnp.where(core == 0, sums[2 * s], sums[2 * s + 1]) for s in range(2)]
    here = jnp.where(hi == 0, sets[0], sets[1])
    there = jnp.where(hi == 0, sets[1], sets[0])

    def strip_of(x, s):
        return lax.dynamic_slice_in_dim(x, s * strip, strip, 1)

    mine = strip_of(here, side)
    got_hi = move(strip_of(there, side), across_hi)
    got_side = move(strip_of(here, 1 - side), across_side)
    got_both = move(strip_of(there, 1 - side), across_both)
    pieces = []
    for k in range(4):
        piece = jnp.where(
            block == k,
            mine,
            jnp.where(
                place(1 - hi, side) == k,
                got_hi,
                jnp.where(place(hi, 1 - side) == k, got_side, got_both),
            ),
        )
        pieces.append(piece)
    return jnp.concatenate(pieces, axis=2) * (1.0 / freq_count)


def solution(mesh):
    in_specs = (
        P(None, None, "lat", None),
        P(None, None, "lat", None),
        P("depth", "lat", None),
        P("depth", "lat", None),
        P(),
        P(),
    )
    out_specs = P("depth", "lat", None)
    return jax.shard_map(local, mesh=mesh, in_specs=in_specs, out_specs=out_specs, check_vma=False)
```
